32 devices in a mesh: dp: 2 (over core), row: 4 (over y, x), col: 4 (over z).
Axes of the slice: x: 2, y: 2, z: 4, core: 2. Of those that a mesh axis runs over, the one named last changes fastest.
Arguments:
- block_input: float32 [768, 10240], P('row', ('dp', 'col')), may hold values from -32 to 32
- segment_ids: int32 [10240], replicated, may hold values from 0 to 12, as said below
- parent_ids: int32 [13], replicated, may hold values from 0 to 12, as said below
- attn_gain: float32 [768], P('row'), may hold values from 0.5 to 1.5
- attn_shift: float32 [768], P('row'), may hold values from -1.25 to 1.25
- qkv_weight: float32 [3, 12, 49152], P(None, 'col', 'row'), may hold values from -0.3125 to 0.3125
- qkv_bias: float32 [3, 768], P(None, 'col'), may hold values from -1.25 to 1.25
- proj_weight: float32 [12, 49152], P('col', 'row'), may hold values from -1.5 to 1.5
- proj_bias: float32 [768], P('row'), may hold values from -1.25 to 1.25
- mlp_gain: float32 [768], P('row'), may hold values from 0.5 to 1.5
- mlp_shift: float32 [768], P('row'), may hold values from -1.25 to 1.25
- up_weight: float32 [768, 3072], P('row', 'col'), may hold values from -0.21875 to 0.21875
- up_bias: float32 [3072], P('col'), may hold values from -1.25 to 1.25
- down_weight: float32 [768, 3072], P('row', 'col'), may hold values from -0.109375 to 0.109375
- down_bias: float32 [768], P('row'), may hold values from -1.25 to 1.25
- cotangent: float32 [768, 10240], P('row', ('dp', 'col')), may hold values from -6 to 6
Outputs:
- block_output: float32 [768, 10240], P('row', ('dp', 'col'))
- input_grad: float32 [768, 10240], P('row', ('dp', 'col'))
- attn_gain_grad: float32 [768], P('row')
- attn_shift_grad: float32 [768], P('row')
- qkv_weight_grad: float32 [3, 12, 49152], P(None, 'col', 'row')
- qkv_bias_grad: float32 [3, 768], P(None, 'col')
- proj_weight_grad: float32 [12, 49152], P('col', 'row')
- proj_bias_grad: float32 [768], P('row')
- mlp_gain_grad: float32 [768], P('row')
- mlp_shift_grad: float32 [768], P('row')
- up_weight_grad: float32 [768, 3072], P('row', 'col')
- up_bias_grad: float32 [3072], P('col')
- down_weight_grad: float32 [768, 3072], P('row', 'col')
- down_bias_grad: float32 [768], P('row')
The draws below stay inside these ranges and needn't reach their ends.
Inputs may be any that keep to these rules, and one draw needn't show every extreme that they name: `segment_ids`: rows split into trees of 10240 consecutive tokens from row 0. A tree has 13 segments, each a run of consecutive tokens: the trunk first (a quarter to a half of the tree), then each of the 4 branches followed by its 2 leaves. Every id names one segment of one tree; tree t holds the ids t * 13 to t * 13 + 12, its trunk the last of them and its first branch the first. `parent_ids`: A branch's parent is its tree's trunk, a leaf's parent its branch; a trunk is its own parent.
All inputs are finite; a program needn't handle non-finite values.
Results may differ from the reference program's by a relative error of at most 0.013.
The reference program's roundings to bfloat16 on the way count: a program that leaves them out, or rounds other values in their place, can miss the bound.
Values may be sent and summed in bfloat16 or wider, within the bound.
No kernel may reach another device: no remote copies, remote signals or barrier semaphores. Data moves between devices by JAX's collectives and lax.ppermute only.
A program may use at most 192 MiB of HBM per device.

```python
import math
import jax
import jax.numpy as jnp
import numpy as np
from jax import lax

D = 768
HEADS = 12
HEAD_DIM = 64
FF = 3072
TOK_DP = 5120
BRANCHES = 4
LEAVES = 2
TREE_SEGS = 13
TREE_TOK = 10240
TREES = 1
TOKENS = 10240
SEGS = 13


def parent_slots():
    slots = [0]
    for branch in range(BRANCHES):
        branch_slot = 1 + branch * (1 + LEAVES)
        slots = slots + [0] + [branch_slot] * LEAVES
    return np.array(slots, dtype=np.int32)


def tree_layout(key):
    slot_table = jnp.asarray(parent_slots())

    def one_tree(tree_key, tree_index):
        trunk_key, share_key, order_key = jax.random.split(tree_key, 3)
        trunk = jax.random.randint(trunk_key, (), TREE_TOK // 4, TREE_TOK // 2 + 1).astype(jnp.int32)
        remaining = TREE_TOK - trunk
        shares = jax.random.randint(share_key, (TREE_SEGS - 1,), 1, 5).astype(jnp.int32)
        pieces = remaining * shares // jnp.sum(shares)
        pieces = pieces.at[TREE_SEGS - 2].add(remaining - jnp.sum(pieces))
        lengths = jnp.concatenate([trunk[None], pieces])
        endings = jnp.cumsum(lengths)
        places = jnp.arange(TREE_TOK, dtype=jnp.int32)
        slot_of = jnp.sum((places[:, None] >= endings[None, :TREE_SEGS - 1]).astype(jnp.int32), axis=1)
        middle_labels = 1 + jax.random.permutation(order_key, TREE_SEGS - 2).astype(jnp.int32)
        labels = jnp.concatenate([jnp.full((1,), TREE_SEGS - 1, jnp.int32), jnp.zeros((1,), jnp.int32), middle_labels])
        offset = (tree_index * TREE_SEGS).astype(jnp.int32)
        token_ids = offset + labels[slot_of]
        parents = jnp.zeros((TREE_SEGS,), jnp.int32).at[labels].set(labels[slot_table]) + offset
        return (token_ids, parents)
    tree_keys = jax.random.split(key, TREES)
    token_ids, parents = jax.vmap(one_tree)(tree_keys, jnp.arange(TREES, dtype=jnp.int32))
    return (token_ids.reshape(TOKENS), parents.reshape(SEGS))


def draw_segment_ids(key, part):
    return tree_layout(jax.random.fold_in(key, 7))[0]


def draw_parent_ids(key, part):
    return tree_layout(jax.random.fold_in(key, 7))[1]


def draw_block_input(key, part):
    noise_key, scale_key, offset_key = jax.random.split(key, 3)
    place = jnp.arange(D, dtype=jnp.float32) / D
    scales = 0.7 * jnp.exp(place * math.log(3.0)) * jnp.exp(jax.random.uniform(scale_key, (D,), minval=-0.35, maxval=0.35))
    offsets = 0.3 + 0.9 * place + jax.random.uniform(offset_key, (D,), minval=-0.3, maxval=0.3)
    noise = jnp.clip(jax.random.normal(noise_key, (TOKENS, D)), -5.0, 5.0)
    return (offsets + scales * noise).astype(jnp.float32).T


def levels(rng, shape, cuts, least, top_value):
    loudness, own = 1.0, jax.random.fold_in(rng, 6)
    for dim, shards_of in cuts:
        draws = jnp.exp(jax.random.uniform(jax.random.fold_in(own, dim), (shards_of,), jnp.float32, least / len(cuts), top_value / len(cuts)))
        loudness = loudness * jnp.repeat(draws, shape[dim] // shards_of).reshape([-1 if axis == dim else 1 for axis in range(len(shape))])
    return loudness


def gaussian(stream_key, extent, width, limit, shards=(), kind=jnp.bfloat16):
    values = width * jax.random.normal(stream_key, extent, jnp.float32)
    if shards:
        values = values * levels(stream_key, extent, shards, -0.22, 0.18)
    return jnp.clip(values, -limit, limit).astype(kind)


def setup_inputs(seed: int = 0) -> dict:
    key_list = jax.random.split(jax.random.key(seed), 17)
    block_input = draw_block_input(jax.random.fold_in(key_list[16], 71), 0)
    segment_ids = draw_segment_ids(jax.random.fold_in(key_list[16], 71), 0)
    parent_ids = draw_parent_ids(jax.random.fold_in(key_list[16], 71), 0)
    attn_gain = jnp.clip(1.0 + 0.1 * jax.random.normal(key_list[3], (D,), jnp.float32), 0.5, 1.5)
    attn_shift = gaussian(key_list[4], (D,), 0.2, 1.25, ((0, 4),), jnp.float32)
    qkv_weight = gaussian(key_list[5], (3, HEADS, D * HEAD_DIM), (D // 2) ** -0.5, 0.3125, ((1, 4), (2, 4)), jnp.float32)
    qkv_bias = gaussian(key_list[6], (3, D), 0.2, 1.25, ((1, 4),), jnp.float32)
    proj_weight = gaussian(key_list[7], (HEADS, D * HEAD_DIM), (max(D // 48, 4)) ** -0.5, 1.5, ((0, 4), (1, 4)), jnp.float32)
    proj_bias = gaussian(key_list[8], (D,), 0.2, 1.25, ((0, 4),), jnp.float32)
    mlp_gain = jnp.clip(1.0 + 0.1 * jax.random.normal(key_list[9], (D,), jnp.float32), 0.5, 1.5)
    mlp_shift = gaussian(key_list[10], (D,), 0.2, 1.25, ((0, 4),), jnp.float32)
    up_weight = gaussian(key_list[11], (D, FF), D ** -0.5, 0.21875, ((0, 4), (1, 4)), jnp.float32)
    up_bias = gaussian(key_list[12], (FF,), 0.2, 1.25, ((0, 4),), jnp.float32)
    down_weight = gaussian(key_list[13], (D, FF), FF ** -0.5, 0.109375, ((0, 4), (1, 4)), jnp.float32)
    down_bias = gaussian(key_list[14], (D,), 0.2, 1.25, ((0, 4),), jnp.float32)
    cotangent = gaussian(key_list[15], (D, TOKENS), 1.0, 6.0, ((0, 4), (1, 8)), jnp.float32)
    return {"block_input": block_input, "segment_ids": segment_ids, "parent_ids": parent_ids, "attn_gain": attn_gain, "attn_shift": attn_shift, "qkv_weight": qkv_weight, "qkv_bias": qkv_bias, "proj_weight": proj_weight, "proj_bias": proj_bias, "mlp_gain": mlp_gain, "mlp_shift": mlp_shift, "up_weight": up_weight, "up_bias": up_bias, "down_weight": down_weight, "down_bias": down_bias, "cotangent": cotangent}


@jax.custom_vjp
def lower_precision(v):
    return lax.optimization_barrier(v.astype(jnp.bfloat16)).astype(jnp.float32)

@jax.custom_vjp
def low_back(v):
    return v

def low_keep(v):
    return (lower_precision(v), None)

def low_pass(kept, grad):
    return (grad,)

def back_keep(v):
    return (v, None)

def back_low(kept, grad):
    return (lower_precision(grad),)
lower_precision.defvjp(low_keep, low_pass)
low_back.defvjp(back_keep, back_low)
highest_precision = lax.Precision.HIGHEST
masked_floor = -1e+30

def layer_norm(inputs, norm_gain, norm_shift):
    average = lax.optimization_barrier(jnp.mean(inputs, axis=-1, keepdims=True))
    squares = lax.optimization_barrier(jnp.mean(inputs * inputs, axis=-1, keepdims=True))
    unit_rows = (inputs - average) * lax.rsqrt(squares - average * average + 1e-05)
    return unit_rows * norm_gain + norm_shift

def attention_tree(queries, keys, values, tree_segs, parent_ids):
    block_rows = min(512, TOK_DP)
    first_up = parent_ids[tree_segs]
    second_up = parent_ids[first_up]
    key_places = jnp.arange(TREE_TOK, dtype=jnp.int32)
    scaling = 1.0 / math.sqrt(HEAD_DIM)

    def one_block(index):
        start = (index * block_rows).astype(jnp.int32)
        block_q = lax.dynamic_slice_in_dim(queries, start, block_rows, 0)
        query_segs = lax.dynamic_slice_in_dim(tree_segs, start, block_rows, 0)
        query_first = lax.dynamic_slice_in_dim(first_up, start, block_rows, 0)
        query_second = lax.dynamic_slice_in_dim(second_up, start, block_rows, 0)
        query_places = start + jnp.arange(block_rows, dtype=jnp.int32)
        related = (tree_segs[None, :] == query_segs[:, None]) | (tree_segs[None, :] == query_first[:, None]) | (tree_segs[None, :] == query_second[:, None])
        visible = (related & (key_places[None, :] <= query_places[:, None]))[None]
        scores = jnp.einsum('qhd,khd->hqk', block_q, keys, precision=highest_precision) * scaling
        scores = low_back(scores)
        magnitude = jnp.where(visible, jnp.abs(scores), masked_floor)
        logsum = jax.nn.logsumexp(magnitude, axis=-1, keepdims=True)
        weights = jnp.where(visible, jnp.exp(magnitude - logsum), 0.0)
        signed = lower_precision(jnp.sign(scores) * weights)
        return jnp.einsum('hqk,khd->qhd', signed, values, precision=highest_precision)
    count = TREE_TOK // block_rows
    blocks = lax.map(jax.checkpoint(one_block), jnp.arange(count, dtype=jnp.int32))
    return blocks.reshape(TREE_TOK, HEADS, HEAD_DIM)

def reference(block_input, segment_ids, parent_ids, attn_gain, attn_shift, qkv_weight, qkv_bias, proj_weight, proj_bias, mlp_gain, mlp_shift, up_weight, up_bias, down_weight, down_bias, cotangent):
    tree_count = TOKENS // TREE_TOK
    tree_segs = segment_ids.reshape(tree_count, TREE_TOK)

    def layer(input_cols, gain_one, shift_one, packed_qkv, query_key_value_bias, packed_proj, bias_proj, gain_two, shift_two, weight_up, bias_up, down_cols, bias_down):
        inputs = input_cols.T
        query_key_value_weight = packed_qkv.reshape(3, HEADS, D, HEAD_DIM).transpose(2, 0, 1, 3).reshape(D, 3, D)
        weight_proj = packed_proj.reshape(HEADS, D, HEAD_DIM).transpose(0, 2, 1).reshape(D, D)
        weight_down = down_cols.T
        normalized_input = lower_precision(layer_norm(inputs, gain_one, shift_one))
        query_key_value = jnp.einsum('lf,fyx->lyx', normalized_input, lower_precision(query_key_value_weight), precision=highest_precision) + query_key_value_bias
        query_key_value = low_back(lower_precision(query_key_value))
        shaped = query_key_value.reshape(tree_count, TREE_TOK, 3, HEADS, HEAD_DIM)

        def one_tree(packed):
            tree_qkv, segs_here = packed
            return attention_tree(tree_qkv[:, 0], tree_qkv[:, 1], tree_qkv[:, 2], segs_here, parent_ids)
        attended = lax.map(one_tree, (shaped, tree_segs)).reshape(TOKENS, D)
        attended = low_back(lower_precision(attended))
        branch = jnp.dot(attended, lower_precision(weight_proj), precision=highest_precision, preferred_element_type=jnp.float32) + bias_proj
        middle = inputs + low_back(branch)
        normed_mid = lower_precision(layer_norm(middle, gain_two, shift_two))
        hidden = jnp.dot(normed_mid, lower_precision(weight_up), precision=highest_precision, preferred_element_type=jnp.float32) + bias_up
        hidden = low_back(hidden)
        activated = lower_precision(jax.nn.gelu(hidden, approximate=True))
        mlp_out = jnp.dot(activated, lower_precision(weight_down), precision=highest_precision, preferred_element_type=jnp.float32) + bias_down
        return (middle + low_back(mlp_out)).T
    block_output, pullback = jax.vjp(layer, block_input, attn_gain, attn_shift, qkv_weight, qkv_bias, proj_weight, proj_bias, mlp_gain, mlp_shift, up_weight, up_bias, down_weight, down_bias)
    grads = pullback(cotangent)
    return (block_output, grads[0], grads[1], grads[2], grads[3], grads[4], grads[5], grads[6], grads[7], grads[8], grads[9], grads[10], grads[11], grads[12])
```

```python
import functools

import jax
import jax.numpy as jnp
from jax import lax
from jax.experimental import pallas as pl
from jax.experimental.pallas import tpu as pltpu
from jax.sharding import PartitionSpec as P

HEAD_DIM = 64
LOG2E = 1.4426950408889634
BIG = 2.0**126
FLOOR = -1e30
KEY_BLOCK = 512
KEY_BLOCK_BACK = 256

def sign_low(s):
    scaled = s.astype(jnp.bfloat16) * jnp.bfloat16(BIG)
    return jnp.minimum(jnp.maximum(scaled, jnp.bfloat16(-1)), jnp.bfloat16(1))

def matmul(a, b, left=1):
    return lax.dot_general(a, b, (((left,), (0,)), ((), ())), preferred_element_type=jnp.float32)

def load_keys(offs, parts, held, sem, rows):
    chunks = parts[0].shape[1] // rows
    for p, part in enumerate(parts):
        for c in range(chunks):
            start = pl.multiple_of(offs[p * chunks + c], rows)
            pltpu.make_async_copy(part.at[:, pl.ds(c * rows, rows), :], held.at[:, pl.ds(start, rows), :], sem.at[p]).start()
    for p, part in enumerate(parts):
        pltpu.make_async_copy(part, held.at[:, pl.ds(0, part.shape[1]), :], sem.at[p]).wait()

def store_keys(offs, parts, held, sem, rows):
    chunks = parts[0].shape[1] // rows
    for p, part in enumerate(parts):
        for c in range(chunks):
            start = pl.multiple_of(offs[p * chunks + c], rows)
            pltpu.make_async_copy(held.at[:, pl.ds(start, rows), :], part.at[:, pl.ds(c * rows, rows), :], sem.at[p]).start()
    for p, part in enumerate(parts):
        pltpu.make_async_copy(held.at[:, pl.ds(0, part.shape[1]), :], part, sem.at[p]).wait()

def visible(hot, anc, pos, start, block, queries):
    hots = hot[pl.ds(start, block), :]
    hots = jnp.concatenate([hots] * (-(-queries // 128)), axis=1)[:, :queries]
    places = start + lax.broadcasted_iota(jnp.int32, (block, queries), 0)
    return ((hots & anc) != 0) & (places <= pos)

def forward_kernel(nh, np_, rows, cnt, lst, offs, q_ref, hot, anc_ref, pos_ref, *rest):
    parts, (o_ref, low_ref, l_ref, held, right, acc, top, sem) = rest[:np_], rest[np_:]
    b = pl.program_id(0)
    queries = q_ref.shape[0]
    @pl.when(b == 0)
    def _():
        right[...] = jnp.zeros_like(right)
        load_keys(offs, parts, held, sem, rows)
    acc[...] = jnp.zeros_like(acc)
    top[...] = jnp.full_like(top, FLOOR)
    turned = q_ref[...].astype(jnp.float32).T.astype(jnp.bfloat16)
    for h in range(nh):
        right[h, 0:HEAD_DIM, :] = turned[h * HEAD_DIM:(h + 1) * HEAD_DIM]
    full, some = cnt[b, 0], cnt[b, 1]

    def step(i, masked):
        start = pl.multiple_of(lst[b, i] * KEY_BLOCK, KEY_BLOCK)
        if masked:
            vis = visible(hot, anc_ref[...], pos_ref[...], start, KEY_BLOCK, queries)
        scores = [matmul(held[h, pl.ds(start, KEY_BLOCK), :], right[h]) for h in range(nh)]
        signed, scales, sums = [], [], []
        for h in range(nh):
            s = scores[h]
            size = jnp.abs(s * LOG2E)
            if masked:
                size = jnp.where(vis, size, FLOOR)
            old = top[h]
            new = jnp.maximum(old, jnp.max(size, axis=0, keepdims=True))
            e = jnp.exp2(size - new)
            if masked:
                e = jnp.where(vis, e, 0.0)
            signed.append(e.astype(jnp.bfloat16) * sign_low(s))
            scales.append(jnp.exp2(old - new))
            top[h] = new
            sums.append(jnp.sum(e, axis=0, keepdims=True))
        for h in range(nh):
            block = held[h, pl.ds(start, KEY_BLOCK), :]
            out = matmul(block[:, HEAD_DIM:], signed[h], 0)
            acc[h, 0:HEAD_DIM, :] = acc[h, 0:HEAD_DIM, :] * scales[h] + out
            acc[h, HEAD_DIM:HEAD_DIM + 1, :] = acc[h, HEAD_DIM:HEAD_DIM + 1, :] * scales[h] + sums[h]

    lax.fori_loop(0, full, lambda i, c: (step(i, False), c)[1], 0)
    lax.fori_loop(full, some, lambda i, c: (step(i, True), c)[1], 0)
    outs = []
    for h in range(nh):
        total = acc[h, HEAD_DIM:HEAD_DIM + 1, :]
        outs.append(acc[h, 0:HEAD_DIM, :] / total)
        o_ref[h] = outs[h]
        l_ref[h] = top[h] + jnp.log2(total)
    low_ref[...] = jnp.concatenate(outs, axis=0).T.astype(jnp.bfloat16)

def query_block(nq):
    return 256 if nq % 256 == 0 else nq

def attend_forward(cnt, lst, offs, q, hot, anc, pos, parts, rows):
    nq, width = q.shape
    nh = width // HEAD_DIM
    nk = hot.shape[0]
    bq = query_block(nq)
    np_ = len(parts)
    return pl.pallas_call(
        functools.partial(forward_kernel, nh, np_, rows),
        out_shape=(jax.ShapeDtypeStruct((nh, HEAD_DIM, nq), jnp.float32), jax.ShapeDtypeStruct((nq, width), jnp.bfloat16), jax.ShapeDtypeStruct((nh, 1, nq), jnp.float32)),
        grid_spec=pltpu.PrefetchScalarGridSpec(
            num_scalar_prefetch=3, grid=(nq // bq,),
            in_specs=[pl.BlockSpec((bq, width), lambda b, *_: (b, 0)),
                      pl.BlockSpec((nk, 128), lambda b, *_: (0, 0)),
                      pl.BlockSpec((1, bq), lambda b, *_: (0, b)),
                      pl.BlockSpec((1, bq), lambda b, *_: (0, b))] + [pl.BlockSpec(memory_space=pl.ANY)] * np_,
            out_specs=[pl.BlockSpec((nh, HEAD_DIM, bq), lambda b, *_: (0, 0, b)),
                       pl.BlockSpec((bq, width), lambda b, *_: (b, 0)),
                       pl.BlockSpec((nh, 1, bq), lambda b, *_: (0, 0, b))],
            scratch_shapes=[pltpu.VMEM((nh, nk, 128), jnp.bfloat16), pltpu.VMEM((nh, 128, bq), jnp.bfloat16),
                            pltpu.VMEM((nh, HEAD_DIM + 8, bq), jnp.float32), pltpu.VMEM((nh, 1, bq), jnp.float32),
                            pltpu.SemaphoreType.DMA((np_,))]),
        compiler_params=pltpu.CompilerParams(vmem_limit_bytes=56 * 1024 * 1024),
    )(cnt, lst, offs, q, hot, anc, pos, *parts)

def backward_kernel(nh, np_, rows, cnt, lst, offs, q_ref, g_ref, o_ref, l_ref, hot, anc_ref, pos_ref, *rest):
    parts, dq_ref, grads, (held, right, left, acc, dqs, sem) = rest[:np_], rest[np_], rest[np_ + 1:2 * np_ + 1], rest[2 * np_ + 1:]
    b = pl.program_id(0)
    queries = q_ref.shape[0]
    @pl.when(b == 0)
    def _():
        right[...] = jnp.zeros_like(right)
        left[...] = jnp.zeros_like(left)
        acc[...] = jnp.zeros_like(acc)
        load_keys(offs, parts, held, sem, rows)
    dqs[...] = jnp.zeros_like(dqs)
    turned = q_ref[...].astype(jnp.float32).T.astype(jnp.bfloat16)
    turned_g = g_ref[...].astype(jnp.float32).T
    deltas = []
    for h in range(nh):
        span = slice(h * HEAD_DIM, (h + 1) * HEAD_DIM)
        right[h, 0:HEAD_DIM, 0:queries] = turned[span]
        right[h, HEAD_DIM:, queries:] = turned_g[span].astype(jnp.bfloat16)
        left[h, 0:queries, 0:HEAD_DIM] = q_ref[:, span]
        left[h, queries:, HEAD_DIM:] = g_ref[:, span]
        deltas.append(jnp.sum(turned_g[span] * o_ref[h], axis=0, keepdims=True))
    full, some = cnt[b, 0], cnt[b, 1]

    def step(i, masked):
        start = pl.multiple_of(lst[b, i] * KEY_BLOCK_BACK, KEY_BLOCK_BACK)
        if masked:
            vis = visible(hot, anc_ref[...], pos_ref[...], start, KEY_BLOCK_BACK, queries)
        both = [matmul(held[h, pl.ds(start, KEY_BLOCK_BACK), :], right[h]) for h in range(nh)]
        pairs = []
        for h in range(nh):
            s, dp = both[h][:, :queries], both[h][:, queries:]
            e = jnp.exp2(jnp.abs(s * LOG2E) - l_ref[h])
            if masked:
                e = jnp.where(vis, e, 0.0)
            sg = sign_low(s)
            signed = e.astype(jnp.bfloat16) * sg
            ds = (e * (dp - sg.astype(jnp.float32) * deltas[h])).astype(jnp.bfloat16)
            pairs.append((ds, signed))
        for h in range(nh):
            ds, signed = pairs[h]
            acc[h, pl.ds(start, KEY_BLOCK_BACK), :] += matmul(jnp.concatenate([ds, signed], axis=1), left[h])
            dqs[h] += matmul(held[h, pl.ds(start, KEY_BLOCK_BACK), 0:HEAD_DIM], ds, 0)

    lax.fori_loop(0, full, lambda i, c: (step(i, False), c)[1], 0)
    lax.fori_loop(full, some, lambda i, c: (step(i, True), c)[1], 0)
    dq_ref[...] = (jnp.concatenate([dqs[h] for h in range(nh)], axis=0) * 0.125).T.astype(jnp.bfloat16)

    @pl.when(b == pl.num_programs(0) - 1)
    def _():
        size = 512
        def turn(i, c):
            at = pl.multiple_of(i * size, size)
            for h in range(nh):
                held[h, pl.ds(at, size), :] = acc[h, pl.ds(at, size), :].astype(jnp.bfloat16)
            return c
        lax.fori_loop(0, held.shape[1] // size, turn, 0)
        store_keys(offs, grads, held, sem, rows)

def attend_backward(cnt, lst, offs, q, g, o, l, hot, anc, pos, parts, rows):
    nq, width = q.shape
    nh = width // HEAD_DIM
    nk = hot.shape[0]
    bq = query_block(nq)
    np_ = len(parts)
    res = pl.pallas_call(
        functools.partial(backward_kernel, nh, np_, rows),
        out_shape=(jax.ShapeDtypeStruct((nq, width), jnp.bfloat16),) + tuple(jax.ShapeDtypeStruct(p.shape, jnp.bfloat16) for p in parts),
        grid_spec=pltpu.PrefetchScalarGridSpec(
            num_scalar_prefetch=3, grid=(nq // bq,),
            in_specs=[pl.BlockSpec((bq, width), lambda b, *_: (b, 0)),
                      pl.BlockSpec((bq, width), lambda b, *_: (b, 0)),
                      pl.BlockSpec((nh, HEAD_DIM, bq), lambda b, *_: (0, 0, b)),
                      pl.BlockSpec((nh, 1, bq), lambda b, *_: (0, 0, b)),
                      pl.BlockSpec((nk, 128), lambda b, *_: (0, 0)),
                      pl.BlockSpec((1, bq), lambda b, *_: (0, b)),
                      pl.BlockSpec((1, bq), lambda b, *_: (0, b))] + [pl.BlockSpec(memory_space=pl.ANY)] * np_,
            out_specs=[pl.BlockSpec((bq, width), lambda b, *_: (b, 0))] + [pl.BlockSpec(memory_space=pl.ANY)] * np_,
            scratch_shapes=[pltpu.VMEM((nh, nk, 128), jnp.bfloat16), pltpu.VMEM((nh, 128, 2 * bq), jnp.bfloat16),
                            pltpu.VMEM((nh, 2 * bq, 128), jnp.bfloat16), pltpu.VMEM((nh, nk, 128), jnp.float32),
                            pltpu.VMEM((nh, HEAD_DIM, bq), jnp.float32),
                            pltpu.SemaphoreType.DMA((np_,))]),
        compiler_params=pltpu.CompilerParams(vmem_limit_bytes=56 * 1024 * 1024),
    )(cnt, lst, offs, q, g, o, l, hot, anc, pos, *parts)
    return res[0], res[1:]


def swap(value, axis, step):
    count = lax.axis_size(axis)
    return lax.ppermute(value, axis, [(source, source ^ step) for source in range(count)])


def exchange(pieces, axis):
    return [pieces[0]] + [swap(pieces[step], axis, step) for step in range(1, len(pieces))]


def gather(value, axis):
    return exchange([value] * lax.axis_size(axis), axis)


def pick(values, index):
    return lax.dynamic_index_in_dim(values, index, 0, keepdims=False)


def reorder(pieces, index):
    stacked = jnp.stack(pieces)
    return jnp.stack([pick(stacked, index ^ place) for place in range(len(pieces))])


def total(pieces):
    result = pieces[0].astype(jnp.float32)
    for piece in pieces[1:]:
        result = result + piece.astype(jnp.float32)
    return result


def low(value):
    return value.astype(jnp.bfloat16)


def dot(left, right, left_dim=1, right_dim=0):
    return lax.dot_general(
        left, right, (((left_dim,), (right_dim,)), ((), ())), preferred_element_type=jnp.float32
    )


def join(pieces, cores):
    width = pieces[0].shape[1] // cores
    return jnp.concatenate(
        [
            jnp.concatenate([piece[:, j * width : (j + 1) * width] for piece in pieces], axis=1)
            for j in range(cores)
        ],
        axis=0,
    )


def split(rows, cores, count):
    width = rows.shape[1] // count
    length = rows.shape[0] // cores
    return [
        jnp.concatenate(
            [
                rows[j * length : (j + 1) * length, k * width : (k + 1) * width]
                for j in range(cores)
            ],
            axis=1,
        )
        for k in range(count)
    ]


def spread(columns, cores, count, core, row):
    features, tokens = columns.shape
    half = tokens // cores
    piece = half // count
    turned = columns.reshape(features, cores, half).transpose(1, 2, 0)
    held = exchange([pick(turned, core ^ j) for j in range(cores)], "dp")
    joined = jnp.concatenate(held, axis=1)
    pieces = [
        lax.dynamic_slice_in_dim(joined, (row ^ k) * piece, piece, 0) for k in range(count)
    ]
    return join(exchange(pieces, "row"), cores)


def collect(rows, cores, count, core, row):
    features = rows.shape[1] // count
    got = exchange(split(rows, cores, count), "row")
    joined = reorder(got, row).reshape(-1, cores * features)
    held = exchange([joined[:, j * features : (j + 1) * features] for j in range(cores)], "dp")
    halves = reorder(held, core)
    return halves.astype(jnp.float32).transpose(2, 0, 1).reshape(features, -1)


def norm_forward(inputs, gain, shift):
    average = jnp.mean(inputs, axis=1, keepdims=True)
    squares = jnp.mean(inputs * inputs, axis=1, keepdims=True)
    spread_rows = lax.rsqrt(squares - average * average + 1e-05)
    unit = (inputs - average) * spread_rows
    return low(unit * gain + shift), unit, spread_rows


def norm_backward(grad, unit, spread_rows, gain):
    scaled = grad * gain
    return spread_rows * (
        scaled
        - jnp.mean(scaled, axis=1, keepdims=True)
        - unit * jnp.mean(scaled * unit, axis=1, keepdims=True)
    )


def gelu_tanh(hidden):
    return jax.nn.gelu(hidden, approximate=True)


def everywhere(value, axis):
    return total(gather(value, axis))


def row_share(values, count, row):
    width = values.shape[1] // count
    pieces = [values[:, k * width : (k + 1) * width] for k in range(count)]
    return total(exchange(pieces, "row"))


def block_lists(hot, anc, pos, key_block, query_rows):
    def reduce(values, size, start, op):
        return lax.reduce(values.reshape(-1, size), jnp.int32(start), op, (1,))

    keys = hot.shape[0] // key_block
    key_or = reduce(hot, key_block, 0, lax.bitwise_or)[None]
    anc_or = reduce(anc, query_rows, 0, lax.bitwise_or)[:, None]
    anc_and = reduce(anc, query_rows, -1, lax.bitwise_and)[:, None]
    first = jnp.min(pos.reshape(-1, query_rows), axis=1)[:, None]
    last = jnp.max(pos.reshape(-1, query_rows), axis=1)[:, None]
    start = jnp.arange(keys, dtype=jnp.int32)[None] * key_block
    some = ((key_or & anc_or) != 0) & (start <= last)
    full = ((key_or & ~anc_and) == 0) & (start + key_block - 1 <= first)
    code = jnp.where(full, 0, jnp.where(some, 1, 2)) * keys + jnp.arange(keys)[None]
    rank = jnp.sum((code[:, None, :] < code[:, :, None]).astype(jnp.int32), axis=2)
    order = jnp.sum(
        jnp.where(
            rank[:, None, :] == jnp.arange(keys)[None, :, None],
            jnp.arange(keys, dtype=jnp.int32)[None, None],
            0,
        ),
        axis=2,
    )
    counts = jnp.stack(
        [jnp.sum(full.astype(jnp.int32), axis=1), jnp.sum((some | full).astype(jnp.int32), axis=1)],
        axis=1,
    )
    return counts.astype(jnp.int32), order.astype(jnp.int32)


def shards(
    block_input,
    segment_ids,
    parent_ids,
    attn_gain,
    attn_shift,
    qkv_weight,
    qkv_bias,
    proj_weight,
    proj_bias,
    mlp_gain,
    mlp_shift,
    up_weight,
    up_bias,
    down_weight,
    down_bias,
    cotangent,
):
    cores, rows, cols = lax.axis_size("dp"), lax.axis_size("row"), lax.axis_size("col")
    core, row, col = lax.axis_index("dp"), lax.axis_index("row"), lax.axis_index("col")
    features, tokens = block_input.shape
    half = tokens // cores
    piece = half // rows
    own = cores * piece
    heads = qkv_weight.shape[1]
    width = heads * HEAD_DIM
    hidden_part = up_weight.shape[1] // cores
    head_part = width // cores
    all_tokens = segment_ids.shape[0]

    tables = jnp.arange(parent_ids.shape[0], dtype=jnp.int32)
    grand_ids = jnp.sum(
        jnp.where(parent_ids[:, None] == tables[None], parent_ids[None], 0), axis=1
    )
    ones = jnp.int32(1)
    anc_table = (
        jnp.left_shift(ones, tables)
        | jnp.left_shift(ones, parent_ids)
        | jnp.left_shift(ones, grand_ids)
    )
    hot_all = jnp.left_shift(ones, segment_ids)
    anc_all = jnp.sum(
        jnp.where(segment_ids[None] == tables[:, None], anc_table[:, None], 0), axis=0
    )
    starts = [
        (core ^ j) * (tokens * cols) + (col ^ k) * tokens + core * half + row * piece
        for j in range(cores)
        for k in range(cols)
    ]
    anc = jnp.concatenate([lax.dynamic_slice_in_dim(anc_all, s, piece, 0) for s in starts])
    pos = jnp.concatenate([s + jnp.arange(piece, dtype=jnp.int32) for s in starts]).astype(
        jnp.int32
    )
    queries = cores * cols * piece
    block_rows = query_block(queries)
    hot = jnp.broadcast_to(hot_all[:, None], (all_tokens, 128))
    lists_forward = block_lists(hot_all, anc, pos, KEY_BLOCK, block_rows)
    lists_backward = block_lists(hot_all, anc, pos, KEY_BLOCK_BACK, block_rows)

    packed = low(qkv_weight).reshape(3, heads, features, HEAD_DIM).transpose(2, 1, 0, 3)
    qkv_low = jnp.concatenate(
        [
            packed[:, :, 1:].reshape(features, 2 * width),
            packed[:, :, 0].reshape(features, width),
        ],
        axis=1,
    )
    qkv_full = jnp.concatenate(gather(qkv_low, "row"), axis=0)
    vectors = jnp.concatenate(
        gather(
            jnp.stack([attn_gain, attn_shift, mlp_gain, mlp_shift, proj_bias, down_bias]), "row"
        ),
        axis=1,
    )
    proj_part = pick(
        low(proj_weight)
        .reshape(heads, features, HEAD_DIM)
        .transpose(0, 2, 1)
        .reshape(cores, head_part, features),
        core,
    )
    proj_rows = gather(jnp.stack(gather(proj_part, "col")), "row")
    proj_half = jnp.concatenate(proj_rows, axis=2)
    proj_full = (
        reorder(gather(proj_half, "dp"), core)
        .transpose(1, 0, 2, 3)
        .reshape(cols * width, rows * features)
    )
    mlp_part = jnp.concatenate(
        [
            lax.dynamic_slice_in_dim(low(w), core * hidden_part, hidden_part, 1)
            for w in (up_weight, down_weight)
        ],
        axis=1,
    )
    mlp_rows = gather(jnp.stack(gather(mlp_part, "col")), "row")
    mlp_all = (
        jnp.stack(mlp_rows)
        .reshape(rows, cols, features, 2, hidden_part)
        .transpose(3, 0, 2, 1, 4)
        .reshape(2, rows * features, cols * hidden_part)
    )
    up_full, down_full = mlp_all[0], mlp_all[1]
    up_bias_full = jnp.concatenate(
        gather(lax.dynamic_slice_in_dim(up_bias, core * hidden_part, hidden_part, 0), "col")
    )

    layer_in = spread(block_input, cores, rows, core, row)
    cot_rows = spread(cotangent, cores, rows, core, row)
    normed_in, first_unit, first_spread = norm_forward(layer_in, vectors[0], vectors[1])
    normed_all = jnp.concatenate(gather(normed_in, "col"), axis=0)
    bias = qkv_bias.reshape(3, heads, HEAD_DIM)
    kv_bias = jnp.concatenate([bias[1], bias[2]], axis=1)
    kv_own = low(
        lax.dot_general(
            qkv_full[:, : 2 * width].reshape(rows * features, heads, 2 * HEAD_DIM),
            normed_all,
            (((0,), (1,)), ((), ())),
            preferred_element_type=jnp.float32,
        ).transpose(0, 2, 1)
        + kv_bias[:, None, :]
    )
    q_own = low(dot(normed_all, qkv_full[:, 2 * width :]) + qkv_bias[0]) * jnp.bfloat16(0.125)
    q_own = (
        q_own.reshape(cols, cores, piece, width).transpose(1, 0, 2, 3).reshape(queries, width)
    )
    parts = [part for held in gather(kv_own, "row") for part in gather(held, "dp")]
    whole_chunks = piece % 16 == 0
    if whole_chunks:
        offsets = jnp.stack(
            [
                ((core ^ jd) ^ je) * (tokens * cols)
                + (col ^ kc) * tokens
                + (core ^ jd) * half
                + (row ^ k) * piece
                for k in range(rows)
                for jd in range(cores)
                for kc in range(cols)
                for je in range(cores)
            ]
        ).astype(jnp.int32)
        chunk = piece
    else:
        e_place, c_place, d_place, r_place = jnp.meshgrid(
            jnp.arange(cores), jnp.arange(cols), jnp.arange(cores), jnp.arange(rows), indexing="ij"
        )
        source = (
            ((row ^ r_place) * cores + (core ^ d_place)) * cols + (col ^ c_place)
        ) * cores + (e_place ^ d_place)
        stacked = jnp.stack(parts).reshape(-1, heads, cols * cores, piece, 2 * HEAD_DIM)
        stacked = stacked.transpose(0, 2, 1, 3, 4).reshape(-1, heads, piece, 2 * HEAD_DIM)
        natural = stacked[source.reshape(-1)].transpose(1, 0, 2, 3)
        parts = [natural.reshape(heads, all_tokens, 2 * HEAD_DIM)]
        offsets = jnp.zeros((1,), jnp.int32)
        chunk = all_tokens
    head_out, attended_low, logsum = attend_forward(
        *lists_forward, offsets, q_own, hot, anc[None], pos[None], parts, chunk
    )
    sent = (
        attended_low.reshape(cores, cols, piece, width)
        .transpose(1, 2, 0, 3)
        .reshape(cols, piece, cores * width)
    )
    attended = join(exchange([sent[k] for k in range(cols)], "col"), cores)

    branch = dot(attended, proj_full) + vectors[4]
    middle = layer_in + branch
    normed_mid, second_unit, second_spread = norm_forward(middle, vectors[2], vectors[3])
    mid_both = jnp.concatenate(gather(normed_mid, "dp"), axis=0)
    hidden = dot(mid_both, up_full) + up_bias_full
    activated = low(gelu_tanh(hidden))
    mlp_both = dot(activated, down_full, 1, 1)

    def own_sum(both):
        return total(exchange([both[j * own : (j + 1) * own] for j in range(cores)], "dp"))

    mlp_out = own_sum(mlp_both) + vectors[5]
    block_output = block_input + collect(low(branch + mlp_out), cores, rows, core, row)
    cot_low = low(cot_rows)
    cot_both = jnp.concatenate(gather(cot_low, "dp"), axis=0)
    act_grad = dot(cot_both, down_full)
    hidden_grad = low(jax.vjp(gelu_tanh, hidden)[1](act_grad)[0])
    mid_norm_grad = own_sum(dot(hidden_grad, up_full, 1, 1))
    up_grad = dot(mid_both, hidden_grad, 0, 0)
    down_grad = dot(cot_both, activated, 0, 0)
    up_bias_part = jnp.sum(hidden_grad, axis=0, dtype=jnp.float32)
    second_back = norm_backward(mid_norm_grad, second_unit, second_spread, vectors[2])
    middle_grad = cot_rows + second_back
    mid_low = low(middle_grad)
    attended_grad = low(dot(mid_low, proj_full, 1, 1))
    proj_grad = dot(attended, mid_low, 0, 0).reshape(cols, cores, head_part, rows * features)
    proj_grad = proj_grad.transpose(1, 0, 2, 3)
    early = jnp.stack(
        [
            jnp.sum(mid_norm_grad * second_unit, axis=0),
            jnp.sum(mid_norm_grad, axis=0),
            jnp.sum(mid_low, axis=0, dtype=jnp.float32),
            jnp.sum(cot_low, axis=0, dtype=jnp.float32),
        ]
    )
    early = everywhere(everywhere(row_share(early, rows, row), "col"), "dp")

    got = exchange(split(attended_grad, cores, cols), "col")
    out_grad = (
        jnp.stack(got)
        .reshape(cols, piece, cores, width)
        .transpose(2, 0, 1, 3)
        .reshape(queries, width)
    )
    query_grad, part_grads = attend_backward(
        *lists_backward,
        offsets,
        q_own,
        out_grad,
        head_out,
        logsum,
        hot,
        anc[None],
        pos[None],
        parts,
        chunk,
    )

    both_grads = jnp.stack([low(up_grad), low(down_grad)]).reshape(
        2, rows, features, cols * hidden_part
    )
    row_sums = total(exchange([both_grads[:, k] for k in range(rows)], "row"))
    row_sums = low(row_sums).reshape(2, features, cols, hidden_part)
    col_sums = low(total(exchange([row_sums[:, :, k] for k in range(cols)], "col")))
    weight_grads = (
        reorder(gather(col_sums, "dp"), core)
        .transpose(1, 2, 0, 3)
        .reshape(2, features, cores * hidden_part)
        .astype(jnp.float32)
    )
    up_weight_grad, down_weight_grad = weight_grads[0], weight_grads[1]
    proj_sum = total(exchange([low(pick(proj_grad, core ^ j)) for j in range(cores)], "dp"))
    proj_sum = low(proj_sum).reshape(cols, head_part, rows, features)
    proj_sum = low(total(exchange([proj_sum[:, :, k] for k in range(rows)], "row")))
    proj_sum = low(total(exchange([proj_sum[k] for k in range(cols)], "col")))
    proj_weight_grad = (
        reorder(gather(proj_sum, "dp"), core)
        .reshape(heads, HEAD_DIM, features)
        .transpose(0, 2, 1)
        .reshape(heads, features * HEAD_DIM)
        .astype(jnp.float32)
    )
    up_bias_sum = everywhere(up_bias_part, "row").reshape(cols, hidden_part)
    up_bias_sum = total(exchange([up_bias_sum[k] for k in range(cols)], "col"))
    up_bias_grad = reorder(gather(up_bias_sum, "dp"), core).reshape(-1)

    if not whole_chunks:
        natural = part_grads[0].reshape(heads, -1, piece, 2 * HEAD_DIM)
        target = jnp.stack(
            [
                (((core ^ jd) ^ je) * cols + (col ^ kc)) * (cores * rows)
                + (core ^ jd) * rows
                + (row ^ k)
                for k in range(rows)
                for jd in range(cores)
                for kc in range(cols)
                for je in range(cores)
            ]
        )
        stacked = natural[:, target].reshape(heads, rows * cores, -1, 2 * HEAD_DIM)
        part_grads = [stacked[:, p] for p in range(rows * cores)]
    chip_grads = [
        low(total(exchange(part_grads[k * cores : (k + 1) * cores], "dp"))) for k in range(rows)
    ]
    kv_grad = low(total(exchange(chip_grads, "row")))
    query_grad = (
        query_grad.reshape(cores, cols, piece, width)
        .transpose(1, 0, 2, 3)
        .reshape(queries, width)
    )
    qkv_grad = jnp.concatenate(
        [kv_grad.transpose(1, 0, 2).reshape(queries, 2 * width), query_grad], axis=1
    )
    first_parts = dot(qkv_grad, qkv_full, 1, 1).reshape(cols, own, rows * features)
    first_grad = total(
        [first_parts[0]] + [swap(low(first_parts[k]), "col", k) for k in range(1, cols)]
    )
    first_back = norm_backward(first_grad, first_unit, first_spread, vectors[0])
    input_grad = cotangent + collect(low(second_back + first_back), cores, rows, core, row)
    late = jnp.stack([jnp.sum(first_grad * first_unit, axis=0), jnp.sum(first_grad, axis=0)])
    late = everywhere(everywhere(row_share(late, rows, row), "col"), "dp")
    wide_grad = dot(normed_all, qkv_grad, 0, 0).reshape(rows, features, 3 * width)
    wide_grad = low(total(exchange([low(wide_grad[k]) for k in range(rows)], "row")))
    wide_grad = everywhere(wide_grad, "dp")

    def unpacked(values):
        lead = values.shape[0]
        kv = values[:, : 2 * width].reshape(lead, heads, 2, HEAD_DIM)
        queries_part = values[:, 2 * width :].reshape(lead, heads, 1, HEAD_DIM)
        return jnp.concatenate([queries_part, kv], axis=2).transpose(2, 1, 0, 3)

    qkv_weight_grad = unpacked(wide_grad).reshape(3, heads, features * HEAD_DIM)
    bias_part = jnp.sum(qkv_grad, axis=0, dtype=jnp.float32)[None]
    bias_sum = everywhere(everywhere(bias_part, "row"), "dp")
    qkv_bias_grad = unpacked(bias_sum).reshape(3, width)
    return (
        block_output,
        input_grad,
        late[0],
        late[1],
        qkv_weight_grad,
        qkv_bias_grad,
        proj_weight_grad,
        early[2],
        early[0],
        early[1],
        up_weight_grad,
        up_bias_grad,
        down_weight_grad,
        early[3],
    )


def solution(mesh):
    return jax.shard_map(
        shards,
        mesh=mesh,
        in_specs=(
            P("row", ("dp", "col")),
            P(),
            P(),
            P("row"),
            P("row"),
            P(None, "col", "row"),
            P(None, "col"),
            P("col", "row"),
            P("row"),
            P("row"),
            P("row"),
            P("row", "col"),
            P("col"),
            P("row", "col"),
            P("row"),
            P("row", ("dp", "col")),
        ),
        out_specs=(
            P("row", ("dp", "col")),
            P("row", ("dp", "col")),
            P("row"),
            P("row"),
            P(None, "col", "row"),
            P(None, "col"),
            P("col", "row"),
            P("row"),
            P("row"),
            P("row"),
            P("row", "col"),
            P("col"),
            P("row", "col"),
            P("row"),
        ),
        check_vma=False,
    )
```

```python
import functools

import jax
import jax.numpy as jnp
from jax import lax
from jax.experimental import pallas as pl
from jax.experimental.pallas import tpu as pltpu
from jax.sharding import PartitionSpec as P

HEAD_DIM = 64
LOG2E = 1.4426950408889634
BIG = 2.0**126
FLOOR = -1e30
KEY_BLOCK = 512
KEY_BLOCK_BACK = 256
VMEM_BYTES = 56 * 1024 * 1024


def sign_low(s):
    scaled = s.astype(jnp.bfloat16) * jnp.bfloat16(BIG)
    return jnp.minimum(jnp.maximum(scaled, jnp.bfloat16(-1)), jnp.bfloat16(1))


def matmul(a, b, left=1):
    return lax.dot_general(a, b, (((left,), (0,)), ((), ())), preferred_element_type=jnp.float32)


def part_copies(offs, parts, held, sem, rows):
    chunks = parts[0].shape[1] // rows
    for p, part in enumerate(parts):
        for c in range(chunks):
            start = pl.multiple_of(offs[p * chunks + c], rows)
            pltpu.make_async_copy(
                part.at[:, pl.ds(c * rows, rows), :], held.at[:, pl.ds(start, rows), :], sem.at[p]
            ).start()
    for p, part in enumerate(parts):
        pltpu.make_async_copy(part, held.at[:, pl.ds(0, part.shape[1]), :], sem.at[p]).wait()


def grad_copies(held, grads, sem):
    if len(grads.shape) == 3:
        pltpu.make_async_copy(held, grads, sem).start()
        pltpu.make_async_copy(held, grads, sem).wait()
        return
    groups, _, cols, pair, rows, _ = grads.shape
    for r in range(groups):
        for c in range(cols):
            for e in range(pair):
                start = ((e * cols + c) * groups + r) * rows
                pltpu.make_async_copy(
                    held.at[:, pl.ds(start, rows), :], grads.at[r, :, c, e, :, :], sem
                ).start()
    pltpu.make_async_copy(held, held, sem).wait()


def visible(keys, anc, pos, start, block, queries):
    repeat = -(-queries // 128)
    codes = jnp.concatenate([keys[pl.ds(start, block), :]] * repeat, axis=1)[:, :queries]
    return ((codes & anc) != 0) & (codes <= pos)


def fill_keys(code, keys):
    def fill(i, carry):
        at = pl.multiple_of(i * 128, 128)
        keys[pl.ds(at, 128), :] = jnp.broadcast_to(code[:, pl.ds(at, 128)], (128, 128)).T
        return carry

    lax.fori_loop(0, keys.shape[0] // 128, fill, 0)


def turn(block):
    return block.astype(jnp.float32).T


def sweep(counts, lists, b, key_block, step):
    full, some = counts[b, 0], counts[b, 1]

    def start(i):
        return pl.multiple_of(lists[b, i] * key_block, key_block)

    def plain(i, carry):
        step(start(i), False)
        return carry

    def masked(i, carry):
        step(start(i), True)
        return carry

    lax.fori_loop(0, full, plain, 0)
    lax.fori_loop(full, some, masked, 0)


def shuffle(source, target, order, rows, first=0):
    for place, origin in enumerate(order):
        at = first + place * rows
        target[at : at + rows, :] = source[origin * rows : (origin + 1) * rows, :]


def unshuffle(source, target, order, rows, first=0):
    for place, origin in enumerate(order):
        part = source[first + place * rows : first + (place + 1) * rows, :]
        part = part[:, : target.shape[1]].astype(target.dtype)
        target[origin * rows : (origin + 1) * rows, :] = part


def forward_kernel(
    heads,
    part_count,
    rows,
    order,
    order_rows,
    block,
    cnt,
    lst,
    offs,
    q_ref,
    code,
    anc_ref,
    pos_ref,
    *rest,
):
    parts = rest[:part_count]
    o_ref, low_ref, qs, os, held, right, acc, top, keys, sem = rest[part_count:]
    b = pl.program_id(0)
    width = heads * HEAD_DIM

    @pl.when(b == 0)
    def _():
        right[...] = jnp.zeros_like(right)
        shuffle(q_ref, qs, order, order_rows)
        fill_keys(code, keys)
        part_copies(offs, parts, held, sem, rows)

    acc[...] = jnp.zeros_like(acc)
    top[...] = jnp.full_like(top, FLOOR)
    at = pl.multiple_of(b * block, block)
    turned = turn(qs[pl.ds(at, block), :]).astype(jnp.bfloat16)
    for h in range(heads):
        right[h, 0:HEAD_DIM, :] = turned[h * HEAD_DIM : (h + 1) * HEAD_DIM]

    def step(start, masked):
        mask = None
        if masked:
            mask = visible(keys, anc_ref[...], pos_ref[...], start, KEY_BLOCK, block)
        scores = [matmul(held[h, pl.ds(start, KEY_BLOCK), :], right[h]) for h in range(heads)]
        signed, scales, sums = [], [], []
        for h in range(heads):
            s = scores[h]
            size = jnp.abs(s * LOG2E)
            if masked:
                size = jnp.where(mask, size, FLOOR)
            old = top[h]
            new = jnp.maximum(old, jnp.max(size, axis=0, keepdims=True))
            e = jnp.exp2(size - new)
            if masked:
                e = jnp.where(mask, e, 0.0)
            signed.append(e.astype(jnp.bfloat16) * sign_low(s))
            scales.append(jnp.exp2(old - new))
            top[h] = new
            sums.append(jnp.sum(e, axis=0, keepdims=True))
        for h in range(heads):
            out = matmul(held[h, pl.ds(start, KEY_BLOCK), HEAD_DIM:], signed[h], 0)
            acc[h, 0:HEAD_DIM, :] = acc[h, 0:HEAD_DIM, :] * scales[h] + out
            acc[h, HEAD_DIM : HEAD_DIM + 1, :] = (
                acc[h, HEAD_DIM : HEAD_DIM + 1, :] * scales[h] + sums[h]
            )

    sweep(cnt, lst, b, KEY_BLOCK, step)
    outs, logs = [], []
    for h in range(heads):
        weight = acc[h, HEAD_DIM : HEAD_DIM + 1, :]
        outs.append(acc[h, 0:HEAD_DIM, :] / weight)
        logs.append(top[h] + jnp.log2(weight))
    fill = jnp.zeros((os.shape[1] - width - heads, block), jnp.float32)
    os[pl.ds(at, block), :] = jnp.concatenate(outs + logs + [fill], axis=0).T

    @pl.when(b == pl.num_programs(0) - 1)
    def _():
        unshuffle(os, o_ref, order, order_rows)
        unshuffle(os, low_ref, order, order_rows)


def query_block(count, whole_count=None):
    return 256 if count % 256 == 0 else whole_count or count


def whole(shape):
    return pl.BlockSpec(shape, lambda b, *_: (0,) * len(shape))


def lanes(size):
    return pl.BlockSpec((1, size), lambda b, *_: (0, b))


def stat_width(heads):
    return -(-(heads * HEAD_DIM + heads) // 128) * 128


def work(passes, count, all_keys, heads):
    return pl.CostEstimate(
        flops=2 * passes * count * all_keys * 256 * heads,
        bytes_accessed=4 * heads * all_keys * 2 * HEAD_DIM,
        transcendentals=count * all_keys * heads,
    )


def attend_forward(cnt, lst, offs, q, code, anc, pos, parts, rows, order, order_rows):
    count, width = q.shape
    heads = width // HEAD_DIM
    all_keys = code.shape[1]
    block = query_block(count)
    part_count = len(parts)
    full = stat_width(heads)
    return pl.pallas_call(
        functools.partial(forward_kernel, heads, part_count, rows, order, order_rows, block),
        out_shape=(
            jax.ShapeDtypeStruct((count, full), jnp.float32),
            jax.ShapeDtypeStruct((count, width), jnp.bfloat16),
        ),
        grid_spec=pltpu.PrefetchScalarGridSpec(
            num_scalar_prefetch=3,
            grid=(count // block,),
            in_specs=[whole((count, width)), whole((1, all_keys)), lanes(block), lanes(block)]
            + [pl.BlockSpec(memory_space=pl.ANY)] * part_count,
            out_specs=[whole((count, full)), whole((count, width))],
            scratch_shapes=[
                pltpu.VMEM((count, width), jnp.bfloat16),
                pltpu.VMEM((count, full), jnp.float32),
                pltpu.VMEM((heads, all_keys, 2 * HEAD_DIM), jnp.bfloat16),
                pltpu.VMEM((heads, 2 * HEAD_DIM, block), jnp.bfloat16),
                pltpu.VMEM((heads, HEAD_DIM + 8, block), jnp.float32),
                pltpu.VMEM((heads, 1, block), jnp.float32),
                pltpu.VMEM((all_keys, 128), jnp.int32),
                pltpu.SemaphoreType.DMA((part_count,)),
            ],
        ),
        compiler_params=pltpu.CompilerParams(vmem_limit_bytes=VMEM_BYTES),
        cost_estimate=work(4, count, all_keys, heads),
    )(cnt, lst, offs, q, code, anc, pos, *parts)


def backward_kernel(
    heads,
    part_count,
    rows,
    order,
    order_rows,
    block,
    cnt,
    lst,
    offs,
    q_own,
    q_other,
    g_own,
    g_other,
    o_own,
    o_other,
    code,
    anc_ref,
    pos_ref,
    *rest,
):
    parts, (dq_own, dq_other, grads) = rest[:part_count], rest[part_count : part_count + 3]
    qs, gs, os, held, right, left, acc, dqs, dsum, stat, keys, sem, out_sem = rest[part_count + 3 :]
    b = pl.program_id(0)
    width = heads * HEAD_DIM

    @pl.when(b == 0)
    def _():
        left[...] = jnp.zeros_like(left)
        acc[...] = jnp.zeros_like(acc)
        shuffle(q_own, qs, order, order_rows)
        shuffle(q_other, qs, order, order_rows, q_own.shape[0])
        shuffle(g_own, gs, order, order_rows)
        shuffle(g_other, gs, order, order_rows, q_own.shape[0])
        shuffle(o_own, os, order, order_rows)
        shuffle(o_other, os, order, order_rows, q_own.shape[0])
        fill_keys(code, keys)
        part_copies(offs, parts, held, sem, rows)

    dqs[...] = jnp.zeros_like(dqs)
    at = pl.multiple_of(b * block, block)
    q, g = qs[pl.ds(at, block), :], gs[pl.ds(at, block), :]
    turned_o = os[pl.ds(at, block), :].T
    turned_g = turn(g)
    for h in range(heads):
        span = slice(h * HEAD_DIM, (h + 1) * HEAD_DIM)
        left[h, 0:block, 0:HEAD_DIM] = q[:, span]
        left[h, block:, HEAD_DIM:] = g[:, span]
        right[h] = turn(left[h]).astype(jnp.bfloat16)
        stat[h : h + 1, :] = turned_o[width + h : width + h + 1]
        stat[8 + h : 9 + h, :] = jnp.sum(turned_g[span] * turned_o[span], axis=0, keepdims=True)

    def step(start, masked):
        mask = None
        if masked:
            mask = visible(keys, anc_ref[...], pos_ref[...], start, KEY_BLOCK_BACK, block)
        both = [matmul(held[h, pl.ds(start, KEY_BLOCK_BACK), :], right[h]) for h in range(heads)]
        pairs = []
        for h in range(heads):
            s, dp = both[h][:, :block], both[h][:, block:]
            e = jnp.exp2(jnp.abs(s * LOG2E) - stat[h : h + 1, :])
            if masked:
                e = jnp.where(mask, e, 0.0)
            sign = sign_low(s)
            signed = e.astype(jnp.bfloat16) * sign
            delta = stat[8 + h : 9 + h, :]
            ds = (e * (dp - sign.astype(jnp.float32) * delta)).astype(jnp.bfloat16)
            pairs.append((ds, signed))
        for h in range(heads):
            ds, signed = pairs[h]
            acc[h, pl.ds(start, KEY_BLOCK_BACK), :] += matmul(
                jnp.concatenate([ds, signed], axis=1), left[h]
            )
            dqs[h] += matmul(held[h, pl.ds(start, KEY_BLOCK_BACK), 0:HEAD_DIM], ds, 0)

    sweep(cnt, lst, b, KEY_BLOCK_BACK, step)
    dsum[pl.ds(at, block), :] = (
        jnp.concatenate([dqs[h] for h in range(heads)], axis=0).T * 0.125
    )

    @pl.when(b == pl.num_programs(0) - 1)
    def _():
        unshuffle(dsum, dq_own, order, order_rows)
        unshuffle(dsum, dq_other, order, order_rows, q_own.shape[0])
        size = 512

        def lower(i, carry):
            spot = pl.multiple_of(i * size, size)
            for h in range(heads):
                held[h, pl.ds(spot, size), :] = acc[h, pl.ds(spot, size), :].astype(jnp.bfloat16)
            return carry

        lax.fori_loop(0, held.shape[1] // size, lower, 0)
        grad_copies(held, grads, out_sem)


def attend_backward(
    cnt, lst, offs, q, g, o, code, anc, pos, parts, rows, order, order_rows, grad_shape
):
    own, width = q[0].shape
    count = 2 * own
    heads = width // HEAD_DIM
    all_keys = code.shape[1]
    block = query_block(own, count)
    part_count = len(parts)
    full = o[0].shape[1]
    return pl.pallas_call(
        functools.partial(backward_kernel, heads, part_count, rows, order, order_rows, block),
        out_shape=(
            jax.ShapeDtypeStruct((own, width), jnp.float32),
            jax.ShapeDtypeStruct((own, width), jnp.float32),
            jax.ShapeDtypeStruct(grad_shape, jnp.bfloat16),
        ),
        grid_spec=pltpu.PrefetchScalarGridSpec(
            num_scalar_prefetch=3,
            grid=(count // block,),
            in_specs=[
                whole((own, width)),
                whole((own, width)),
                whole((own, width)),
                whole((own, width)),
                whole((own, full)),
                whole((own, full)),
                whole((1, all_keys)),
                lanes(block),
                lanes(block),
            ]
            + [pl.BlockSpec(memory_space=pl.ANY)] * part_count,
            out_specs=[whole((own, width)), whole((own, width)), pl.BlockSpec(memory_space=pl.ANY)],
            scratch_shapes=[
                pltpu.VMEM((count, width), jnp.bfloat16),
                pltpu.VMEM((count, width), jnp.bfloat16),
                pltpu.VMEM((count, full), jnp.float32),
                pltpu.VMEM((heads, all_keys, 2 * HEAD_DIM), jnp.bfloat16),
                pltpu.VMEM((heads, 2 * HEAD_DIM, 2 * block), jnp.bfloat16),
                pltpu.VMEM((heads, 2 * block, 2 * HEAD_DIM), jnp.bfloat16),
                pltpu.VMEM((heads, all_keys, 2 * HEAD_DIM), jnp.float32),
                pltpu.VMEM((heads, HEAD_DIM, block), jnp.float32),
                pltpu.VMEM((count, width), jnp.float32),
                pltpu.VMEM((16, block), jnp.float32),
                pltpu.VMEM((all_keys, 128), jnp.int32),
                pltpu.SemaphoreType.DMA((part_count,)),
                pltpu.SemaphoreType.DMA,
            ],
        ),
        compiler_params=pltpu.CompilerParams(vmem_limit_bytes=VMEM_BYTES),
        cost_estimate=work(5, count, all_keys, heads),
    )(cnt, lst, offs, *q, *g, *o, code, anc, pos, *parts)


def swap(value, axis, step):
    count = lax.axis_size(axis)
    return lax.ppermute(value, axis, [(source, source ^ step) for source in range(count)])


def exchange(pieces, axis):
    return [pieces[0]] + [swap(pieces[step], axis, step) for step in range(1, len(pieces))]


def gather(value, axis):
    return exchange([value] * lax.axis_size(axis), axis)


def after(value, *others):
    return lax.optimization_barrier((value,) + others)[0]


def pick(values, index, axis=0):
    return lax.dynamic_index_in_dim(values, index, axis, keepdims=False)


def reorder(pieces, index):
    stacked = jnp.stack(pieces)
    return jnp.stack([pick(stacked, index ^ place) for place in range(len(pieces))])


def total(pieces):
    result = pieces[0].astype(jnp.float32)
    for piece in pieces[1:]:
        result = result + piece.astype(jnp.float32)
    return result


def low(value):
    return value.astype(jnp.bfloat16)


def dot(left, right, left_dim=1, right_dim=0):
    return lax.dot_general(
        left, right, (((left_dim,), (right_dim,)), ((), ())), preferred_element_type=jnp.float32
    )


def trade(values, axis):
    return lax.all_to_all(values, axis, 0, 0)


def share(value, axis):
    return trade(jnp.broadcast_to(value[None], (lax.axis_size(axis),) + value.shape), axis)


def spread(columns, extra, cores, rows):
    features, tokens = columns.shape
    piece = tokens // (cores * rows)
    turned = columns.reshape(features, cores * rows, piece).transpose(1, 2, 0)
    if extra is not None:
        fill = jnp.broadcast_to(extra[None], (cores * rows,) + extra.shape)
        turned = jnp.concatenate([turned, fill], axis=1)
    got = trade(turned, ("dp", "row")).reshape(cores, rows, -1, features)
    held = got[:, :, :piece].transpose(0, 2, 1, 3).reshape(cores * piece, rows * features)
    if extra is None:
        return held
    return held, got[0, :, piece:].transpose(1, 0, 2).reshape(-1, rows * features)


def collect(first, second, extra, cores, rows):
    features = first.shape[1] // rows
    both = jnp.stack([first, second]).reshape(2, cores, -1, rows, features)
    piece = both.shape[2]
    sent = both.transpose(1, 3, 2, 0, 4).reshape(cores * rows, piece, 2 * features)
    lines = extra.reshape(-1, 2, rows, features).transpose(2, 0, 1, 3).reshape(rows, -1, 2 * features)
    lines = jnp.pad(lines, ((0, 0), (0, 16 - lines.shape[1]), (0, 0)))
    lines = jnp.broadcast_to(lines[None], (cores,) + lines.shape)
    lines = lines.reshape((cores * rows,) + lines.shape[2:])
    got = trade(jnp.concatenate([sent, lines], axis=1), ("dp", "row"))
    turned = got[:, :piece].transpose(2, 0, 1).reshape(2, features, -1).astype(jnp.float32)
    sums = jnp.sum(got[:, piece:].astype(jnp.float32), axis=0)
    return turned[0], turned[1], sums


def norm_forward(inputs, gain, shift):
    average = jnp.mean(inputs, axis=1, keepdims=True)
    squares = jnp.mean(inputs * inputs, axis=1, keepdims=True)
    spread_rows = lax.rsqrt(squares - average * average + 1e-05)
    unit = (inputs - average) * spread_rows
    return low(unit * gain + shift), unit, spread_rows


def norm_backward(grad, unit, spread_rows, gain):
    scaled = grad * gain
    return spread_rows * (
        scaled
        - jnp.mean(scaled, axis=1, keepdims=True)
        - unit * jnp.mean(scaled * unit, axis=1, keepdims=True)
    )


def gelu_tanh(hidden):
    return jax.nn.gelu(hidden, approximate=True)


def everywhere(value, axis):
    return total(gather(value, axis))


def side_by_side(pieces):
    return pieces.transpose(1, 0, 2).reshape(pieces.shape[1], -1)


def three_low(value):
    first = low(value)
    second = low(value - first.astype(jnp.float32))
    third = low(value - first.astype(jnp.float32) - second.astype(jnp.float32))
    return jnp.stack([first, second, third])


def block_lists(hot, places, anc, pos, key_block, query_rows):
    def reduce(values, size, start, op):
        return lax.reduce(values.reshape(-1, size), jnp.int32(start), op, (1,))

    keys = hot.shape[0] // key_block
    key_or = reduce(hot, key_block, 0, lax.bitwise_or)[None]
    start = jnp.min(places.reshape(-1, key_block), axis=1)[None]
    end = jnp.max(places.reshape(-1, key_block), axis=1)[None]
    anc_or = reduce(anc, query_rows, 0, lax.bitwise_or)[:, None]
    anc_and = reduce(anc, query_rows, -1, lax.bitwise_and)[:, None]
    first = jnp.min(pos.reshape(-1, query_rows), axis=1)[:, None]
    last = jnp.max(pos.reshape(-1, query_rows), axis=1)[:, None]
    full = ((key_or & ~anc_and) == 0) & (end <= first)
    some = (((key_or & anc_or) != 0) & (start <= last)) | full
    numbers = jnp.arange(keys, dtype=jnp.int32)
    code = jnp.where(full, 0, jnp.where(some, 1, 2)) * keys + numbers[None]
    rank = jnp.sum((code[:, None, :] < code[:, :, None]).astype(jnp.int32), axis=2)
    order = jnp.sum(
        jnp.where(rank[:, None, :] == numbers[None, :, None], numbers[None, None], 0), axis=2
    )
    counts = jnp.stack(
        [jnp.sum(full.astype(jnp.int32), axis=1), jnp.sum(some.astype(jnp.int32), axis=1)], axis=1
    )
    return counts.astype(jnp.int32), order.astype(jnp.int32)


def shards(
    block_input,
    segment_ids,
    parent_ids,
    attn_gain,
    attn_shift,
    qkv_weight,
    qkv_bias,
    proj_weight,
    proj_bias,
    mlp_gain,
    mlp_shift,
    up_weight,
    up_bias,
    down_weight,
    down_bias,
    cotangent,
):
    cores, rows, cols = lax.axis_size("dp"), lax.axis_size("row"), lax.axis_size("col")
    core, row, col = lax.axis_index("dp"), lax.axis_index("row"), lax.axis_index("col")
    features, tokens = block_input.shape
    half = tokens // cores
    piece = half // rows
    own = cores * piece
    width_all = rows * features
    heads = qkv_weight.shape[1]
    width = heads * HEAD_DIM
    head_width = 2 * HEAD_DIM
    hidden_part = up_weight.shape[1] // cores
    head_part = width // cores
    segments = parent_ids.shape[0]
    queries = cols * own
    block_rows = query_block(queries)
    whole_chunks = piece % 16 == 0

    vectors = jnp.stack([attn_gain, attn_shift, mlp_gain, mlp_shift, proj_bias, down_bias])
    vectors = jnp.pad(vectors, ((0, 2), (0, 0)))
    layer_in, vectors = spread(block_input, vectors, cores, rows)

    packed = low(qkv_weight).reshape(3, heads, features, HEAD_DIM)
    qkv_low = jnp.concatenate(
        [packed[kind, h] for h in range(heads) for kind in (1, 2)]
        + [packed[0, h] for h in range(heads)],
        axis=1,
    )
    bias = qkv_bias.reshape(3, heads, HEAD_DIM)
    bias_row = jnp.concatenate(
        [bias[kind, h] for h in range(heads) for kind in (1, 2)] + [bias[0].reshape(-1)]
    )

    proj_low = (
        low(proj_weight).reshape(heads, features, HEAD_DIM).transpose(0, 2, 1)
    ).reshape(width, features)
    up_low, down_low = [
        lax.dynamic_slice_in_dim(low(w), core * hidden_part, hidden_part, 1)
        for w in (up_weight, down_weight)
    ]
    up_bias_part = three_low(lax.dynamic_slice_in_dim(up_bias, core * hidden_part, hidden_part, 0))
    bias_rows = jnp.pad(up_bias_part, ((0, 13), (0, 0)))
    mlp_low = jnp.concatenate([up_low, down_low, bias_rows], axis=0)
    mlp_cols = jnp.concatenate(gather(mlp_low, "col"), axis=1)
    proj_full = (
        lax.all_gather(proj_low, ("row", "col"))
        .reshape(rows, cols * width, features)
        .transpose(1, 0, 2)
        .reshape(cols * width, width_all)
    )
    sent_rows = 2 * features
    up_bias_full = jnp.sum(mlp_cols[sent_rows : sent_rows + 3].astype(jnp.float32), axis=0)

    ones = jnp.int32(1)
    tables = jnp.arange(segments, dtype=jnp.int32)
    grand_ids = jnp.sum(
        jnp.where(parent_ids[:, None] == tables[None], parent_ids[None], 0), axis=1
    )
    anc_table = (
        jnp.left_shift(ones, tables)
        | jnp.left_shift(ones, parent_ids)
        | jnp.left_shift(ones, grand_ids)
    )
    all_places = jnp.arange(segment_ids.shape[0], dtype=jnp.int32)
    hot_all = jnp.left_shift(ones, segment_ids)
    anc_all = jnp.sum(
        jnp.where(segment_ids[None] == tables[:, None], anc_table[:, None], 0), axis=0
    )
    chunk_ids = [(c, e) for c in range(cols) for e in range(cores)]
    if whole_chunks:
        inner = [(c, e) for e in range(cores) for c in range(cols)]
    else:
        inner = chunk_ids
    order = [chunk_ids.index(chunk) for chunk in inner]
    order_rows = piece
    if not whole_chunks:
        order, order_rows = [0], queries

    def query_info(which):
        starts = [
            (e * cols + c) * tokens + which * half + row * piece for c, e in inner
        ]
        anc = [lax.dynamic_slice_in_dim(anc_all, s, piece, 0) for s in starts]
        pos = [s + jnp.arange(piece, dtype=jnp.int32) for s in starts]
        return anc, pos

    anc_own, pos_own = query_info(core)
    anc_other, pos_other = query_info(core ^ 1)
    anc = jnp.concatenate(anc_own + anc_other)
    pos = jnp.concatenate(pos_own + pos_other).astype(jnp.int32)
    limit = ((pos + 1) << segments) - 1
    codes = (all_places << segments) | hot_all
    core_places = pick(all_places.reshape(-1, cores, half), core, 1).reshape(-1)
    core_hot = pick(hot_all.reshape(-1, cores, half), core, 1).reshape(-1)
    core_codes = (core_places << segments) | core_hot
    lists_forward = block_lists(
        hot_all, all_places, anc[:queries], pos[:queries], KEY_BLOCK, block_rows
    )
    lists_backward = block_lists(
        core_hot, core_places, anc, pos, KEY_BLOCK_BACK, query_block(queries, 2 * queries)
    )
    setup = (lists_forward, lists_backward, anc[None], limit[None], codes[None], core_codes[None])

    layer_in, qkv_low, setup, mlp_cols = lax.optimization_barrier(
        (layer_in, qkv_low, setup, mlp_cols)
    )
    lists_forward, lists_backward, anc, limit, codes, core_codes = setup
    qkv_full = share(qkv_low, "row").reshape(width_all, 3 * width)
    normed_in, first_unit, first_spread = norm_forward(layer_in, vectors[0], vectors[1])
    normed_all = reorder(gather(normed_in, "col"), col).reshape(queries, width_all)
    cot_rows = spread(after(cotangent, normed_in, qkv_full), None, cores, rows)
    cot_low = low(cot_rows)
    normed_all, cot_low = lax.optimization_barrier((normed_all, cot_low))
    qkv = low(dot(normed_all, qkv_full) + bias_row)
    kv_own = jnp.stack([qkv[:, h * head_width : (h + 1) * head_width] for h in range(heads)])
    q_own = qkv[:, 2 * width :] * jnp.bfloat16(0.125)
    core_parts = gather(kv_own, "row")

    parts = [part for held in core_parts for part in gather(held, "dp")]
    q_own, proj_full = lax.optimization_barrier((q_own, proj_full))
    q_other = swap(q_own, "dp", 1)
    mlp_got = gather(after(mlp_cols[:sent_rows], *core_parts), "row")
    if whole_chunks:
        offsets = jnp.stack(
            [
                (e * cols + c) * tokens + (core ^ jd) * half + (row ^ k) * piece
                for k in range(rows)
                for jd in range(cores)
                for c, e in chunk_ids
            ]
        ).astype(jnp.int32)
        core_offsets = jnp.stack(
            [
                (e * cols + c) * half + (row ^ k) * piece
                for k in range(rows)
                for c, e in chunk_ids
            ]
        ).astype(jnp.int32)
        chunk, core_chunk = piece, piece
        grad_shape = (rows, heads, cols, cores, piece, head_width)
    else:

        def natural(pieces, count):
            sorted_parts = [
                [pieces[k * count + j] for j in range(count)] for k in range(rows)
            ]
            by_core = [reorder(p, core) if count > 1 else jnp.stack(p) for p in sorted_parts]
            stacked = reorder(by_core, row).reshape(
                rows, count, heads, cols, cores, piece, head_width
            )
            return [stacked.transpose(2, 4, 3, 1, 0, 5, 6).reshape(heads, -1, head_width)]

        parts, core_parts = natural(parts, cores), natural(core_parts, 1)
        offsets = core_offsets = jnp.zeros((1,), jnp.int32)
        chunk, core_chunk = parts[0].shape[1], core_parts[0].shape[1]
        grad_shape = core_parts[0].shape
    head_out, attended_low = attend_forward(
        *lists_forward,
        offsets,
        q_own,
        codes,
        anc[:, :queries],
        limit[:, :queries],
        parts,
        chunk,
        order,
        order_rows,
    )
    attended_low, mlp_got = lax.optimization_barrier((attended_low, mlp_got))
    attended = side_by_side(trade(attended_low.reshape(cols, own, width), "col"))
    out_other = swap(head_out, "dp", 1)

    hidden_all = cols * hidden_part

    def by_row(first, count):
        whole_rows = jnp.zeros((rows, count, hidden_all), jnp.bfloat16)
        for k in range(rows):
            part = mlp_got[k][None, first : first + count]
            whole_rows = lax.dynamic_update_slice_in_dim(whole_rows, part, row ^ k, 0)
        return whole_rows

    up_full = by_row(0, features).reshape(width_all, hidden_all)
    down_full = by_row(features, features).reshape(width_all, hidden_all)
    branch = dot(attended, proj_full) + vectors[4]
    middle = layer_in + branch
    normed_mid, second_unit, second_spread = norm_forward(middle, vectors[2], vectors[3])
    mid_both = jnp.concatenate(gather(normed_mid, "dp"), axis=0)
    cot_both = jnp.concatenate(gather(cot_low, "dp"), axis=0)
    hidden = dot(mid_both, up_full) + up_bias_full
    activated = low(gelu_tanh(hidden))
    act_grad = dot(cot_both, down_full)
    hidden_grad = low(jax.vjp(gelu_tanh, hidden)[1](act_grad)[0])

    def own_sum(both):
        return total(exchange([both[j * own : (j + 1) * own] for j in range(cores)], "dp"))

    mid_norm_grad = own_sum(dot(hidden_grad, up_full, 1, 1))
    second_back = norm_backward(mid_norm_grad, second_unit, second_spread, vectors[2])
    middle_grad = cot_rows + second_back
    mid_low = low(middle_grad)
    attended_grad = low(dot(mid_low, proj_full, 1, 1))

    sent = attended_grad.reshape(own, cols, width).transpose(1, 0, 2)
    out_grad = trade(sent, "col").reshape(queries, width)
    grad_other = swap(out_grad, "dp", 1)

    hidden_late, cot_late = lax.optimization_barrier((hidden_grad, cot_both, sent))[:2]
    up_grad = low(dot(mid_both, hidden_late, 0, 0))
    down_grad = low(dot(cot_late, activated, 0, 0))
    proj_grad = low(dot(attended, mid_low, 0, 0)).reshape(cols, cores, head_part, width_all)
    proj_sum = total([pick(proj_grad, core, 1), swap(pick(proj_grad, core ^ 1, 1), "dp", 1)])
    pack = hidden_part // features
    proj_sent = (
        low(proj_sum)
        .reshape(cols, pack, head_part // pack, rows, features)
        .transpose(3, 2, 0, 1, 4)
    )
    proj_sent = jnp.stack([pick(proj_sent, col ^ k, 2) for k in range(cols)], axis=2)
    proj_sent = proj_sent.reshape(rows, head_part // pack, cols * pack * features)
    bias_grad = low(jnp.sum(hidden_late, axis=0, dtype=jnp.float32))
    bias_sent = jnp.pad(bias_grad[None], ((0, 15), (0, 0)))
    grads_sent = jnp.concatenate(
        [
            up_grad.reshape(rows, features, hidden_all),
            down_grad.reshape(rows, features, hidden_all),
            proj_sent,
            jnp.broadcast_to(bias_sent[None], (rows,) + bias_sent.shape),
        ],
        axis=1,
    )
    grads_sent = [pick(grads_sent, row ^ k) for k in range(rows)]
    grads_sent, grad_other = lax.optimization_barrier((grads_sent, grad_other))
    grads_got = exchange(grads_sent, "row")
    query_grad, query_grad_other, part_grads = attend_backward(
        *lists_backward,
        core_offsets,
        (q_own, q_other),
        (out_grad, grad_other),
        (head_out, out_other),
        core_codes,
        anc,
        limit,
        core_parts,
        core_chunk,
        order,
        order_rows,
        grad_shape,
    )
    if not whole_chunks:
        part_grads = part_grads.reshape(heads, cores, cols, rows, piece, head_width)
        part_grads = part_grads.transpose(3, 0, 2, 1, 4, 5)

    part_grads, grads_got = lax.optimization_barrier((part_grads, grads_got))
    kv_got = trade(part_grads.reshape(rows, heads, queries, head_width), "row")
    kv_grad = low(jnp.sum(kv_got.astype(jnp.float32), axis=0))
    query_low = low(query_grad + swap(query_grad_other, "dp", 1))
    qkv_grad = jnp.concatenate([kv_grad[h] for h in range(heads)] + [query_low], axis=1)
    first_parts = low(dot(qkv_grad, qkv_full, 1, 1)).reshape(cols, own, width_all)
    row_sums = low(total(grads_got))
    col_sums = low(
        total(
            exchange(
                [
                    row_sums[:, k * hidden_part : (k + 1) * hidden_part]
                    for k in range(cols)
                ],
                "col",
            )
        )
    )
    mlp_both = dot(activated, down_full, 1, 1)
    mlp_out = own_sum(mlp_both) + vectors[5]
    output_rows = low(branch + mlp_out)
    first_parts, col_sums, output_rows = lax.optimization_barrier(
        (first_parts, col_sums, output_rows)
    )
    first_grad = jnp.sum(trade(first_parts, "col").astype(jnp.float32), axis=0)

    other_sums = swap(col_sums, "dp", 1)
    first_sums = jnp.where(core == 0, col_sums, other_sums).astype(jnp.float32)
    second_sums = jnp.where(core == 0, other_sums, col_sums).astype(jnp.float32)
    both_sums = jnp.concatenate([first_sums, second_sums], axis=1)
    up_weight_grad = both_sums[:features]
    down_weight_grad = both_sums[features : 2 * features]
    up_bias_grad = both_sums[2 * features + head_part // pack]

    def proj_rows(sums):
        values = sums[2 * features : 2 * features + head_part // pack]
        values = values[:, : pack * features].reshape(head_part // pack, pack, features)
        return values.transpose(1, 0, 2).reshape(head_part, features)

    proj_weight_grad = (
        jnp.concatenate([proj_rows(first_sums), proj_rows(second_sums)], axis=0)
        .reshape(heads, HEAD_DIM, features)
        .transpose(0, 2, 1)
        .reshape(heads, features * HEAD_DIM)
    )
    early = jnp.stack(
        [
            jnp.sum(mid_norm_grad * second_unit, axis=0),
            jnp.sum(mid_norm_grad, axis=0),
            jnp.sum(mid_low, axis=0, dtype=jnp.float32),
            jnp.sum(cot_low, axis=0, dtype=jnp.float32),
        ]
    )

    def vector_sums(values):
        pieces = values.reshape(-1, rows, features).transpose(1, 0, 2)
        summed = total(exchange([pick(pieces, row ^ k) for k in range(rows)], "row"))
        return everywhere(everywhere(summed, "col"), "dp")

    first_back = norm_backward(first_grad, first_unit, first_spread, vectors[0])
    late = jnp.stack([jnp.sum(first_grad * first_unit, axis=0), jnp.sum(first_grad, axis=0)])
    output_grown, input_grown, late_sums = collect(
        output_rows, low(second_back + first_back), three_low(late), cores, rows
    )
    block_output = block_input + output_grown
    input_grad = cotangent + input_grown
    late_sums = everywhere(jnp.sum(late_sums, axis=0).reshape(2, features), "col")
    sums = vector_sums(early)
    wide = low(dot(normed_all, qkv_grad, 0, 0)).reshape(rows, features, 3 * width)
    bias_part = low(jnp.sum(qkv_grad, axis=0, dtype=jnp.float32))
    bias_part = jnp.broadcast_to(
        jnp.pad(bias_part[None], ((0, 15), (0, 0)))[None], (rows, 16, 3 * width)
    )
    wide = jnp.concatenate([wide, bias_part], axis=1)
    wide_pieces = [pick(wide, row ^ k) for k in range(rows)]
    wide_sum = low(total(exchange(wide_pieces, "row")))
    wide_sum = everywhere(wide_sum, "dp")

    def unpacked(values):
        lead = values.shape[0]
        kv = values[:, : 2 * width].reshape(lead, heads, 2, HEAD_DIM).transpose(2, 1, 0, 3)
        q = values[:, 2 * width :].reshape(lead, heads, HEAD_DIM).transpose(1, 0, 2)
        return jnp.concatenate([q[None], kv], axis=0)

    qkv_weight_grad = unpacked(wide_sum[:features]).reshape(3, heads, features * HEAD_DIM)
    qkv_bias_grad = unpacked(wide_sum[features : features + 1]).reshape(3, width)
    return (
        block_output,
        input_grad,
        late_sums[0],
        late_sums[1],
        qkv_weight_grad,
        qkv_bias_grad,
        proj_weight_grad,
        sums[2],
        sums[0],
        sums[1],
        up_weight_grad,
        up_bias_grad,
        down_weight_grad,
        sums[3],
    )


def solution(mesh):
    return jax.shard_map(
        shards,
        mesh=mesh,
        in_specs=(
            P("row", ("dp", "col")),
            P(),
            P(),
            P("row"),
            P("row"),
            P(None, "col", "row"),
            P(None, "col"),
            P("col", "row"),
            P("row"),
            P("row"),
            P("row"),
            P("row", "col"),
            P("col"),
            P("row", "col"),
            P("row"),
            P("row", ("dp", "col")),
        ),
        out_specs=(
            P("row", ("dp", "col")),
            P("row", ("dp", "col")),
            P("row"),
            P("row"),
            P(None, "col", "row"),
            P(None, "col"),
            P("col", "row"),
            P("row"),
            P("row"),
            P("row"),
            P("row", "col"),
            P("col"),
            P("row", "col"),
            P("row"),
        ),
        check_vma=False,
    )
```

```python
import functools

import jax
import jax.numpy as jnp
from jax import lax
from jax.experimental import pallas as pl
from jax.experimental.pallas import tpu as pltpu
from jax.sharding import PartitionSpec as P

HEAD_DIM = 64
LOG2E = 1.4426950408889634
BIG = 2.0**126
FLOOR = -1e30
KEY_BLOCK = 512
KEY_BLOCK_BACK = 512
SUB_BLOCK = 128
AHEAD = 2
VMEM_BYTES = 56 * 1024 * 1024


def sign_low(s):
    scaled = s.astype(jnp.bfloat16) * jnp.bfloat16(BIG)
    return jnp.minimum(jnp.maximum(scaled, jnp.bfloat16(-1)), jnp.bfloat16(1))


def matmul(a, b, left=1):
    return lax.dot_general(a, b, (((left,), (0,)), ((), ())), preferred_element_type=jnp.float32)


def start_parts(offs, parts, held, sem, rows):
    chunks = parts[0].shape[1] // rows
    for p, part in enumerate(parts):
        for c in range(chunks):
            start = pl.multiple_of(offs[p * chunks + c], rows)
            pltpu.make_async_copy(
                part.at[:, pl.ds(c * rows, rows), :], held.at[:, pl.ds(start, rows), :], sem.at[p]
            ).start()


def wait_parts(parts, held, sem):
    for p, part in enumerate(parts):
        pltpu.make_async_copy(part, held.at[:, pl.ds(0, part.shape[1]), :], sem.at[p]).wait()


def lower(acc, held, first, count):
    for h in range(held.shape[0]):
        held[h, pl.ds(first, count), :] = acc[h, pl.ds(first, count), :].astype(jnp.bfloat16)


def store_grads(acc, held, grads, sem):
    if len(grads.shape) == 3:
        lower(acc, held, 0, held.shape[1])
        pltpu.make_async_copy(held, grads, sem).start()
    else:
        groups, _, cols, pair, rows, _ = grads.shape
        for e in range(pair):
            for c in range(cols):
                first = (e * cols + c) * groups * rows
                lower(acc, held, first, groups * rows)
                for r in range(groups):
                    pltpu.make_async_copy(
                        held.at[:, pl.ds(first + r * rows, rows), :],
                        grads.at[r, :, c, e, :, :],
                        sem,
                    ).start()
    pltpu.make_async_copy(held, held, sem).wait()


def visible(keys, anc, pos, start, block, queries):
    repeat = -(-queries // 128)
    codes = jnp.concatenate([keys[pl.ds(start, block), :]] * repeat, axis=1)[:, :queries]
    return ((codes & anc) != 0) & (codes <= pos)


def fill_keys(code, keys):
    def fill(i, carry):
        at = pl.multiple_of(i * 128, 128)
        keys[pl.ds(at, 128), :] = jnp.broadcast_to(code[:, pl.ds(at, 128)], (128, 128)).T
        return carry

    lax.fori_loop(0, keys.shape[0] // 128, fill, 0, unroll=8)


def turn(block):
    return block.astype(jnp.float32).T


def sweep(counts, lists, b, key_block, step):
    full, some = counts[b, 0], counts[b, 1]

    def start(i):
        return pl.multiple_of(lists[b, i] * key_block, key_block)

    def plain(i, carry):
        step(start(i), False)
        return carry

    def masked(i, carry):
        step(start(i), True)
        return carry

    lax.fori_loop(0, full, plain, 0)
    lax.fori_loop(full, some, masked, 0)


def shuffle(source, target, order, rows, first=0):
    for place, origin in enumerate(order):
        at = first + place * rows
        target[at : at + rows, :] = source[origin * rows : (origin + 1) * rows, :]


def unshuffle(source, target, order, rows, first=0):
    for place, origin in enumerate(order):
        part = source[first + place * rows : first + (place + 1) * rows, :]
        part = part[:, : target.shape[1]].astype(target.dtype)
        target[origin * rows : (origin + 1) * rows, :] = part


def forward_kernel(
    heads,
    part_count,
    rows,
    order,
    order_rows,
    block,
    cnt,
    lst,
    offs,
    q_ref,
    code,
    anc_ref,
    pos_ref,
    *rest,
):
    parts = rest[:part_count]
    o_ref, low_ref, qs, os, held, right, acc, top, keys, sem = rest[part_count:]
    b = pl.program_id(0)
    width = heads * HEAD_DIM

    @pl.when(b == 0)
    def _():
        start_parts(offs, parts, held, sem, rows)
        right[...] = jnp.zeros_like(right)
        shuffle(q_ref, qs, order, order_rows)
        fill_keys(code, keys)
        wait_parts(parts, held, sem)

    acc[...] = jnp.zeros_like(acc)
    top[...] = jnp.full_like(top, FLOOR)
    at = pl.multiple_of(b * block, block)
    turned = turn(qs[pl.ds(at, block), :]).astype(jnp.bfloat16)
    for h in range(heads):
        right[h, 0:HEAD_DIM, :] = turned[h * HEAD_DIM : (h + 1) * HEAD_DIM]

    def step(start, masked):
        mask = None
        if masked:
            mask = visible(keys, anc_ref[...], pos_ref[...], start, KEY_BLOCK, block)
        scores = [matmul(held[h, pl.ds(start, KEY_BLOCK), :], right[h]) for h in range(heads)]
        signed, scales, sums = [], [], []
        for h in range(heads):
            s = scores[h]
            size = jnp.abs(s * LOG2E)
            if masked:
                size = jnp.where(mask, size, FLOOR)
            old = top[h]
            new = jnp.maximum(old, jnp.max(size, axis=0, keepdims=True))
            e = jnp.exp2(size - new)
            signed.append(e.astype(jnp.bfloat16) * sign_low(s))
            scales.append(jnp.exp2(old - new))
            top[h] = new
            sums.append(jnp.sum(e, axis=0, keepdims=True))
        for h in range(heads):
            out = matmul(held[h, pl.ds(start, KEY_BLOCK), HEAD_DIM:], signed[h], 0)
            acc[h, 0:HEAD_DIM, :] = acc[h, 0:HEAD_DIM, :] * scales[h] + out
            acc[h, HEAD_DIM : HEAD_DIM + 1, :] = (
                acc[h, HEAD_DIM : HEAD_DIM + 1, :] * scales[h] + sums[h]
            )

    sweep(cnt, lst, b, KEY_BLOCK, step)
    outs, logs = [], []
    for h in range(heads):
        weight = acc[h, HEAD_DIM : HEAD_DIM + 1, :]
        outs.append(acc[h, 0:HEAD_DIM, :] / weight)
        logs.append(top[h] + jnp.log2(weight))
    fill = jnp.zeros((os.shape[1] - width - heads, block), jnp.float32)
    os[pl.ds(at, block), :] = jnp.concatenate(outs + logs + [fill], axis=0).T

    @pl.when(b == pl.num_programs(0) - 1)
    def _():
        unshuffle(os, o_ref, order, order_rows)
        unshuffle(os, low_ref, order, order_rows)


def query_block(count, whole_count=None):
    return 256 if count % 256 == 0 else whole_count or count


def whole(shape):
    return pl.BlockSpec(shape, lambda b, *_: (0,) * len(shape))


def lanes(size):
    return pl.BlockSpec((1, size), lambda b, *_: (0, b))


def stat_width(heads):
    return -(-(heads * HEAD_DIM + heads) // 128) * 128


def work(passes, count, all_keys, heads):
    return pl.CostEstimate(
        flops=2 * passes * count * all_keys * 256 * heads,
        bytes_accessed=4 * heads * all_keys * 2 * HEAD_DIM,
        transcendentals=count * all_keys * heads,
    )


def attend_forward(cnt, lst, offs, q, code, anc, pos, parts, rows, order, order_rows):
    count, width = q.shape
    heads = width // HEAD_DIM
    all_keys = code.shape[1]
    block = query_block(count)
    part_count = len(parts)
    full = stat_width(heads)
    return pl.pallas_call(
        functools.partial(forward_kernel, heads, part_count, rows, order, order_rows, block),
        out_shape=(
            jax.ShapeDtypeStruct((count, full), jnp.float32),
            jax.ShapeDtypeStruct((count, width), jnp.bfloat16),
        ),
        grid_spec=pltpu.PrefetchScalarGridSpec(
            num_scalar_prefetch=3,
            grid=(count // block,),
            in_specs=[whole((count, width)), whole((1, all_keys)), lanes(block), lanes(block)]
            + [pl.BlockSpec(memory_space=pl.ANY)] * part_count,
            out_specs=[whole((count, full)), whole((count, width))],
            scratch_shapes=[
                pltpu.VMEM((count, width), jnp.bfloat16),
                pltpu.VMEM((count, full), jnp.float32),
                pltpu.VMEM((heads, all_keys, 2 * HEAD_DIM), jnp.bfloat16),
                pltpu.VMEM((heads, 2 * HEAD_DIM, block), jnp.bfloat16),
                pltpu.VMEM((heads, HEAD_DIM + 8, block), jnp.float32),
                pltpu.VMEM((heads, 1, block), jnp.float32),
                pltpu.VMEM((all_keys, 128), jnp.int32),
                pltpu.SemaphoreType.DMA((part_count,)),
            ],
        ),
        compiler_params=pltpu.CompilerParams(vmem_limit_bytes=VMEM_BYTES),
        cost_estimate=work(4, count, all_keys, heads),
    )(cnt, lst, offs, q, code, anc, pos, *parts)


def backward_kernel(
    heads,
    part_count,
    rows,
    order,
    order_rows,
    block,
    cnt,
    lst,
    offs,
    q_own,
    q_other,
    g_own,
    g_other,
    o_own,
    o_other,
    code,
    anc_ref,
    pos_ref,
    *rest,
):
    parts, (dq_own, dq_other, grads) = rest[:part_count], rest[part_count : part_count + 3]
    qs, gs, os, held, right, left, acc, dqs, dsum, stat, keys, sem, out_sem = rest[part_count + 3 :]
    b = pl.program_id(0)
    width = heads * HEAD_DIM

    @pl.when(b == 0)
    def _():
        start_parts(offs, parts, held, sem, rows)
        left[...] = jnp.zeros_like(left)
        right[...] = jnp.zeros_like(right)
        acc[...] = jnp.zeros_like(acc)
        shuffle(q_own, qs, order, order_rows)
        shuffle(q_other, qs, order, order_rows, q_own.shape[0])
        shuffle(g_own, gs, order, order_rows)
        shuffle(g_other, gs, order, order_rows, q_own.shape[0])
        shuffle(o_own, os, order, order_rows)
        shuffle(o_other, os, order, order_rows, q_own.shape[0])
        fill_keys(code, keys)
        wait_parts(parts, held, sem)

    dqs[...] = jnp.zeros_like(dqs)
    at = pl.multiple_of(b * block, block)
    q, g = qs[pl.ds(at, block), :], gs[pl.ds(at, block), :]
    turned_o = os[pl.ds(at, block), :].T
    turned_q = turn(q).astype(jnp.bfloat16)
    turned_g = turn(g)
    for h in range(heads):
        span = slice(h * HEAD_DIM, (h + 1) * HEAD_DIM)
        left[h, 0:block, 0:HEAD_DIM] = q[:, span]
        left[h, block:, HEAD_DIM:] = g[:, span]
        right[h, 0:HEAD_DIM, 0:block] = turned_q[span]
        right[h, HEAD_DIM:, block:] = turned_g[span].astype(jnp.bfloat16)
        stat[h : h + 1, :] = turned_o[width + h : width + h + 1]
        stat[8 + h : 9 + h, :] = jnp.sum(turned_g[span] * turned_o[span], axis=0, keepdims=True)

    def step(start, masked):
        mask = None
        if masked:
            mask = visible(keys, anc_ref[...], pos_ref[...], start, KEY_BLOCK_BACK, block)
        units = [(h, at) for at in range(0, KEY_BLOCK_BACK, SUB_BLOCK) for h in range(heads)]

        def scores(h, at):
            both = matmul(held[h, pl.ds(start + at, SUB_BLOCK), :], right[h])
            return both[:, :block], both[:, block:]

        def gradients(h, at, s, dp):
            e = jnp.exp2(jnp.abs(s * LOG2E) - stat[h : h + 1, :])
            if masked:
                e = jnp.where(mask[at : at + SUB_BLOCK], e, 0.0)
            sign = sign_low(s)
            signed = e.astype(jnp.bfloat16) * sign
            delta = stat[8 + h : 9 + h, :]
            ds = (e * (dp - sign.astype(jnp.float32) * delta)).astype(jnp.bfloat16)
            return ds, signed

        def gather_up(h, at, ds, signed):
            spot = pl.ds(start + at, SUB_BLOCK)
            acc[h, spot, :] += matmul(jnp.concatenate([ds, signed], axis=1), left[h])
            dqs[h] += matmul(held[h, spot, 0:HEAD_DIM], ds, 0)

        ready = [scores(*unit) for unit in units[:AHEAD]]
        last = None
        for i, unit in enumerate(units):
            if i + AHEAD < len(units):
                ready.append(scores(*units[i + AHEAD]))
            pair = gradients(*unit, *ready[i])
            if last is not None:
                gather_up(*last)
            last = unit + pair
        gather_up(*last)

    sweep(cnt, lst, b, KEY_BLOCK_BACK, step)
    fill = jnp.zeros((dsum.shape[1] - width, block), jnp.float32)
    dsum[pl.ds(at, block), :] = (
        jnp.concatenate([dqs[h] for h in range(heads)] + [fill], axis=0).T * 0.125
    )

    @pl.when(b == pl.num_programs(0) - 1)
    def _():
        store_grads(acc, held, grads, out_sem)
        unshuffle(dsum, dq_own, order, order_rows)
        unshuffle(dsum, dq_other, order, order_rows, q_own.shape[0])


def attend_backward(
    cnt, lst, offs, q, g, o, code, anc, pos, parts, rows, order, order_rows, grad_shape
):
    own, width = q[0].shape
    count = 2 * own
    heads = width // HEAD_DIM
    all_keys = code.shape[1]
    block = query_block(own, count)
    part_count = len(parts)
    full = o[0].shape[1]
    return pl.pallas_call(
        functools.partial(backward_kernel, heads, part_count, rows, order, order_rows, block),
        out_shape=(
            jax.ShapeDtypeStruct((own, full), jnp.float32),
            jax.ShapeDtypeStruct((own, full), jnp.float32),
            jax.ShapeDtypeStruct(grad_shape, jnp.bfloat16),
        ),
        grid_spec=pltpu.PrefetchScalarGridSpec(
            num_scalar_prefetch=3,
            grid=(count // block,),
            in_specs=[
                whole((own, width)),
                whole((own, width)),
                whole((own, width)),
                whole((own, width)),
                whole((own, full)),
                whole((own, full)),
                whole((1, all_keys)),
                lanes(block),
                lanes(block),
            ]
            + [pl.BlockSpec(memory_space=pl.ANY)] * part_count,
            out_specs=[whole((own, full)), whole((own, full)), pl.BlockSpec(memory_space=pl.ANY)],
            scratch_shapes=[
                pltpu.VMEM((count, width), jnp.bfloat16),
                pltpu.VMEM((count, width), jnp.bfloat16),
                pltpu.VMEM((count, full), jnp.float32),
                pltpu.VMEM((heads, all_keys, 2 * HEAD_DIM), jnp.bfloat16),
                pltpu.VMEM((heads, 2 * HEAD_DIM, 2 * block), jnp.bfloat16),
                pltpu.VMEM((heads, 2 * block, 2 * HEAD_DIM), jnp.bfloat16),
                pltpu.VMEM((heads, all_keys, 2 * HEAD_DIM), jnp.float32),
                pltpu.VMEM((heads, HEAD_DIM, block), jnp.float32),
                pltpu.VMEM((count, full), jnp.float32),
                pltpu.VMEM((16, block), jnp.float32),
                pltpu.VMEM((all_keys, 128), jnp.int32),
                pltpu.SemaphoreType.DMA((part_count,)),
                pltpu.SemaphoreType.DMA,
            ],
        ),
        compiler_params=pltpu.CompilerParams(vmem_limit_bytes=VMEM_BYTES),
        cost_estimate=work(5, count, all_keys, heads),
    )(cnt, lst, offs, *q, *g, *o, code, anc, pos, *parts)


def swap(value, axis, step):
    count = lax.axis_size(axis)
    return lax.ppermute(value, axis, [(source, source ^ step) for source in range(count)])


def exchange(pieces, axis):
    return [pieces[0]] + [swap(pieces[step], axis, step) for step in range(1, len(pieces))]


def gather(value, axis):
    return exchange([value] * lax.axis_size(axis), axis)


def after(value, *others):
    return lax.optimization_barrier((value,) + others)[0]


def pick(values, index, axis=0):
    return lax.dynamic_index_in_dim(values, index, axis, keepdims=False)


def reorder(pieces, index):
    stacked = jnp.stack(pieces)
    return jnp.stack([pick(stacked, index ^ place) for place in range(len(pieces))])


def total(pieces):
    result = pieces[0].astype(jnp.float32)
    for piece in pieces[1:]:
        result = result + piece.astype(jnp.float32)
    return result


def low(value):
    return value.astype(jnp.bfloat16)


def dot(left, right, left_dim=1, right_dim=0):
    return lax.dot_general(
        left, right, (((left_dim,), (right_dim,)), ((), ())), preferred_element_type=jnp.float32
    )


def trade(values, axis):
    return lax.all_to_all(values, axis, 0, 0)


def share(value, axis):
    return trade(jnp.broadcast_to(value[None], (lax.axis_size(axis),) + value.shape), axis)


def spread(columns, extra, cores, rows):
    features, tokens = columns.shape
    piece = tokens // (cores * rows)
    turned = columns.reshape(features, cores * rows, piece).transpose(1, 2, 0)
    if extra is not None:
        fill = jnp.broadcast_to(extra[None], (cores * rows,) + extra.shape)
        turned = jnp.concatenate([turned, fill], axis=1)
    got = trade(turned, ("dp", "row")).reshape(cores, rows, -1, features)
    held = got[:, :, :piece].transpose(0, 2, 1, 3).reshape(cores * piece, rows * features)
    if extra is None:
        return held
    return held, got[0, :, piece:].transpose(1, 0, 2).reshape(-1, rows * features)


def by_device(values, cores, rows):
    features = values.shape[1] // rows
    sent = values.reshape(cores, -1, rows, features).transpose(0, 2, 1, 3)
    return sent.reshape(cores * rows, -1, features)


def collect(first, second, extra, cores, rows):
    second = by_device(second, cores, rows)
    _, piece, features = second.shape
    sent = jnp.concatenate([first, second], axis=2)
    lines = extra.reshape(-1, 2, rows, features).transpose(2, 0, 1, 3).reshape(rows, -1, 2 * features)
    lines = jnp.pad(lines, ((0, 0), (0, 16 - lines.shape[1]), (0, 0)))
    lines = jnp.broadcast_to(lines[None], (cores,) + lines.shape)
    lines = lines.reshape((cores * rows,) + lines.shape[2:])
    got = trade(jnp.concatenate([sent, lines], axis=1), ("dp", "row"))
    turned = got[:, :piece].transpose(2, 0, 1).reshape(2, features, -1).astype(jnp.float32)
    sums = jnp.sum(got[:, piece:].astype(jnp.float32), axis=0)
    return turned[0], turned[1], sums


def norm_forward(inputs, gain, shift):
    average = jnp.mean(inputs, axis=1, keepdims=True)
    squares = jnp.mean(inputs * inputs, axis=1, keepdims=True)
    spread_rows = lax.rsqrt(squares - average * average + 1e-05)
    unit = (inputs - average) * spread_rows
    return low(unit * gain + shift), unit, spread_rows


def norm_backward(grad, unit, spread_rows, gain):
    scaled = grad * gain
    return spread_rows * (
        scaled
        - jnp.mean(scaled, axis=1, keepdims=True)
        - unit * jnp.mean(scaled * unit, axis=1, keepdims=True)
    )


def gelu_tanh(hidden):
    return jax.nn.gelu(hidden, approximate=True)


def everywhere(value, axis):
    return total(gather(value, axis))


def side_by_side(pieces):
    return pieces.transpose(1, 0, 2).reshape(pieces.shape[1], -1)


def three_low(value):
    first = low(value)
    second = low(value - first.astype(jnp.float32))
    third = low(value - first.astype(jnp.float32) - second.astype(jnp.float32))
    return jnp.stack([first, second, third])


def block_lists(hot, places, anc, pos, key_block, query_rows):
    def reduce(values, size, start, op):
        return lax.reduce(values.reshape(-1, size), jnp.int32(start), op, (1,))

    keys = hot.shape[0] // key_block
    key_or = reduce(hot, key_block, 0, lax.bitwise_or)[None]
    start = jnp.min(places.reshape(-1, key_block), axis=1)[None]
    end = jnp.max(places.reshape(-1, key_block), axis=1)[None]
    anc_or = reduce(anc, query_rows, 0, lax.bitwise_or)[:, None]
    anc_and = reduce(anc, query_rows, -1, lax.bitwise_and)[:, None]
    first = jnp.min(pos.reshape(-1, query_rows), axis=1)[:, None]
    last = jnp.max(pos.reshape(-1, query_rows), axis=1)[:, None]
    full = ((key_or & ~anc_and) == 0) & (end <= first)
    some = (((key_or & anc_or) != 0) & (start <= last)) | full
    numbers = jnp.arange(keys, dtype=jnp.int32)
    code = jnp.where(full, 0, jnp.where(some, 1, 2)) * keys + numbers[None]
    rank = jnp.sum((code[:, None, :] < code[:, :, None]).astype(jnp.int32), axis=2)
    order = jnp.sum(
        jnp.where(rank[:, None, :] == numbers[None, :, None], numbers[None, None], 0), axis=2
    )
    counts = jnp.stack(
        [jnp.sum(full.astype(jnp.int32), axis=1), jnp.sum(some.astype(jnp.int32), axis=1)], axis=1
    )
    return counts.astype(jnp.int32), order.astype(jnp.int32)


def shards(
    block_input,
    segment_ids,
    parent_ids,
    attn_gain,
    attn_shift,
    qkv_weight,
    qkv_bias,
    proj_weight,
    proj_bias,
    mlp_gain,
    mlp_shift,
    up_weight,
    up_bias,
    down_weight,
    down_bias,
    cotangent,
):
    cores, rows, cols = lax.axis_size("dp"), lax.axis_size("row"), lax.axis_size("col")
    core, row, col = lax.axis_index("dp"), lax.axis_index("row"), lax.axis_index("col")
    features, tokens = block_input.shape
    half = tokens // cores
    piece = half // rows
    own = cores * piece
    width_all = rows * features
    heads = qkv_weight.shape[1]
    width = heads * HEAD_DIM
    head_width = 2 * HEAD_DIM
    hidden_part = up_weight.shape[1] // cores
    head_part = width // cores
    segments = parent_ids.shape[0]
    queries = cols * own
    block_rows = query_block(queries)
    whole_chunks = piece % 16 == 0

    vectors = jnp.stack([attn_gain, attn_shift, mlp_gain, mlp_shift, proj_bias, down_bias])
    vectors = jnp.pad(vectors, ((0, 2), (0, 0)))
    layer_in, vectors = spread(block_input, vectors, cores, rows)

    packed = low(qkv_weight).reshape(3, heads, features, HEAD_DIM)
    qkv_low = jnp.concatenate(
        [packed[kind, h] for h in range(heads) for kind in (1, 2)]
        + [packed[0, h] for h in range(heads)],
        axis=1,
    )
    bias = qkv_bias.reshape(3, heads, HEAD_DIM)
    bias_row = jnp.concatenate(
        [bias[kind, h] for h in range(heads) for kind in (1, 2)] + [bias[0].reshape(-1)]
    )

    proj_low = (
        low(proj_weight).reshape(heads, features, HEAD_DIM).transpose(0, 2, 1)
    ).reshape(width, features)
    up_low, down_low = [
        lax.dynamic_slice_in_dim(low(w), core * hidden_part, hidden_part, 1)
        for w in (up_weight, down_weight)
    ]
    up_bias_part = three_low(lax.dynamic_slice_in_dim(up_bias, core * hidden_part, hidden_part, 0))
    bias_rows = jnp.pad(up_bias_part, ((0, 13), (0, 0)))
    mlp_low = jnp.concatenate([up_low, down_low, bias_rows], axis=0)
    mlp_cols = jnp.concatenate(gather(mlp_low, "col"), axis=1)
    proj_full = (
        lax.all_gather(proj_low, ("row", "col"))
        .reshape(rows, cols * width, features)
        .transpose(1, 0, 2)
        .reshape(cols * width, width_all)
    )
    sent_rows = 2 * features
    up_bias_full = jnp.sum(mlp_cols[sent_rows : sent_rows + 3].astype(jnp.float32), axis=0)

    ones = jnp.int32(1)
    tables = jnp.arange(segments, dtype=jnp.int32)
    grand_ids = jnp.sum(
        jnp.where(parent_ids[:, None] == tables[None], parent_ids[None], 0), axis=1
    )
    anc_table = (
        jnp.left_shift(ones, tables)
        | jnp.left_shift(ones, parent_ids)
        | jnp.left_shift(ones, grand_ids)
    )
    all_places = jnp.arange(segment_ids.shape[0], dtype=jnp.int32)
    hot_all = jnp.left_shift(ones, segment_ids)
    anc_all = jnp.sum(
        jnp.where(segment_ids[None] == tables[:, None], anc_table[:, None], 0), axis=0
    )
    chunk_ids = [(c, e) for c in range(cols) for e in range(cores)]
    if whole_chunks:
        inner = [(c, e) for e in range(cores) for c in range(cols)]
    else:
        inner = chunk_ids
    order = [chunk_ids.index(chunk) for chunk in inner]
    order_rows = piece
    if not whole_chunks:
        order, order_rows = [0], queries

    def query_info(which):
        starts = [
            (e * cols + c) * tokens + which * half + row * piece for c, e in inner
        ]
        anc = [lax.dynamic_slice_in_dim(anc_all, s, piece, 0) for s in starts]
        pos = [s + jnp.arange(piece, dtype=jnp.int32) for s in starts]
        return anc, pos

    anc_own, pos_own = query_info(core)
    anc_other, pos_other = query_info(core ^ 1)
    anc = jnp.concatenate(anc_own + anc_other)
    pos = jnp.concatenate(pos_own + pos_other).astype(jnp.int32)
    limit = ((pos + 1) << segments) - 1
    codes = (all_places << segments) | hot_all
    core_places = pick(all_places.reshape(-1, cores, half), core, 1).reshape(-1)
    core_hot = pick(hot_all.reshape(-1, cores, half), core, 1).reshape(-1)
    core_codes = (core_places << segments) | core_hot
    lists_forward = block_lists(
        hot_all, all_places, anc[:queries], pos[:queries], KEY_BLOCK, block_rows
    )
    lists_backward = block_lists(
        core_hot, core_places, anc, pos, KEY_BLOCK_BACK, query_block(queries, 2 * queries)
    )
    setup = (lists_forward, lists_backward, anc[None], limit[None], codes[None], core_codes[None])

    layer_in, qkv_low, setup, mlp_cols = lax.optimization_barrier(
        (layer_in, qkv_low, setup, mlp_cols)
    )
    lists_forward, lists_backward, anc, limit, codes, core_codes = setup
    qkv_full = share(qkv_low, "row").reshape(width_all, 3 * width)
    normed_in, first_unit, first_spread = norm_forward(layer_in, vectors[0], vectors[1])
    normed_all = reorder(gather(normed_in, "col"), col).reshape(queries, width_all)
    cot_rows = spread(after(cotangent, normed_in, qkv_full), None, cores, rows)
    cot_low = low(cot_rows)
    normed_all, cot_low = lax.optimization_barrier((normed_all, cot_low))
    qkv = low(dot(normed_all, qkv_full) + bias_row)
    kv_own = jnp.stack([qkv[:, h * head_width : (h + 1) * head_width] for h in range(heads)])
    q_own = qkv[:, 2 * width :] * jnp.bfloat16(0.125)
    core_parts = gather(kv_own, "row")

    cot_both = jnp.concatenate(gather(cot_low, "dp"), axis=0)
    q_own, proj_full, cot_both, core_parts = lax.optimization_barrier(
        (q_own, proj_full, cot_both, core_parts)
    )
    parts = [part for held in core_parts for part in gather(held, "dp")]
    q_other = swap(q_own, "dp", 1)
    mlp_got = gather(after(mlp_cols[:sent_rows], *core_parts), "row")
    if whole_chunks:
        offsets = jnp.stack(
            [
                (e * cols + c) * tokens + (core ^ jd) * half + (row ^ k) * piece
                for k in range(rows)
                for jd in range(cores)
                for c, e in chunk_ids
            ]
        ).astype(jnp.int32)
        core_offsets = jnp.stack(
            [
                (e * cols + c) * half + (row ^ k) * piece
                for k in range(rows)
                for c, e in chunk_ids
            ]
        ).astype(jnp.int32)
        chunk, core_chunk = piece, piece
        grad_shape = (rows, heads, cols, cores, piece, head_width)
    else:

        def natural(pieces, count):
            sorted_parts = [
                [pieces[k * count + j] for j in range(count)] for k in range(rows)
            ]
            by_core = [reorder(p, core) if count > 1 else jnp.stack(p) for p in sorted_parts]
            stacked = reorder(by_core, row).reshape(
                rows, count, heads, cols, cores, piece, head_width
            )
            return [stacked.transpose(2, 4, 3, 1, 0, 5, 6).reshape(heads, -1, head_width)]

        parts, core_parts = natural(parts, cores), natural(core_parts, 1)
        offsets = core_offsets = jnp.zeros((1,), jnp.int32)
        chunk, core_chunk = parts[0].shape[1], core_parts[0].shape[1]
        grad_shape = core_parts[0].shape
    head_out, attended_low = attend_forward(
        *lists_forward,
        offsets,
        q_own,
        codes,
        anc[:, :queries],
        limit[:, :queries],
        parts,
        chunk,
        order,
        order_rows,
    )
    attended_low, mlp_got = lax.optimization_barrier((attended_low, mlp_got))
    attended = side_by_side(trade(attended_low.reshape(cols, own, width), "col"))
    out_other = swap(head_out, "dp", 1)

    hidden_all = cols * hidden_part

    def by_row(first, count):
        whole_rows = jnp.zeros((rows, count, hidden_all), jnp.bfloat16)
        for k in range(rows):
            part = mlp_got[k][None, first : first + count]
            whole_rows = lax.dynamic_update_slice_in_dim(whole_rows, part, row ^ k, 0)
        return whole_rows

    up_full = by_row(0, features).reshape(width_all, hidden_all)
    down_full = by_row(features, features).reshape(width_all, hidden_all)
    branch = dot(attended, proj_full) + vectors[4]
    middle = layer_in + branch
    normed_mid, second_unit, second_spread = norm_forward(middle, vectors[2], vectors[3])
    mid_both = jnp.concatenate(gather(normed_mid, "dp"), axis=0)
    hidden = dot(mid_both, up_full) + up_bias_full
    activated = low(gelu_tanh(hidden))
    act_grad = dot(cot_both, down_full)
    hidden_grad = low(jax.vjp(gelu_tanh, hidden)[1](act_grad)[0])

    def own_sum(both):
        return total(exchange([both[j * own : (j + 1) * own] for j in range(cores)], "dp"))

    mid_norm_grad = own_sum(dot(hidden_grad, up_full, 1, 1))
    second_back = norm_backward(mid_norm_grad, second_unit, second_spread, vectors[2])
    middle_grad = cot_rows + second_back
    mid_low = low(middle_grad)
    attended_grad = low(dot(mid_low, proj_full, 1, 1))

    sent = attended_grad.reshape(own, cols, width).transpose(1, 0, 2)
    sent, hidden_late, cot_late, activated_late = lax.optimization_barrier(
        (sent, hidden_grad, cot_both, activated)
    )
    out_grad = trade(sent, "col").reshape(queries, width)
    grad_other = swap(out_grad, "dp", 1)

    up_grad = low(dot(mid_both, hidden_late, 0, 0))
    down_grad = low(dot(cot_late, activated_late, 0, 0))
    proj_grad = low(dot(attended, mid_low, 0, 0)).reshape(cols, cores, head_part, width_all)
    proj_sum = total([pick(proj_grad, core, 1), swap(pick(proj_grad, core ^ 1, 1), "dp", 1)])
    pack = hidden_part // features
    proj_sent = (
        low(proj_sum)
        .reshape(cols, pack, head_part // pack, rows, features)
        .transpose(3, 2, 0, 1, 4)
    )
    proj_sent = jnp.stack([pick(proj_sent, col ^ k, 2) for k in range(cols)], axis=2)
    proj_sent = proj_sent.reshape(rows, head_part // pack, cols * pack * features)
    bias_grad = low(jnp.sum(hidden_late, axis=0, dtype=jnp.float32))
    bias_sent = jnp.pad(bias_grad[None], ((0, 15), (0, 0)))
    grads_sent = jnp.concatenate(
        [
            up_grad.reshape(rows, features, hidden_all),
            down_grad.reshape(rows, features, hidden_all),
            proj_sent,
            jnp.broadcast_to(bias_sent[None], (rows,) + bias_sent.shape),
        ],
        axis=1,
    )
    grads_sent = [pick(grads_sent, row ^ k) for k in range(rows)]
    grads_sent, grad_other = lax.optimization_barrier((grads_sent, grad_other))
    grads_got = exchange(grads_sent, "row")
    early = jnp.stack(
        [
            jnp.sum(mid_norm_grad * second_unit, axis=0),
            jnp.sum(mid_norm_grad, axis=0),
            jnp.sum(mid_low, axis=0, dtype=jnp.float32),
            jnp.sum(cot_low, axis=0, dtype=jnp.float32),
        ]
    )

    query_grad, query_grad_other, part_grads = attend_backward(
        *lists_backward,
        core_offsets,
        (q_own, q_other),
        (out_grad, grad_other),
        (head_out, out_other),
        core_codes,
        anc,
        limit,
        core_parts,
        core_chunk,
        order,
        order_rows,
        grad_shape,
    )
    if not whole_chunks:
        part_grads = part_grads.reshape(heads, cores, cols, rows, piece, head_width)
        part_grads = part_grads.transpose(3, 0, 2, 1, 4, 5)

    part_grads, grads_got, activated_late = lax.optimization_barrier(
        (part_grads, grads_got, activated_late)
    )
    kv_got = trade(part_grads.reshape(rows, heads, queries, head_width), "row")
    kv_grad = low(jnp.sum(kv_got.astype(jnp.float32), axis=0))
    query_low = low((query_grad + swap(query_grad_other, "dp", 1))[:, :width])
    qkv_grad = jnp.concatenate([kv_grad[h] for h in range(heads)] + [query_low], axis=1)
    first_parts = low(dot(qkv_grad, qkv_full, 1, 1)).reshape(cols, own, width_all)
    row_sums = low(total(grads_got))
    col_sums = low(
        total(
            exchange(
                [
                    row_sums[:, k * hidden_part : (k + 1) * hidden_part]
                    for k in range(cols)
                ],
                "col",
            )
        )
    )
    mlp_both = dot(activated_late, down_full, 1, 1)
    mlp_out = own_sum(mlp_both) + vectors[5]
    output_rows = by_device(low(branch + mlp_out), cores, rows)
    first_parts, col_sums, output_rows, qkv_grad, early = lax.optimization_barrier(
        (first_parts, col_sums, output_rows, qkv_grad, early)
    )
    first_grad = jnp.sum(trade(first_parts, "col").astype(jnp.float32), axis=0)

    other_sums = swap(col_sums, "dp", 1)
    first_sums = jnp.where(core == 0, col_sums, other_sums).astype(jnp.float32)
    second_sums = jnp.where(core == 0, other_sums, col_sums).astype(jnp.float32)
    both_sums = jnp.concatenate([first_sums, second_sums], axis=1)
    up_weight_grad = both_sums[:features]
    down_weight_grad = both_sums[features : 2 * features]
    up_bias_grad = both_sums[2 * features + head_part // pack]

    def proj_rows(sums):
        values = sums[2 * features : 2 * features + head_part // pack]
        values = values[:, : pack * features].reshape(head_part // pack, pack, features)
        return values.transpose(1, 0, 2).reshape(head_part, features)

    proj_weight_grad = (
        jnp.concatenate([proj_rows(first_sums), proj_rows(second_sums)], axis=0)
        .reshape(heads, HEAD_DIM, features)
        .transpose(0, 2, 1)
        .reshape(heads, features * HEAD_DIM)
    )
    def vector_sums(values):
        pieces = values.reshape(-1, rows, features).transpose(1, 0, 2)
        summed = total(exchange([pick(pieces, row ^ k) for k in range(rows)], "row"))
        return everywhere(everywhere(summed, "col"), "dp")

    first_back = norm_backward(first_grad, first_unit, first_spread, vectors[0])
    late = jnp.stack([jnp.sum(first_grad * first_unit, axis=0), jnp.sum(first_grad, axis=0)])
    output_grown, input_grown, late_sums = collect(
        output_rows, low(second_back + first_back), three_low(late), cores, rows
    )
    block_output = block_input + output_grown
    input_grad = cotangent + input_grown
    late_sums = everywhere(jnp.sum(late_sums, axis=0).reshape(2, features), "col")
    sums = vector_sums(early)
    wide = low(dot(normed_all, qkv_grad, 0, 0)).reshape(rows, features, 3 * width)
    bias_part = low(jnp.sum(qkv_grad, axis=0, dtype=jnp.float32))
    bias_part = jnp.broadcast_to(
        jnp.pad(bias_part[None], ((0, 15), (0, 0)))[None], (rows, 16, 3 * width)
    )
    wide = jnp.concatenate([wide, bias_part], axis=1)
    wide_pieces = [pick(wide, row ^ k) for k in range(rows)]
    wide_sum = low(total(exchange(wide_pieces, "row")))
    wide_sum = everywhere(wide_sum, "dp")

    def unpacked(values):
        lead = values.shape[0]
        kv = values[:, : 2 * width].reshape(lead, heads, 2, HEAD_DIM).transpose(2, 1, 0, 3)
        q = values[:, 2 * width :].reshape(lead, heads, HEAD_DIM).transpose(1, 0, 2)
        return jnp.concatenate([q[None], kv], axis=0)

    qkv_weight_grad = unpacked(wide_sum[:features]).reshape(3, heads, features * HEAD_DIM)
    qkv_bias_grad = unpacked(wide_sum[features : features + 1]).reshape(3, width)
    return (
        block_output,
        input_grad,
        late_sums[0],
        late_sums[1],
        qkv_weight_grad,
        qkv_bias_grad,
        proj_weight_grad,
        sums[2],
        sums[0],
        sums[1],
        up_weight_grad,
        up_bias_grad,
        down_weight_grad,
        sums[3],
    )


def solution(mesh):
    return jax.shard_map(
        shards,
        mesh=mesh,
        in_specs=(
            P("row", ("dp", "col")),
            P(),
            P(),
            P("row"),
            P("row"),
            P(None, "col", "row"),
            P(None, "col"),
            P("col", "row"),
            P("row"),
            P("row"),
            P("row"),
            P("row", "col"),
            P("col"),
            P("row", "col"),
            P("row"),
            P("row", ("dp", "col")),
        ),
        out_specs=(
            P("row", ("dp", "col")),
            P("row", ("dp", "col")),
            P("row"),
            P("row"),
            P(None, "col", "row"),
            P(None, "col"),
            P("col", "row"),
            P("row"),
            P("row"),
            P("row"),
            P("row", "col"),
            P("col"),
            P("row", "col"),
            P("row"),
        ),
        check_vma=False,
    )
```

```python
import functools

import jax
import jax.numpy as jnp
from jax import lax
from jax.experimental import pallas as pl
from jax.experimental.pallas import tpu as pltpu
from jax.sharding import PartitionSpec as P

HEAD_DIM = 64
LOG2E = 1.4426950408889634
BIG = 2.0**126
FLOOR = -1e30
KEY_BLOCK = 512
KEY_BLOCK_BACK = 512
SUB_BLOCK = 128
AHEAD = 2
VMEM_BYTES = 56 * 1024 * 1024


def sign_low(s):
    scaled = s.astype(jnp.bfloat16) * jnp.bfloat16(BIG)
    return jnp.minimum(jnp.maximum(scaled, jnp.bfloat16(-1)), jnp.bfloat16(1))


def matmul(a, b, left=1):
    return lax.dot_general(a, b, (((left,), (0,)), ((), ())), preferred_element_type=jnp.float32)


def start_parts(offs, parts, held, sem, rows):
    chunks = parts[0].shape[1] // rows
    for p, part in enumerate(parts):
        for c in range(chunks):
            start = pl.multiple_of(offs[p * chunks + c], rows)
            pltpu.make_async_copy(
                part.at[:, pl.ds(c * rows, rows), :], held.at[:, pl.ds(start, rows), :], sem.at[p]
            ).start()


def wait_parts(parts, held, sem):
    for p, part in enumerate(parts):
        pltpu.make_async_copy(part, held.at[:, pl.ds(0, part.shape[1]), :], sem.at[p]).wait()


def lower(acc, held, first, count):
    for h in range(held.shape[0]):
        held[h, pl.ds(first, count), :] = acc[h, pl.ds(first, count), :].astype(jnp.bfloat16)


def store_grads(acc, held, grads, sem):
    if len(grads.shape) == 3:
        lower(acc, held, 0, held.shape[1])
        pltpu.make_async_copy(held, grads, sem).start()
    else:
        groups, _, cols, pair, rows, _ = grads.shape
        for e in range(pair):
            for c in range(cols):
                first = (e * cols + c) * groups * rows
                lower(acc, held, first, groups * rows)
                for r in range(groups):
                    pltpu.make_async_copy(
                        held.at[:, pl.ds(first + r * rows, rows), :],
                        grads.at[r, :, c, e, :, :],
                        sem,
                    ).start()
    pltpu.make_async_copy(held, held, sem).wait()


def visible(keys, anc, pos, start, block, queries):
    repeat = -(-queries // 128)
    codes = jnp.concatenate([keys[pl.ds(start, block), :]] * repeat, axis=1)[:, :queries]
    return ((codes & anc) != 0) & (codes <= pos)


def fill_keys(code, keys):
    def fill(i, carry):
        at = pl.multiple_of(i * 128, 128)
        keys[pl.ds(at, 128), :] = jnp.broadcast_to(code[:, pl.ds(at, 128)], (128, 128)).T
        return carry

    lax.fori_loop(0, keys.shape[0] // 128, fill, 0, unroll=8)


def turn(block):
    return block.astype(jnp.float32).T


def sweep(counts, lists, b, key_block, step):
    full, some = counts[b, 0], counts[b, 1]

    def start(i):
        return pl.multiple_of(lists[b, i] * key_block, key_block)

    def plain(i, carry):
        step(start(i), False)
        return carry

    def masked(i, carry):
        step(start(i), True)
        return carry

    lax.fori_loop(0, full, plain, 0)
    lax.fori_loop(full, some, masked, 0)


def shuffle(source, target, order, rows, first=0, stride=2):
    for place, origin in enumerate(order):
        at = (place * stride + first) * rows
        target[at : at + rows, :] = source[origin * rows : (origin + 1) * rows, :]


def unshuffle(source, target, order, rows, first=0, stride=2):
    for place, origin in enumerate(order):
        at = (place * stride + first) * rows
        part = source[at : at + rows, :]
        part = part[:, : target.shape[1]].astype(target.dtype)
        target[origin * rows : (origin + 1) * rows, :] = part


def forward_kernel(
    heads,
    part_count,
    rows,
    order,
    order_rows,
    block,
    cnt,
    lst,
    offs,
    q_ref,
    code,
    anc_ref,
    pos_ref,
    *rest,
):
    parts = rest[:part_count]
    o_ref, low_ref, qs, os, held, right, acc, top, keys, sem = rest[part_count:]
    b = pl.program_id(0)
    width = heads * HEAD_DIM

    @pl.when(b == 0)
    def _():
        start_parts(offs, parts, held, sem, rows)
        right[...] = jnp.zeros_like(right)
        shuffle(q_ref, qs, order, order_rows, 0, 1)
        fill_keys(code, keys)
        wait_parts(parts, held, sem)

    acc[...] = jnp.zeros_like(acc)
    top[...] = jnp.full_like(top, FLOOR)
    at = pl.multiple_of(b * block, block)
    turned = turn(qs[pl.ds(at, block), :]).astype(jnp.bfloat16)
    for h in range(heads):
        right[h, 0:HEAD_DIM, :] = turned[h * HEAD_DIM : (h + 1) * HEAD_DIM]

    def step(start, masked):
        mask = None
        if masked:
            mask = visible(keys, anc_ref[...], pos_ref[...], start, KEY_BLOCK, block)
        scores = [matmul(held[h, pl.ds(start, KEY_BLOCK), :], right[h]) for h in range(heads)]
        signed, scales, sums = [], [], []
        for h in range(heads):
            s = scores[h]
            size = jnp.abs(s * LOG2E)
            if masked:
                size = jnp.where(mask, size, FLOOR)
            old = top[h]
            new = jnp.maximum(old, jnp.max(size, axis=0, keepdims=True))
            e = jnp.exp2(size - new)
            signed.append(e.astype(jnp.bfloat16) * sign_low(s))
            scales.append(jnp.exp2(old - new))
            top[h] = new
            sums.append(jnp.sum(e, axis=0, keepdims=True))
        for h in range(heads):
            out = matmul(held[h, pl.ds(start, KEY_BLOCK), HEAD_DIM:], signed[h], 0)
            acc[h, 0:HEAD_DIM, :] = acc[h, 0:HEAD_DIM, :] * scales[h] + out
            acc[h, HEAD_DIM : HEAD_DIM + 1, :] = (
                acc[h, HEAD_DIM : HEAD_DIM + 1, :] * scales[h] + sums[h]
            )

    sweep(cnt, lst, b, KEY_BLOCK, step)
    outs, logs = [], []
    for h in range(heads):
        weight = acc[h, HEAD_DIM : HEAD_DIM + 1, :]
        outs.append(acc[h, 0:HEAD_DIM, :] / weight)
        logs.append(top[h] + jnp.log2(weight))
    fill = jnp.zeros((os.shape[1] - width - heads, block), jnp.float32)
    os[pl.ds(at, block), :] = jnp.concatenate(outs + logs + [fill], axis=0).T

    @pl.when(b == pl.num_programs(0) - 1)
    def _():
        unshuffle(os, o_ref, order, order_rows, 0, 1)
        unshuffle(os, low_ref, order, order_rows, 0, 1)


def query_block(count, whole_count=None):
    return 256 if count % 256 == 0 else whole_count or count


def whole(shape):
    return pl.BlockSpec(shape, lambda b, *_: (0,) * len(shape))


def lanes(size):
    return pl.BlockSpec((1, size), lambda b, *_: (0, b))


def stat_width(heads):
    return -(-(heads * HEAD_DIM + heads) // 128) * 128


def work(passes, count, all_keys, heads):
    return pl.CostEstimate(
        flops=2 * passes * count * all_keys * 256 * heads,
        bytes_accessed=4 * heads * all_keys * 2 * HEAD_DIM,
        transcendentals=count * all_keys * heads,
    )


def attend_forward(cnt, lst, offs, q, code, anc, pos, parts, rows, order, order_rows):
    count, width = q.shape
    heads = width // HEAD_DIM
    all_keys = code.shape[1]
    block = query_block(count)
    part_count = len(parts)
    full = stat_width(heads)
    return pl.pallas_call(
        functools.partial(forward_kernel, heads, part_count, rows, order, order_rows, block),
        out_shape=(
            jax.ShapeDtypeStruct((count, full), jnp.float32),
            jax.ShapeDtypeStruct((count, width), jnp.bfloat16),
        ),
        grid_spec=pltpu.PrefetchScalarGridSpec(
            num_scalar_prefetch=3,
            grid=(count // block,),
            in_specs=[whole((count, width)), whole((1, all_keys)), lanes(block), lanes(block)]
            + [pl.BlockSpec(memory_space=pl.ANY)] * part_count,
            out_specs=[whole((count, full)), whole((count, width))],
            scratch_shapes=[
                pltpu.VMEM((count, width), jnp.bfloat16),
                pltpu.VMEM((count, full), jnp.float32),
                pltpu.VMEM((heads, all_keys, 2 * HEAD_DIM), jnp.bfloat16),
                pltpu.VMEM((heads, 2 * HEAD_DIM, block), jnp.bfloat16),
                pltpu.VMEM((heads, HEAD_DIM + 8, block), jnp.float32),
                pltpu.VMEM((heads, 1, block), jnp.float32),
                pltpu.VMEM((all_keys, 128), jnp.int32),
                pltpu.SemaphoreType.DMA((part_count,)),
            ],
        ),
        compiler_params=pltpu.CompilerParams(vmem_limit_bytes=VMEM_BYTES),
        cost_estimate=work(4, count, all_keys, heads),
    )(cnt, lst, offs, q, code, anc, pos, *parts)


def backward_kernel(
    heads,
    part_count,
    rows,
    order,
    order_rows,
    block,
    cnt,
    lst,
    offs,
    q_own,
    q_other,
    g_own,
    g_other,
    o_own,
    o_other,
    code,
    anc_ref,
    pos_ref,
    *rest,
):
    parts, (dq_own, dq_other, grads) = rest[:part_count], rest[part_count : part_count + 3]
    qs, gs, os, held, right, left, acc, dqs, dsum, stat, keys, sem, out_sem = rest[part_count + 3 :]
    b = pl.program_id(0)
    width = heads * HEAD_DIM

    @pl.when(b == 0)
    def _():
        start_parts(offs, parts, held, sem, rows)
        left[...] = jnp.zeros_like(left)
        right[...] = jnp.zeros_like(right)
        acc[...] = jnp.zeros_like(acc)
        shuffle(q_own, qs, order, order_rows)
        shuffle(q_other, qs, order, order_rows, 1)
        shuffle(g_own, gs, order, order_rows)
        shuffle(g_other, gs, order, order_rows, 1)
        shuffle(o_own, os, order, order_rows)
        shuffle(o_other, os, order, order_rows, 1)
        fill_keys(code, keys)
        wait_parts(parts, held, sem)

    dqs[...] = jnp.zeros_like(dqs)
    at = pl.multiple_of(b * block, block)
    q, g = qs[pl.ds(at, block), :], gs[pl.ds(at, block), :]
    turned_o = os[pl.ds(at, block), :].T
    turned_q = turn(q).astype(jnp.bfloat16)
    turned_g = turn(g)
    for h in range(heads):
        span = slice(h * HEAD_DIM, (h + 1) * HEAD_DIM)
        left[h, 0:block, 0:HEAD_DIM] = q[:, span]
        left[h, block:, HEAD_DIM:] = g[:, span]
        right[h, 0:HEAD_DIM, 0:block] = turned_q[span]
        right[h, HEAD_DIM:, block:] = turned_g[span].astype(jnp.bfloat16)
        stat[h : h + 1, :] = turned_o[width + h : width + h + 1]
        stat[8 + h : 9 + h, :] = jnp.sum(turned_g[span] * turned_o[span], axis=0, keepdims=True)

    def step(start, masked):
        mask = None
        if masked:
            mask = visible(keys, anc_ref[...], pos_ref[...], start, KEY_BLOCK_BACK, block)
        units = [(h, at) for at in range(0, KEY_BLOCK_BACK, SUB_BLOCK) for h in range(heads)]

        def scores(h, at):
            both = matmul(held[h, pl.ds(start + at, SUB_BLOCK), :], right[h])
            return both[:, :block], both[:, block:]

        def gradients(h, at, s, dp):
            e = jnp.exp2(jnp.abs(s * LOG2E) - stat[h : h + 1, :])
            if masked:
                e = jnp.where(mask[at : at + SUB_BLOCK], e, 0.0)
            sign = sign_low(s)
            signed = e.astype(jnp.bfloat16) * sign
            delta = stat[8 + h : 9 + h, :]
            ds = (e * (dp - sign.astype(jnp.float32) * delta)).astype(jnp.bfloat16)
            return ds, signed

        def gather_up(h, at, ds, signed):
            spot = pl.ds(start + at, SUB_BLOCK)
            acc[h, spot, :] += matmul(jnp.concatenate([ds, signed], axis=1), left[h])
            dqs[h] += matmul(held[h, spot, 0:HEAD_DIM], ds, 0)

        ready = [scores(*unit) for unit in units[:AHEAD]]
        last = None
        for i, unit in enumerate(units):
            if i + AHEAD < len(units):
                ready.append(scores(*units[i + AHEAD]))
            pair = gradients(*unit, *ready[i])
            if last is not None:
                gather_up(*last)
            last = unit + pair
        gather_up(*last)

    sweep(cnt, lst, b, KEY_BLOCK_BACK, step)
    fill = jnp.zeros((dsum.shape[1] - width, block), jnp.float32)
    dsum[pl.ds(at, block), :] = (
        jnp.concatenate([dqs[h] for h in range(heads)] + [fill], axis=0).T * 0.125
    )

    @pl.when(b == pl.num_programs(0) - 1)
    def _():
        store_grads(acc, held, grads, out_sem)
        unshuffle(dsum, dq_own, order, order_rows)
        unshuffle(dsum, dq_other, order, order_rows, 1)


def attend_backward(
    cnt, lst, offs, q, g, o, code, anc, pos, parts, rows, order, order_rows, grad_shape
):
    own, width = q[0].shape
    count = 2 * own
    heads = width // HEAD_DIM
    all_keys = code.shape[1]
    block = query_block(own, count)
    part_count = len(parts)
    full = o[0].shape[1]
    return pl.pallas_call(
        functools.partial(backward_kernel, heads, part_count, rows, order, order_rows, block),
        out_shape=(
            jax.ShapeDtypeStruct((own, full), jnp.float32),
            jax.ShapeDtypeStruct((own, full), jnp.float32),
            jax.ShapeDtypeStruct(grad_shape, jnp.bfloat16),
        ),
        grid_spec=pltpu.PrefetchScalarGridSpec(
            num_scalar_prefetch=3,
            grid=(count // block,),
            in_specs=[
                whole((own, width)),
                whole((own, width)),
                whole((own, width)),
                whole((own, width)),
                whole((own, full)),
                whole((own, full)),
                whole((1, all_keys)),
                lanes(block),
                lanes(block),
            ]
            + [pl.BlockSpec(memory_space=pl.ANY)] * part_count,
            out_specs=[whole((own, full)), whole((own, full)), pl.BlockSpec(memory_space=pl.ANY)],
            scratch_shapes=[
                pltpu.VMEM((count, width), jnp.bfloat16),
                pltpu.VMEM((count, width), jnp.bfloat16),
                pltpu.VMEM((count, full), jnp.float32),
                pltpu.VMEM((heads, all_keys, 2 * HEAD_DIM), jnp.bfloat16),
                pltpu.VMEM((heads, 2 * HEAD_DIM, 2 * block), jnp.bfloat16),
                pltpu.VMEM((heads, 2 * block, 2 * HEAD_DIM), jnp.bfloat16),
                pltpu.VMEM((heads, all_keys, 2 * HEAD_DIM), jnp.float32),
                pltpu.VMEM((heads, HEAD_DIM, block), jnp.float32),
                pltpu.VMEM((count, full), jnp.float32),
                pltpu.VMEM((16, block), jnp.float32),
                pltpu.VMEM((all_keys, 128), jnp.int32),
                pltpu.SemaphoreType.DMA((part_count,)),
                pltpu.SemaphoreType.DMA,
            ],
        ),
        compiler_params=pltpu.CompilerParams(vmem_limit_bytes=VMEM_BYTES),
        cost_estimate=work(5, count, all_keys, heads),
    )(cnt, lst, offs, *q, *g, *o, code, anc, pos, *parts)


def swap(value, axis, step):
    count = lax.axis_size(axis)
    return lax.ppermute(value, axis, [(source, source ^ step) for source in range(count)])


def exchange(pieces, axis):
    return [pieces[0]] + [swap(pieces[step], axis, step) for step in range(1, len(pieces))]


def gather(value, axis):
    return exchange([value] * lax.axis_size(axis), axis)


def after(value, *others):
    return lax.optimization_barrier((value,) + others)[0]


def pick(values, index, axis=0):
    return lax.dynamic_index_in_dim(values, index, axis, keepdims=False)


def reorder(pieces, index):
    stacked = jnp.stack(pieces)
    return jnp.stack([pick(stacked, index ^ place) for place in range(len(pieces))])


def total(pieces):
    result = pieces[0].astype(jnp.float32)
    for piece in pieces[1:]:
        result = result + piece.astype(jnp.float32)
    return result


def low(value):
    return value.astype(jnp.bfloat16)


def dot(left, right, left_dim=1, right_dim=0):
    return lax.dot_general(
        left, right, (((left_dim,), (right_dim,)), ((), ())), preferred_element_type=jnp.float32
    )


def trade(values, axis):
    return lax.all_to_all(values, axis, 0, 0)


def share(value, axis):
    return trade(jnp.broadcast_to(value[None], (lax.axis_size(axis),) + value.shape), axis)


def spread(columns, extra, cores, rows):
    features, tokens = columns.shape
    piece = tokens // (cores * rows)
    turned = columns.reshape(features, cores * rows, piece).transpose(1, 2, 0)
    if extra is not None:
        fill = jnp.broadcast_to(extra[None], (cores * rows,) + extra.shape)
        turned = jnp.concatenate([turned, fill], axis=1)
    got = trade(turned, ("dp", "row")).reshape(cores, rows, -1, features)
    held = got[:, :, :piece].transpose(0, 2, 1, 3).reshape(cores * piece, rows * features)
    if extra is None:
        return held
    return held, got[0, :, piece:].transpose(1, 0, 2).reshape(-1, rows * features)


def by_device(values, cores, rows):
    features = values.shape[1] // rows
    sent = values.reshape(cores, -1, rows, features).transpose(0, 2, 1, 3)
    return sent.reshape(cores * rows, -1, features)


def collect(first, second, extra, cores, rows):
    second = by_device(second, cores, rows)
    _, piece, features = second.shape
    sent = jnp.concatenate([first, second], axis=2)
    lines = extra.reshape(-1, 2, rows, features).transpose(2, 0, 1, 3).reshape(rows, -1, 2 * features)
    lines = jnp.pad(lines, ((0, 0), (0, 16 - lines.shape[1]), (0, 0)))
    lines = jnp.broadcast_to(lines[None], (cores,) + lines.shape)
    lines = lines.reshape((cores * rows,) + lines.shape[2:])
    got = trade(jnp.concatenate([sent, lines], axis=1), ("dp", "row"))
    turned = got[:, :piece].transpose(2, 0, 1).reshape(2, features, -1).astype(jnp.float32)
    sums = jnp.sum(got[:, piece:].astype(jnp.float32), axis=0)
    return turned[0], turned[1], sums


def norm_forward(inputs, gain, shift):
    average = jnp.mean(inputs, axis=1, keepdims=True)
    squares = jnp.mean(inputs * inputs, axis=1, keepdims=True)
    spread_rows = lax.rsqrt(squares - average * average + 1e-05)
    unit = (inputs - average) * spread_rows
    return low(unit * gain + shift), unit, spread_rows


def norm_backward(grad, unit, spread_rows, gain):
    scaled = grad * gain
    return spread_rows * (
        scaled
        - jnp.mean(scaled, axis=1, keepdims=True)
        - unit * jnp.mean(scaled * unit, axis=1, keepdims=True)
    )


def gelu_tanh(hidden):
    return jax.nn.gelu(hidden, approximate=True)


def everywhere(value, axis):
    return total(gather(value, axis))


def side_by_side(pieces):
    return pieces.transpose(1, 0, 2).reshape(pieces.shape[1], -1)


def three_low(value):
    first = low(value)
    second = low(value - first.astype(jnp.float32))
    third = low(value - first.astype(jnp.float32) - second.astype(jnp.float32))
    return jnp.stack([first, second, third])


def block_lists(hot, places, anc, pos, key_block, query_rows):
    def reduce(values, size, start, op):
        return lax.reduce(values.reshape(-1, size), jnp.int32(start), op, (1,))

    keys = hot.shape[0] // key_block
    key_or = reduce(hot, key_block, 0, lax.bitwise_or)[None]
    start = jnp.min(places.reshape(-1, key_block), axis=1)[None]
    end = jnp.max(places.reshape(-1, key_block), axis=1)[None]
    anc_or = reduce(anc, query_rows, 0, lax.bitwise_or)[:, None]
    anc_and = reduce(anc, query_rows, -1, lax.bitwise_and)[:, None]
    first = jnp.min(pos.reshape(-1, query_rows), axis=1)[:, None]
    last = jnp.max(pos.reshape(-1, query_rows), axis=1)[:, None]
    full = ((key_or & ~anc_and) == 0) & (end <= first)
    some = (((key_or & anc_or) != 0) & (start <= last)) | full
    numbers = jnp.arange(keys, dtype=jnp.int32)
    code = jnp.where(full, 0, jnp.where(some, 1, 2)) * keys + numbers[None]
    rank = jnp.sum((code[:, None, :] < code[:, :, None]).astype(jnp.int32), axis=2)
    order = jnp.sum(
        jnp.where(rank[:, None, :] == numbers[None, :, None], numbers[None, None], 0), axis=2
    )
    counts = jnp.stack(
        [jnp.sum(full.astype(jnp.int32), axis=1), jnp.sum(some.astype(jnp.int32), axis=1)], axis=1
    )
    return counts.astype(jnp.int32), order.astype(jnp.int32)


def shards(
    block_input,
    segment_ids,
    parent_ids,
    attn_gain,
    attn_shift,
    qkv_weight,
    qkv_bias,
    proj_weight,
    proj_bias,
    mlp_gain,
    mlp_shift,
    up_weight,
    up_bias,
    down_weight,
    down_bias,
    cotangent,
):
    cores, rows, cols = lax.axis_size("dp"), lax.axis_size("row"), lax.axis_size("col")
    core, row, col = lax.axis_index("dp"), lax.axis_index("row"), lax.axis_index("col")
    features, tokens = block_input.shape
    half = tokens // cores
    piece = half // rows
    own = cores * piece
    width_all = rows * features
    heads = qkv_weight.shape[1]
    width = heads * HEAD_DIM
    head_width = 2 * HEAD_DIM
    hidden_part = up_weight.shape[1] // cores
    head_part = width // cores
    segments = parent_ids.shape[0]
    queries = cols * own
    block_rows = query_block(queries)
    whole_chunks = piece % 16 == 0

    vectors = jnp.stack([attn_gain, attn_shift, mlp_gain, mlp_shift, proj_bias, down_bias])
    vectors = jnp.pad(vectors, ((0, 2), (0, 0)))
    layer_in, vectors = spread(block_input, vectors, cores, rows)

    packed = low(qkv_weight).reshape(3, heads, features, HEAD_DIM)
    qkv_low = jnp.concatenate(
        [packed[kind, h] for h in range(heads) for kind in (1, 2)]
        + [packed[0, h] for h in range(heads)],
        axis=1,
    )
    bias = qkv_bias.reshape(3, heads, HEAD_DIM)
    bias_row = jnp.concatenate(
        [bias[kind, h] for h in range(heads) for kind in (1, 2)] + [bias[0].reshape(-1)]
    )

    proj_low = (
        low(proj_weight).reshape(heads, features, HEAD_DIM).transpose(0, 2, 1)
    ).reshape(width, features)
    up_low, down_low = [
        lax.dynamic_slice_in_dim(low(w), core * hidden_part, hidden_part, 1)
        for w in (up_weight, down_weight)
    ]
    up_bias_part = three_low(lax.dynamic_slice_in_dim(up_bias, core * hidden_part, hidden_part, 0))
    bias_rows = jnp.pad(up_bias_part, ((0, 13), (0, 0)))
    mlp_low = jnp.concatenate([up_low, down_low, bias_rows], axis=0)
    mlp_cols = jnp.concatenate(gather(mlp_low, "col"), axis=1)
    proj_full = (
        lax.all_gather(proj_low, ("row", "col"))
        .reshape(rows, cols * width, features)
        .transpose(1, 0, 2)
        .reshape(cols * width, width_all)
    )
    sent_rows = 2 * features
    up_bias_full = jnp.sum(mlp_cols[sent_rows : sent_rows + 3].astype(jnp.float32), axis=0)

    ones = jnp.int32(1)
    tables = jnp.arange(segments, dtype=jnp.int32)
    grand_ids = jnp.sum(
        jnp.where(parent_ids[:, None] == tables[None], parent_ids[None], 0), axis=1
    )
    anc_table = (
        jnp.left_shift(ones, tables)
        | jnp.left_shift(ones, parent_ids)
        | jnp.left_shift(ones, grand_ids)
    )
    all_places = jnp.arange(segment_ids.shape[0], dtype=jnp.int32)
    hot_all = jnp.left_shift(ones, segment_ids)
    anc_all = jnp.sum(
        jnp.where(segment_ids[None] == tables[:, None], anc_table[:, None], 0), axis=0
    )
    chunk_ids = [(c, e) for c in range(cols) for e in range(cores)]
    if whole_chunks:
        inner = [(c, e) for e in range(cores) for c in range(cols)]
    else:
        inner = chunk_ids
    order = [chunk_ids.index(chunk) for chunk in inner]
    order_rows = piece
    if not whole_chunks:
        order, order_rows = [0], queries

    def query_info(which):
        starts = [
            (e * cols + c) * tokens + which * half + row * piece for c, e in inner
        ]
        anc = [lax.dynamic_slice_in_dim(anc_all, s, piece, 0) for s in starts]
        pos = [s + jnp.arange(piece, dtype=jnp.int32) for s in starts]
        return anc, pos

    anc_own, pos_own = query_info(core)
    anc_other, pos_other = query_info(core ^ 1)
    if whole_chunks:
        anc_both = [chunk for pair in zip(anc_own, anc_other) for chunk in pair]
        pos_both = [chunk for pair in zip(pos_own, pos_other) for chunk in pair]
    else:
        anc_both, pos_both = anc_own + anc_other, pos_own + pos_other
    anc, anc_both = jnp.concatenate(anc_own), jnp.concatenate(anc_both)
    pos = jnp.concatenate(pos_own).astype(jnp.int32)
    pos_both = jnp.concatenate(pos_both).astype(jnp.int32)
    limit = ((pos + 1) << segments) - 1
    limit_both = ((pos_both + 1) << segments) - 1
    codes = (all_places << segments) | hot_all
    core_places = pick(all_places.reshape(-1, cores, half), core, 1).reshape(-1)
    core_hot = pick(hot_all.reshape(-1, cores, half), core, 1).reshape(-1)
    core_codes = (core_places << segments) | core_hot
    lists_forward = block_lists(
        hot_all, all_places, anc, pos, KEY_BLOCK, block_rows
    )
    lists_backward = block_lists(
        core_hot, core_places, anc_both, pos_both, KEY_BLOCK_BACK, query_block(queries, 2 * queries)
    )
    rows_forward = (anc[None], limit[None])
    rows_backward = (anc_both[None], limit_both[None])
    setup = (lists_forward, lists_backward, rows_forward, rows_backward, codes[None], core_codes[None])

    layer_in, qkv_low, setup, mlp_cols = lax.optimization_barrier(
        (layer_in, qkv_low, setup, mlp_cols)
    )
    lists_forward, lists_backward, rows_forward, rows_backward, codes, core_codes = setup
    qkv_full = share(qkv_low, "row").reshape(width_all, 3 * width)
    normed_in, first_unit, first_spread = norm_forward(layer_in, vectors[0], vectors[1])
    normed_all = reorder(gather(normed_in, "col"), col).reshape(queries, width_all)
    cot_rows = spread(after(cotangent, normed_in, qkv_full), None, cores, rows)
    cot_low = low(cot_rows)
    normed_all, cot_low = lax.optimization_barrier((normed_all, cot_low))
    qkv = low(dot(normed_all, qkv_full) + bias_row)
    kv_own = jnp.stack([qkv[:, h * head_width : (h + 1) * head_width] for h in range(heads)])
    q_own = qkv[:, 2 * width :] * jnp.bfloat16(0.125)
    core_parts = gather(kv_own, "row")

    cot_both = jnp.concatenate(gather(cot_low, "dp"), axis=0)
    q_own, proj_full, cot_both, core_parts = lax.optimization_barrier(
        (q_own, proj_full, cot_both, core_parts)
    )
    parts = [part for held in core_parts for part in gather(held, "dp")]
    q_other = swap(q_own, "dp", 1)
    mlp_got = gather(after(mlp_cols[:sent_rows], *core_parts), "row")
    if whole_chunks:
        offsets = jnp.stack(
            [
                (e * cols + c) * tokens + (core ^ jd) * half + (row ^ k) * piece
                for k in range(rows)
                for jd in range(cores)
                for c, e in chunk_ids
            ]
        ).astype(jnp.int32)
        core_offsets = jnp.stack(
            [
                (e * cols + c) * half + (row ^ k) * piece
                for k in range(rows)
                for c, e in chunk_ids
            ]
        ).astype(jnp.int32)
        chunk, core_chunk = piece, piece
        grad_shape = (rows, heads, cols, cores, piece, head_width)
    else:

        def natural(pieces, count):
            sorted_parts = [
                [pieces[k * count + j] for j in range(count)] for k in range(rows)
            ]
            by_core = [reorder(p, core) if count > 1 else jnp.stack(p) for p in sorted_parts]
            stacked = reorder(by_core, row).reshape(
                rows, count, heads, cols, cores, piece, head_width
            )
            return [stacked.transpose(2, 4, 3, 1, 0, 5, 6).reshape(heads, -1, head_width)]

        parts, core_parts = natural(parts, cores), natural(core_parts, 1)
        offsets = core_offsets = jnp.zeros((1,), jnp.int32)
        chunk, core_chunk = parts[0].shape[1], core_parts[0].shape[1]
        grad_shape = core_parts[0].shape
    head_out, attended_low = attend_forward(
        *lists_forward,
        offsets,
        q_own,
        codes,
        *rows_forward,
        parts,
        chunk,
        order,
        order_rows,
    )
    attended_low, mlp_got = lax.optimization_barrier((attended_low, mlp_got))
    attended = side_by_side(trade(attended_low.reshape(cols, own, width), "col"))
    out_other = swap(head_out, "dp", 1)

    hidden_all = cols * hidden_part

    def by_row(first, count):
        whole_rows = jnp.zeros((rows, count, hidden_all), jnp.bfloat16)
        for k in range(rows):
            part = mlp_got[k][None, first : first + count]
            whole_rows = lax.dynamic_update_slice_in_dim(whole_rows, part, row ^ k, 0)
        return whole_rows

    up_full = by_row(0, features).reshape(width_all, hidden_all)
    down_full = by_row(features, features).reshape(width_all, hidden_all)
    branch = dot(attended, proj_full) + vectors[4]
    middle = layer_in + branch
    normed_mid, second_unit, second_spread = norm_forward(middle, vectors[2], vectors[3])
    mid_both = jnp.concatenate(gather(normed_mid, "dp"), axis=0)
    hidden = dot(mid_both, up_full) + up_bias_full
    activated = low(gelu_tanh(hidden))
    act_grad = dot(cot_both, down_full)
    hidden_grad = low(jax.vjp(gelu_tanh, hidden)[1](act_grad)[0])

    def own_sum(both):
        return total(exchange([both[j * own : (j + 1) * own] for j in range(cores)], "dp"))

    mid_norm_grad = own_sum(dot(hidden_grad, up_full, 1, 1))
    second_back = norm_backward(mid_norm_grad, second_unit, second_spread, vectors[2])
    middle_grad = cot_rows + second_back
    mid_low = low(middle_grad)
    attended_grad = low(dot(mid_low, proj_full, 1, 1))

    sent = attended_grad.reshape(own, cols, width).transpose(1, 0, 2)
    sent, hidden_late, cot_late, activated_late = lax.optimization_barrier(
        (sent, hidden_grad, cot_both, activated)
    )
    out_grad = trade(sent, "col").reshape(queries, width)
    grad_other = swap(out_grad, "dp", 1)

    up_grad = low(dot(mid_both, hidden_late, 0, 0))
    down_grad = low(dot(cot_late, activated_late, 0, 0))
    proj_grad = low(dot(attended, mid_low, 0, 0)).reshape(cols, cores, head_part, width_all)
    proj_sum = total([pick(proj_grad, core, 1), swap(pick(proj_grad, core ^ 1, 1), "dp", 1)])
    pack = hidden_part // features
    proj_sent = (
        low(proj_sum)
        .reshape(cols, pack, head_part // pack, rows, features)
        .transpose(3, 2, 0, 1, 4)
    )
    proj_sent = jnp.stack([pick(proj_sent, col ^ k, 2) for k in range(cols)], axis=2)
    proj_sent = proj_sent.reshape(rows, head_part // pack, cols * pack * features)
    bias_grad = low(jnp.sum(hidden_late, axis=0, dtype=jnp.float32))
    bias_sent = jnp.pad(bias_grad[None], ((0, 15), (0, 0)))
    up_grad = up_grad.reshape(rows, features, hidden_all)
    down_grad = down_grad.reshape(rows, features, hidden_all)
    grads_sent = [
        jnp.concatenate(
            [pick(part, row ^ k) for part in (up_grad, down_grad, proj_sent)] + [bias_sent], axis=0
        )
        for k in range(rows)
    ]
    grads_sent, rows_backward = lax.optimization_barrier((grads_sent, rows_backward))
    grads_got = exchange(grads_sent, "row")
    early = jnp.stack(
        [
            jnp.sum(mid_norm_grad * second_unit, axis=0),
            jnp.sum(mid_norm_grad, axis=0),
            jnp.sum(mid_low, axis=0, dtype=jnp.float32),
            jnp.sum(cot_low, axis=0, dtype=jnp.float32),
        ]
    )

    query_grad, query_grad_other, part_grads = attend_backward(
        *lists_backward,
        core_offsets,
        (q_own, q_other),
        (out_grad, grad_other),
        (head_out, out_other),
        core_codes,
        *rows_backward,
        core_parts,
        core_chunk,
        order,
        order_rows,
        grad_shape,
    )
    if not whole_chunks:
        part_grads = part_grads.reshape(heads, cores, cols, rows, piece, head_width)
        part_grads = part_grads.transpose(3, 0, 2, 1, 4, 5)

    part_grads, grads_got, activated_late = lax.optimization_barrier(
        (part_grads, grads_got, activated_late)
    )
    kv_got = trade(part_grads.reshape(rows, heads, queries, head_width), "row")
    kv_grad = low(jnp.sum(kv_got.astype(jnp.float32), axis=0))
    query_low = low((query_grad + swap(query_grad_other, "dp", 1))[:, :width])
    qkv_grad = jnp.concatenate([kv_grad[h] for h in range(heads)] + [query_low], axis=1)
    first_parts = low(dot(qkv_grad, qkv_full, 1, 1)).reshape(cols, own, width_all)
    row_sums = low(total(grads_got))
    col_sums = low(
        total(
            exchange(
                [
                    row_sums[:, k * hidden_part : (k + 1) * hidden_part]
                    for k in range(cols)
                ],
                "col",
            )
        )
    )
    mlp_both = dot(activated_late, down_full, 1, 1)
    mlp_out = own_sum(mlp_both) + vectors[5]
    output_rows = by_device(low(branch + mlp_out), cores, rows)
    first_parts, col_sums, output_rows, qkv_grad, early = lax.optimization_barrier(
        (first_parts, col_sums, output_rows, qkv_grad, early)
    )
    first_grad = jnp.sum(trade(first_parts, "col").astype(jnp.float32), axis=0)

    other_sums = swap(col_sums, "dp", 1)
    first_sums = jnp.where(core == 0, col_sums, other_sums).astype(jnp.float32)
    second_sums = jnp.where(core == 0, other_sums, col_sums).astype(jnp.float32)
    both_sums = jnp.concatenate([first_sums, second_sums], axis=1)
    up_weight_grad = both_sums[:features]
    down_weight_grad = both_sums[features : 2 * features]
    up_bias_grad = both_sums[2 * features + head_part // pack]

    def proj_rows(sums):
        values = sums[2 * features : 2 * features + head_part // pack]
        values = values[:, : pack * features].reshape(head_part // pack, pack, features)
        return values.transpose(1, 0, 2).reshape(head_part, features)

    proj_weight_grad = (
        jnp.concatenate([proj_rows(first_sums), proj_rows(second_sums)], axis=0)
        .reshape(heads, HEAD_DIM, features)
        .transpose(0, 2, 1)
        .reshape(heads, features * HEAD_DIM)
    )
    def vector_sums(values):
        pieces = values.reshape(-1, rows, features).transpose(1, 0, 2)
        summed = total(exchange([pick(pieces, row ^ k) for k in range(rows)], "row"))
        return everywhere(everywhere(summed, "col"), "dp")

    first_back = norm_backward(first_grad, first_unit, first_spread, vectors[0])
    late = jnp.stack([jnp.sum(first_grad * first_unit, axis=0), jnp.sum(first_grad, axis=0)])
    output_grown, input_grown, late_sums = collect(
        output_rows, low(second_back + first_back), three_low(late), cores, rows
    )
    block_output = block_input + output_grown
    input_grad = cotangent + input_grown
    late_sums = everywhere(jnp.sum(late_sums, axis=0).reshape(2, features), "col")
    sums = vector_sums(early)
    wide = low(dot(normed_all, qkv_grad, 0, 0)).reshape(rows, features, 3 * width)
    bias_part = low(jnp.sum(qkv_grad, axis=0, dtype=jnp.float32))
    bias_part = jnp.broadcast_to(
        jnp.pad(bias_part[None], ((0, 15), (0, 0)))[None], (rows, 16, 3 * width)
    )
    wide = jnp.concatenate([wide, bias_part], axis=1)
    wide_pieces = [pick(wide, row ^ k) for k in range(rows)]
    wide_sum = low(total(exchange(wide_pieces, "row")))
    wide_sum = everywhere(wide_sum, "dp")

    def unpacked(values):
        lead = values.shape[0]
        kv = values[:, : 2 * width].reshape(lead, heads, 2, HEAD_DIM).transpose(2, 1, 0, 3)
        q = values[:, 2 * width :].reshape(lead, heads, HEAD_DIM).transpose(1, 0, 2)
        return jnp.concatenate([q[None], kv], axis=0)

    qkv_weight_grad = unpacked(wide_sum[:features]).reshape(3, heads, features * HEAD_DIM)
    qkv_bias_grad = unpacked(wide_sum[features : features + 1]).reshape(3, width)
    return (
        block_output,
        input_grad,
        late_sums[0],
        late_sums[1],
        qkv_weight_grad,
        qkv_bias_grad,
        proj_weight_grad,
        sums[2],
        sums[0],
        sums[1],
        up_weight_grad,
        up_bias_grad,
        down_weight_grad,
        sums[3],
    )


def solution(mesh):
    return jax.shard_map(
        shards,
        mesh=mesh,
        in_specs=(
            P("row", ("dp", "col")),
            P(),
            P(),
            P("row"),
            P("row"),
            P(None, "col", "row"),
            P(None, "col"),
            P("col", "row"),
            P("row"),
            P("row"),
            P("row"),
            P("row", "col"),
            P("col"),
            P("row", "col"),
            P("row"),
            P("row", ("dp", "col")),
        ),
        out_specs=(
            P("row", ("dp", "col")),
            P("row", ("dp", "col")),
            P("row"),
            P("row"),
            P(None, "col", "row"),
            P(None, "col"),
            P("col", "row"),
            P("row"),
            P("row"),
            P("row"),
            P("row", "col"),
            P("col"),
            P("row", "col"),
            P("row"),
        ),
        check_vma=False,
    )
```

```python
import functools

import jax
import jax.numpy as jnp
from jax import lax
from jax.experimental import pallas as pl
from jax.experimental.pallas import tpu as pltpu
from jax.sharding import PartitionSpec as P

HEAD_DIM = 64
LOG2E = 1.4426950408889634
BIG = 2.0**126
FLOOR = -1e30
KEY_BLOCK = 512
KEY_BLOCK_BACK = 512
SUB_BLOCK = 128
AHEAD = 2
VMEM_BYTES = 56 * 1024 * 1024


def sign_low(s):
    scaled = s.astype(jnp.bfloat16) * jnp.bfloat16(BIG)
    return jnp.minimum(jnp.maximum(scaled, jnp.bfloat16(-1)), jnp.bfloat16(1))


def matmul(a, b, left=1):
    return lax.dot_general(a, b, (((left,), (0,)), ((), ())), preferred_element_type=jnp.float32)


def start_parts(offs, parts, held, sem, rows):
    chunks = parts[0].shape[1] // rows
    for p, part in enumerate(parts):
        for c in range(chunks):
            start = pl.multiple_of(offs[p * chunks + c], rows)
            pltpu.make_async_copy(
                part.at[:, pl.ds(c * rows, rows), :], held.at[:, pl.ds(start, rows), :], sem.at[p]
            ).start()


def wait_parts(parts, held, sem):
    for p, part in enumerate(parts):
        pltpu.make_async_copy(part, held.at[:, pl.ds(0, part.shape[1]), :], sem.at[p]).wait()


def lower(acc, held, first, count):
    for h in range(held.shape[0]):
        held[h, pl.ds(first, count), :] = acc[h, pl.ds(first, count), :].astype(jnp.bfloat16)


def store_grads(acc, held, grads, sem):
    if len(grads.shape) == 3:
        lower(acc, held, 0, held.shape[1])
        pltpu.make_async_copy(held, grads, sem).start()
    else:
        groups, _, cols, pair, rows, _ = grads.shape
        for e in range(pair):
            for c in range(cols):
                first = (e * cols + c) * groups * rows
                lower(acc, held, first, groups * rows)
                for r in range(groups):
                    pltpu.make_async_copy(
                        held.at[:, pl.ds(first + r * rows, rows), :],
                        grads.at[r, :, c, e, :, :],
                        sem,
                    ).start()
    pltpu.make_async_copy(held, held, sem).wait()


def visible(keys, anc, pos, start, block, queries):
    repeat = -(-queries // 128)
    codes = jnp.concatenate([keys[pl.ds(start, block), :]] * repeat, axis=1)[:, :queries]
    return ((codes & anc) != 0) & (codes <= pos)


def fill_keys(code, keys):
    def fill(i, carry):
        at = pl.multiple_of(i * 128, 128)
        keys[pl.ds(at, 128), :] = jnp.broadcast_to(code[:, pl.ds(at, 128)], (128, 128)).T
        return carry

    lax.fori_loop(0, keys.shape[0] // 128, fill, 0, unroll=8)


def turn(block):
    return block.astype(jnp.float32).T


def sweep(counts, lists, b, key_block, step):
    full, some = counts[b, 0], counts[b, 1]

    def start(i):
        return pl.multiple_of(lists[b, i] * key_block, key_block)

    def plain(i, carry):
        step(start(i), False)
        return carry

    def masked(i, carry):
        step(start(i), True)
        return carry

    lax.fori_loop(0, full, plain, 0)
    lax.fori_loop(full, some, masked, 0)


def shuffle(source, target, order, rows, first=0, stride=2):
    for place, origin in enumerate(order):
        at = (place * stride + first) * rows
        target[at : at + rows, :] = source[origin * rows : (origin + 1) * rows, :]


def unshuffle(source, target, order, rows, first=0, stride=2):
    for place, origin in enumerate(order):
        at = (place * stride + first) * rows
        part = source[at : at + rows, :]
        part = part[:, : target.shape[1]].astype(target.dtype)
        target[origin * rows : (origin + 1) * rows, :] = part


def forward_kernel(
    heads,
    part_count,
    rows,
    order,
    order_rows,
    block,
    cnt,
    lst,
    offs,
    q_ref,
    code,
    anc_ref,
    pos_ref,
    *rest,
):
    parts = rest[:part_count]
    o_ref, low_ref, qs, os, held, right, acc, top, keys, sem = rest[part_count:]
    b = pl.program_id(0)
    width = heads * HEAD_DIM

    @pl.when(b == 0)
    def _():
        start_parts(offs, parts, held, sem, rows)
        right[...] = jnp.zeros_like(right)
        shuffle(q_ref, qs, order, order_rows, 0, 1)
        fill_keys(code, keys)
        wait_parts(parts, held, sem)

    acc[...] = jnp.zeros_like(acc)
    top[...] = jnp.full_like(top, FLOOR)
    at = pl.multiple_of(b * block, block)
    turned = turn(qs[pl.ds(at, block), :]).astype(jnp.bfloat16)
    for h in range(heads):
        right[h, 0:HEAD_DIM, :] = turned[h * HEAD_DIM : (h + 1) * HEAD_DIM]

    def step(start, masked):
        mask = None
        if masked:
            mask = visible(keys, anc_ref[...], pos_ref[...], start, KEY_BLOCK, block)
        scores = [matmul(held[h, pl.ds(start, KEY_BLOCK), :], right[h]) for h in range(heads)]
        signed, scales, sums = [], [], []
        for h in range(heads):
            s = scores[h]
            size = jnp.abs(s * LOG2E)
            if masked:
                size = jnp.where(mask, size, FLOOR)
            old = top[h]
            new = jnp.maximum(old, jnp.max(size, axis=0, keepdims=True))
            e = jnp.exp2(size - new)
            signed.append(e.astype(jnp.bfloat16) * sign_low(s))
            scales.append(jnp.exp2(old - new))
            top[h] = new
            sums.append(jnp.sum(e, axis=0, keepdims=True))
        for h in range(heads):
            out = matmul(held[h, pl.ds(start, KEY_BLOCK), HEAD_DIM:], signed[h], 0)
            acc[h, 0:HEAD_DIM, :] = acc[h, 0:HEAD_DIM, :] * scales[h] + out
            acc[h, HEAD_DIM : HEAD_DIM + 1, :] = (
                acc[h, HEAD_DIM : HEAD_DIM + 1, :] * scales[h] + sums[h]
            )

    sweep(cnt, lst, b, KEY_BLOCK, step)
    outs, logs = [], []
    for h in range(heads):
        weight = acc[h, HEAD_DIM : HEAD_DIM + 1, :]
        outs.append(acc[h, 0:HEAD_DIM, :] / weight)
        logs.append(top[h] + jnp.log2(weight))
    fill = jnp.zeros((os.shape[1] - width - heads, block), jnp.float32)
    os[pl.ds(at, block), :] = jnp.concatenate(outs + logs + [fill], axis=0).T

    @pl.when(b == pl.num_programs(0) - 1)
    def _():
        unshuffle(os, o_ref, order, order_rows, 0, 1)
        unshuffle(os, low_ref, order, order_rows, 0, 1)


def query_block(count, whole_count=None):
    return 256 if count % 256 == 0 else whole_count or count


def whole(shape):
    return pl.BlockSpec(shape, lambda b, *_: (0,) * len(shape))


def lanes(size):
    return pl.BlockSpec((1, size), lambda b, *_: (0, b))


def stat_width(heads):
    return -(-(heads * HEAD_DIM + heads) // 128) * 128


def work(passes, count, all_keys, heads):
    return pl.CostEstimate(
        flops=2 * passes * count * all_keys * 256 * heads,
        bytes_accessed=4 * heads * all_keys * 2 * HEAD_DIM,
        transcendentals=count * all_keys * heads,
    )


def attend_forward(cnt, lst, offs, q, code, anc, pos, parts, rows, order, order_rows):
    count, width = q.shape
    heads = width // HEAD_DIM
    all_keys = code.shape[1]
    block = query_block(count)
    part_count = len(parts)
    full = stat_width(heads)
    return pl.pallas_call(
        functools.partial(forward_kernel, heads, part_count, rows, order, order_rows, block),
        out_shape=(
            jax.ShapeDtypeStruct((count, full), jnp.float32),
            jax.ShapeDtypeStruct((count, width), jnp.bfloat16),
        ),
        grid_spec=pltpu.PrefetchScalarGridSpec(
            num_scalar_prefetch=3,
            grid=(count // block,),
            in_specs=[whole((count, width)), whole((1, all_keys)), lanes(block), lanes(block)]
            + [pl.BlockSpec(memory_space=pl.ANY)] * part_count,
            out_specs=[whole((count, full)), whole((count, width))],
            scratch_shapes=[
                pltpu.VMEM((count, width), jnp.bfloat16),
                pltpu.VMEM((count, full), jnp.float32),
                pltpu.VMEM((heads, all_keys, 2 * HEAD_DIM), jnp.bfloat16),
                pltpu.VMEM((heads, 2 * HEAD_DIM, block), jnp.bfloat16),
                pltpu.VMEM((heads, HEAD_DIM + 8, block), jnp.float32),
                pltpu.VMEM((heads, 1, block), jnp.float32),
                pltpu.VMEM((all_keys, 128), jnp.int32),
                pltpu.SemaphoreType.DMA((part_count,)),
            ],
        ),
        compiler_params=pltpu.CompilerParams(vmem_limit_bytes=VMEM_BYTES),
        cost_estimate=work(4, count, all_keys, heads),
    )(cnt, lst, offs, q, code, anc, pos, *parts)


def backward_kernel(
    heads,
    part_count,
    rows,
    order,
    order_rows,
    block,
    cnt,
    lst,
    offs,
    q_own,
    q_other,
    g_own,
    g_other,
    o_own,
    o_other,
    code,
    anc_ref,
    pos_ref,
    *rest,
):
    parts, (dq_own, dq_other, grads) = rest[:part_count], rest[part_count : part_count + 3]
    qs, gs, os, held, right, left, acc, dqs, dsum, stat, keys, sem, out_sem = rest[part_count + 3 :]
    b = pl.program_id(0)
    width = heads * HEAD_DIM

    @pl.when(b == 0)
    def _():
        start_parts(offs, parts, held, sem, rows)
        left[...] = jnp.zeros_like(left)
        right[...] = jnp.zeros_like(right)
        acc[...] = jnp.zeros_like(acc)
        shuffle(q_own, qs, order, order_rows)
        shuffle(q_other, qs, order, order_rows, 1)
        shuffle(g_own, gs, order, order_rows)
        shuffle(g_other, gs, order, order_rows, 1)
        shuffle(o_own, os, order, order_rows)
        shuffle(o_other, os, order, order_rows, 1)
        fill_keys(code, keys)
        wait_parts(parts, held, sem)

    dqs[...] = jnp.zeros_like(dqs)
    at = pl.multiple_of(b * block, block)
    q, g = qs[pl.ds(at, block), :], gs[pl.ds(at, block), :]
    turned_o = os[pl.ds(at, block), :].T
    turned_q = turn(q).astype(jnp.bfloat16)
    turned_g = turn(g)
    for h in range(heads):
        span = slice(h * HEAD_DIM, (h + 1) * HEAD_DIM)
        left[h, 0:block, 0:HEAD_DIM] = q[:, span]
        left[h, block:, HEAD_DIM:] = g[:, span]
        right[h, 0:HEAD_DIM, 0:block] = turned_q[span]
        right[h, HEAD_DIM:, block:] = turned_g[span].astype(jnp.bfloat16)
        stat[h : h + 1, :] = turned_o[width + h : width + h + 1]
        stat[8 + h : 9 + h, :] = jnp.sum(turned_g[span] * turned_o[span], axis=0, keepdims=True)

    def step(start, masked):
        mask = None
        if masked:
            mask = visible(keys, anc_ref[...], pos_ref[...], start, KEY_BLOCK_BACK, block)
        units = [(h, at) for at in range(0, KEY_BLOCK_BACK, SUB_BLOCK) for h in range(heads)]

        def scores(h, at):
            both = matmul(held[h, pl.ds(start + at, SUB_BLOCK), :], right[h])
            return both[:, :block], both[:, block:]

        def gradients(h, at, s, dp):
            e = jnp.exp2(jnp.abs(s * LOG2E) - stat[h : h + 1, :])
            if masked:
                e = jnp.where(mask[at : at + SUB_BLOCK], e, 0.0)
            sign = sign_low(s)
            signed = e.astype(jnp.bfloat16) * sign
            delta = stat[8 + h : 9 + h, :]
            ds = (e * (dp - sign.astype(jnp.float32) * delta)).astype(jnp.bfloat16)
            return ds, signed

        def gather_up(h, at, ds, signed):
            spot = pl.ds(start + at, SUB_BLOCK)
            acc[h, spot, :] += matmul(jnp.concatenate([ds, signed], axis=1), left[h])
            dqs[h] += matmul(held[h, spot, 0:HEAD_DIM], ds, 0)

        ready = [scores(*unit) for unit in units[:AHEAD]]
        last = None
        for i, unit in enumerate(units):
            if i + AHEAD < len(units):
                ready.append(scores(*units[i + AHEAD]))
            pair = gradients(*unit, *ready[i])
            if last is not None:
                gather_up(*last)
            last = unit + pair
        gather_up(*last)

    sweep(cnt, lst, b, KEY_BLOCK_BACK, step)
    fill = jnp.zeros((dsum.shape[1] - width, block), jnp.float32)
    dsum[pl.ds(at, block), :] = (
        jnp.concatenate([dqs[h] for h in range(heads)] + [fill], axis=0).T * 0.125
    )

    @pl.when(b == pl.num_programs(0) - 1)
    def _():
        store_grads(acc, held, grads, out_sem)
        unshuffle(dsum, dq_own, order, order_rows)
        unshuffle(dsum, dq_other, order, order_rows, 1)


def attend_backward(
    cnt, lst, offs, q, g, o, code, anc, pos, parts, rows, order, order_rows, grad_shape
):
    own, width = q[0].shape
    count = 2 * own
    heads = width // HEAD_DIM
    all_keys = code.shape[1]
    block = query_block(own, count)
    part_count = len(parts)
    full = o[0].shape[1]
    return pl.pallas_call(
        functools.partial(backward_kernel, heads, part_count, rows, order, order_rows, block),
        out_shape=(
            jax.ShapeDtypeStruct((own, full), jnp.float32),
            jax.ShapeDtypeStruct((own, full), jnp.float32),
            jax.ShapeDtypeStruct(grad_shape, jnp.bfloat16),
        ),
        grid_spec=pltpu.PrefetchScalarGridSpec(
            num_scalar_prefetch=3,
            grid=(count // block,),
            in_specs=[
                whole((own, width)),
                whole((own, width)),
                whole((own, width)),
                whole((own, width)),
                whole((own, full)),
                whole((own, full)),
                whole((1, all_keys)),
                lanes(block),
                lanes(block),
            ]
            + [pl.BlockSpec(memory_space=pl.ANY)] * part_count,
            out_specs=[whole((own, full)), whole((own, full)), pl.BlockSpec(memory_space=pl.ANY)],
            scratch_shapes=[
                pltpu.VMEM((count, width), jnp.bfloat16),
                pltpu.VMEM((count, width), jnp.bfloat16),
                pltpu.VMEM((count, full), jnp.float32),
                pltpu.VMEM((heads, all_keys, 2 * HEAD_DIM), jnp.bfloat16),
                pltpu.VMEM((heads, 2 * HEAD_DIM, 2 * block), jnp.bfloat16),
                pltpu.VMEM((heads, 2 * block, 2 * HEAD_DIM), jnp.bfloat16),
                pltpu.VMEM((heads, all_keys, 2 * HEAD_DIM), jnp.float32),
                pltpu.VMEM((heads, HEAD_DIM, block), jnp.float32),
                pltpu.VMEM((count, full), jnp.float32),
                pltpu.VMEM((16, block), jnp.float32),
                pltpu.VMEM((all_keys, 128), jnp.int32),
                pltpu.SemaphoreType.DMA((part_count,)),
                pltpu.SemaphoreType.DMA,
            ],
        ),
        compiler_params=pltpu.CompilerParams(vmem_limit_bytes=VMEM_BYTES),
        cost_estimate=work(5, count, all_keys, heads),
    )(cnt, lst, offs, *q, *g, *o, code, anc, pos, *parts)


def swap(value, axis, step):
    count = lax.axis_size(axis)
    return lax.ppermute(value, axis, [(source, source ^ step) for source in range(count)])


def exchange(pieces, axis):
    return [pieces[0]] + [swap(pieces[step], axis, step) for step in range(1, len(pieces))]


def gather(value, axis):
    return exchange([value] * lax.axis_size(axis), axis)


def after(value, *others):
    return lax.optimization_barrier((value,) + others)[0]


def gather_square(value, axis):
    if lax.axis_size(axis) != 4 or value.shape[1] % 32:
        return gather(value, axis)
    half = value.shape[1] // 2
    near, other = swap(value, axis, 1), swap(value, axis, 2)
    far = [swap(near[:, :half], axis, 2), swap(other[:, half:], axis, 1)]
    return [value, near, other, jnp.concatenate(far, axis=1)]


def pick(values, index, axis=0):
    return lax.dynamic_index_in_dim(values, index, axis, keepdims=False)


def reorder(pieces, index):
    stacked = jnp.stack(pieces)
    return jnp.stack([pick(stacked, index ^ place) for place in range(len(pieces))])


def total(pieces):
    result = pieces[0].astype(jnp.float32)
    for piece in pieces[1:]:
        result = result + piece.astype(jnp.float32)
    return result


def low(value):
    return value.astype(jnp.bfloat16)


def dot(left, right, left_dim=1, right_dim=0):
    return lax.dot_general(
        left, right, (((left_dim,), (right_dim,)), ((), ())), preferred_element_type=jnp.float32
    )


def trade(values, axis):
    return lax.all_to_all(values, axis, 0, 0)


def share(value, axis):
    return trade(jnp.broadcast_to(value[None], (lax.axis_size(axis),) + value.shape), axis)


def spread(columns, extra, cores, rows):
    features, tokens = columns.shape
    piece = tokens // (cores * rows)
    turned = columns.reshape(features, cores * rows, piece).transpose(1, 2, 0)
    if extra is not None:
        fill = jnp.broadcast_to(extra[None], (cores * rows,) + extra.shape)
        turned = jnp.concatenate([turned, fill], axis=1)
    got = trade(turned, ("dp", "row")).reshape(cores, rows, -1, features)
    held = got[:, :, :piece].transpose(0, 2, 1, 3).reshape(cores * piece, rows * features)
    if extra is None:
        return held
    return held, got[0, :, piece:].transpose(1, 0, 2).reshape(-1, rows * features)


def by_device(values, cores, rows):
    features = values.shape[1] // rows
    sent = values.reshape(cores, -1, rows, features).transpose(0, 2, 1, 3)
    return sent.reshape(cores * rows, -1, features)


def collect(first, second, extra, cores, rows):
    second = by_device(second, cores, rows)
    _, piece, features = second.shape
    sent = jnp.concatenate([first, second], axis=2)
    lines = extra.reshape(-1, 2, rows, features).transpose(2, 0, 1, 3).reshape(rows, -1, 2 * features)
    lines = jnp.pad(lines, ((0, 0), (0, 16 - lines.shape[1]), (0, 0)))
    lines = jnp.broadcast_to(lines[None], (cores,) + lines.shape)
    lines = lines.reshape((cores * rows,) + lines.shape[2:])
    got = trade(jnp.concatenate([sent, lines], axis=1), ("dp", "row"))
    turned = got[:, :piece].transpose(2, 0, 1).reshape(2, features, -1).astype(jnp.float32)
    sums = jnp.sum(got[:, piece:].astype(jnp.float32), axis=0)
    return turned[0], turned[1], sums


def norm_forward(inputs, gain, shift):
    average = jnp.mean(inputs, axis=1, keepdims=True)
    squares = jnp.mean(inputs * inputs, axis=1, keepdims=True)
    spread_rows = lax.rsqrt(squares - average * average + 1e-05)
    unit = (inputs - average) * spread_rows
    return low(unit * gain + shift), unit, spread_rows


def norm_backward(grad, unit, spread_rows, gain):
    scaled = grad * gain
    return spread_rows * (
        scaled
        - jnp.mean(scaled, axis=1, keepdims=True)
        - unit * jnp.mean(scaled * unit, axis=1, keepdims=True)
    )


def gelu_tanh(hidden):
    return jax.nn.gelu(hidden, approximate=True)


def everywhere(value, axis):
    return total(gather(value, axis))


def side_by_side(pieces):
    return pieces.transpose(1, 0, 2).reshape(pieces.shape[1], -1)


def three_low(value):
    first = low(value)
    second = low(value - first.astype(jnp.float32))
    third = low(value - first.astype(jnp.float32) - second.astype(jnp.float32))
    return jnp.stack([first, second, third])


def block_lists(hot, places, anc, pos, key_block, query_rows):
    def reduce(values, size, start, op):
        return lax.reduce(values.reshape(-1, size), jnp.int32(start), op, (1,))

    keys = hot.shape[0] // key_block
    key_or = reduce(hot, key_block, 0, lax.bitwise_or)[None]
    start = jnp.min(places.reshape(-1, key_block), axis=1)[None]
    end = jnp.max(places.reshape(-1, key_block), axis=1)[None]
    anc_or = reduce(anc, query_rows, 0, lax.bitwise_or)[:, None]
    anc_and = reduce(anc, query_rows, -1, lax.bitwise_and)[:, None]
    first = jnp.min(pos.reshape(-1, query_rows), axis=1)[:, None]
    last = jnp.max(pos.reshape(-1, query_rows), axis=1)[:, None]
    full = ((key_or & ~anc_and) == 0) & (end <= first)
    some = (((key_or & anc_or) != 0) & (start <= last)) | full
    numbers = jnp.arange(keys, dtype=jnp.int32)
    code = jnp.where(full, 0, jnp.where(some, 1, 2)) * keys + numbers[None]
    rank = jnp.sum((code[:, None, :] < code[:, :, None]).astype(jnp.int32), axis=2)
    order = jnp.sum(
        jnp.where(rank[:, None, :] == numbers[None, :, None], numbers[None, None], 0), axis=2
    )
    counts = jnp.stack(
        [jnp.sum(full.astype(jnp.int32), axis=1), jnp.sum(some.astype(jnp.int32), axis=1)], axis=1
    )
    return counts.astype(jnp.int32), order.astype(jnp.int32)


def shards(
    block_input,
    segment_ids,
    parent_ids,
    attn_gain,
    attn_shift,
    qkv_weight,
    qkv_bias,
    proj_weight,
    proj_bias,
    mlp_gain,
    mlp_shift,
    up_weight,
    up_bias,
    down_weight,
    down_bias,
    cotangent,
):
    cores, rows, cols = lax.axis_size("dp"), lax.axis_size("row"), lax.axis_size("col")
    core, row, col = lax.axis_index("dp"), lax.axis_index("row"), lax.axis_index("col")
    features, tokens = block_input.shape
    half = tokens // cores
    piece = half // rows
    own = cores * piece
    width_all = rows * features
    heads = qkv_weight.shape[1]
    width = heads * HEAD_DIM
    head_width = 2 * HEAD_DIM
    hidden_part = up_weight.shape[1] // cores
    head_part = width // cores
    segments = parent_ids.shape[0]
    queries = cols * own
    block_rows = query_block(queries)
    whole_chunks = piece % 16 == 0

    vectors = jnp.stack([attn_gain, attn_shift, mlp_gain, mlp_shift, proj_bias, down_bias])
    vectors = jnp.pad(vectors, ((0, 2), (0, 0)))
    layer_in, vectors = spread(block_input, vectors, cores, rows)

    packed = low(qkv_weight).reshape(3, heads, features, HEAD_DIM)
    qkv_low = jnp.concatenate(
        [packed[kind, h] for h in range(heads) for kind in (1, 2)]
        + [packed[0, h] for h in range(heads)],
        axis=1,
    )
    bias = qkv_bias.reshape(3, heads, HEAD_DIM)
    bias_row = jnp.concatenate(
        [bias[kind, h] for h in range(heads) for kind in (1, 2)] + [bias[0].reshape(-1)]
    )

    proj_low = (
        low(proj_weight).reshape(heads, features, HEAD_DIM).transpose(0, 2, 1)
    ).reshape(width, features)
    up_low, down_low = [
        lax.dynamic_slice_in_dim(low(w), core * hidden_part, hidden_part, 1)
        for w in (up_weight, down_weight)
    ]
    up_bias_part = three_low(lax.dynamic_slice_in_dim(up_bias, core * hidden_part, hidden_part, 0))
    bias_rows = jnp.pad(up_bias_part, ((0, 13), (0, 0)))
    mlp_low = jnp.concatenate([up_low, down_low, bias_rows], axis=0)
    mlp_cols = jnp.concatenate(gather(mlp_low, "col"), axis=1)
    proj_all = lax.all_gather(proj_low, ("row", "col"))
    sent_rows = 2 * features
    up_bias_full = jnp.sum(mlp_cols[sent_rows : sent_rows + 3].astype(jnp.float32), axis=0)

    ones = jnp.int32(1)
    tables = jnp.arange(segments, dtype=jnp.int32)
    grand_ids = jnp.sum(
        jnp.where(parent_ids[:, None] == tables[None], parent_ids[None], 0), axis=1
    )
    anc_table = (
        jnp.left_shift(ones, tables)
        | jnp.left_shift(ones, parent_ids)
        | jnp.left_shift(ones, grand_ids)
    )
    all_places = jnp.arange(segment_ids.shape[0], dtype=jnp.int32)
    hot_all = jnp.left_shift(ones, segment_ids)
    anc_all = jnp.sum(
        jnp.where(segment_ids[None] == tables[:, None], anc_table[:, None], 0), axis=0
    )
    chunk_ids = [(c, e) for c in range(cols) for e in range(cores)]
    if whole_chunks:
        inner = [(c, e) for e in range(cores) for c in range(cols)]
    else:
        inner = chunk_ids
    order = [chunk_ids.index(chunk) for chunk in inner]
    order_rows = piece
    if not whole_chunks:
        order, order_rows = [0], queries

    def query_info(which):
        starts = [
            (e * cols + c) * tokens + which * half + row * piece for c, e in inner
        ]
        anc = [lax.dynamic_slice_in_dim(anc_all, s, piece, 0) for s in starts]
        pos = [s + jnp.arange(piece, dtype=jnp.int32) for s in starts]
        return anc, pos

    anc_own, pos_own = query_info(core)
    anc_other, pos_other = query_info(core ^ 1)
    if whole_chunks:
        anc_both = [chunk for pair in zip(anc_own, anc_other) for chunk in pair]
        pos_both = [chunk for pair in zip(pos_own, pos_other) for chunk in pair]
    else:
        anc_both, pos_both = anc_own + anc_other, pos_own + pos_other
    anc, anc_both = jnp.concatenate(anc_own), jnp.concatenate(anc_both)
    pos = jnp.concatenate(pos_own).astype(jnp.int32)
    pos_both = jnp.concatenate(pos_both).astype(jnp.int32)
    limit = ((pos + 1) << segments) - 1
    limit_both = ((pos_both + 1) << segments) - 1
    codes = (all_places << segments) | hot_all
    core_places = pick(all_places.reshape(-1, cores, half), core, 1).reshape(-1)
    core_hot = pick(hot_all.reshape(-1, cores, half), core, 1).reshape(-1)
    core_codes = (core_places << segments) | core_hot
    lists_forward = block_lists(
        hot_all, all_places, anc, pos, KEY_BLOCK, block_rows
    )
    lists_backward = block_lists(
        core_hot, core_places, anc_both, pos_both, KEY_BLOCK_BACK, query_block(queries, 2 * queries)
    )
    rows_forward = (anc[None], limit[None])
    rows_backward = (anc_both[None], limit_both[None])
    setup = (lists_forward, lists_backward, rows_forward, rows_backward, codes[None], core_codes[None])

    layer_in, qkv_low, setup, mlp_cols = lax.optimization_barrier(
        (layer_in, qkv_low, setup, mlp_cols)
    )
    lists_forward, lists_backward, rows_forward, rows_backward, codes, core_codes = setup
    qkv_full = share(qkv_low, "row").reshape(width_all, 3 * width)
    normed_in, first_unit, first_spread = norm_forward(layer_in, vectors[0], vectors[1])
    normed_all = reorder(gather(normed_in, "col"), col).reshape(queries, width_all)
    cot_rows = spread(after(cotangent, normed_in, qkv_full), None, cores, rows)
    cot_low = low(cot_rows)
    normed_all, cot_low = lax.optimization_barrier((normed_all, cot_low))
    qkv = low(dot(normed_all, qkv_full) + bias_row)
    kv_own = jnp.stack([qkv[:, h * head_width : (h + 1) * head_width] for h in range(heads)])
    q_own = qkv[:, 2 * width :] * jnp.bfloat16(0.125)
    core_parts = gather_square(kv_own, "row")

    cot_both = jnp.concatenate(gather(cot_low, "dp"), axis=0)
    q_own, cot_both, core_parts = lax.optimization_barrier((q_own, cot_both, core_parts))
    parts = [part for held in core_parts for part in gather(held, "dp")]
    q_other = swap(q_own, "dp", 1)
    mlp_got = gather(after(mlp_cols[:sent_rows], *core_parts), "row")
    if whole_chunks:
        offsets = jnp.stack(
            [
                (e * cols + c) * tokens + (core ^ jd) * half + (row ^ k) * piece
                for k in range(rows)
                for jd in range(cores)
                for c, e in chunk_ids
            ]
        ).astype(jnp.int32)
        core_offsets = jnp.stack(
            [
                (e * cols + c) * half + (row ^ k) * piece
                for k in range(rows)
                for c, e in chunk_ids
            ]
        ).astype(jnp.int32)
        chunk, core_chunk = piece, piece
        grad_shape = (rows, heads, cols, cores, piece, head_width)
    else:

        def natural(pieces, count):
            sorted_parts = [
                [pieces[k * count + j] for j in range(count)] for k in range(rows)
            ]
            by_core = [reorder(p, core) if count > 1 else jnp.stack(p) for p in sorted_parts]
            stacked = reorder(by_core, row).reshape(
                rows, count, heads, cols, cores, piece, head_width
            )
            return [stacked.transpose(2, 4, 3, 1, 0, 5, 6).reshape(heads, -1, head_width)]

        parts, core_parts = natural(parts, cores), natural(core_parts, 1)
        offsets = core_offsets = jnp.zeros((1,), jnp.int32)
        chunk, core_chunk = parts[0].shape[1], core_parts[0].shape[1]
        grad_shape = core_parts[0].shape
    head_out, attended_low = attend_forward(
        *lists_forward,
        offsets,
        q_own,
        codes,
        *rows_forward,
        parts,
        chunk,
        order,
        order_rows,
    )
    attended_low, mlp_got, proj_all = lax.optimization_barrier((attended_low, mlp_got, proj_all))
    proj_full = (
        proj_all.reshape(rows, cols * width, features)
        .transpose(1, 0, 2)
        .reshape(cols * width, width_all)
    )
    attended = side_by_side(trade(attended_low.reshape(cols, own, width), "col"))
    out_other = swap(head_out, "dp", 1)

    hidden_all = cols * hidden_part

    def by_row(first, count):
        whole_rows = jnp.zeros((rows, count, hidden_all), jnp.bfloat16)
        for k in range(rows):
            part = mlp_got[k][None, first : first + count]
            whole_rows = lax.dynamic_update_slice_in_dim(whole_rows, part, row ^ k, 0)
        return whole_rows

    up_full = by_row(0, features).reshape(width_all, hidden_all)
    down_full = by_row(features, features).reshape(width_all, hidden_all)
    branch = dot(attended, proj_full) + vectors[4]
    middle = layer_in + branch
    normed_mid, second_unit, second_spread = norm_forward(middle, vectors[2], vectors[3])
    mid_both = jnp.concatenate(gather(normed_mid, "dp"), axis=0)
    hidden = dot(mid_both, up_full) + up_bias_full
    activated = low(gelu_tanh(hidden))
    act_grad = dot(cot_both, down_full)
    hidden_grad = low(jax.vjp(gelu_tanh, hidden)[1](act_grad)[0])

    def own_sum(both):
        return total(exchange([both[j * own : (j + 1) * own] for j in range(cores)], "dp"))

    mid_norm_grad = own_sum(dot(hidden_grad, up_full, 1, 1))
    second_back = norm_backward(mid_norm_grad, second_unit, second_spread, vectors[2])
    middle_grad = cot_rows + second_back
    mid_low = low(middle_grad)
    attended_grad = low(dot(mid_low, proj_full, 1, 1))

    sent = attended_grad.reshape(own, cols, width).transpose(1, 0, 2)
    sent, hidden_late, cot_late, activated_late = lax.optimization_barrier(
        (sent, hidden_grad, cot_both, activated)
    )
    out_grad = trade(sent, "col").reshape(queries, width)
    grad_other = swap(out_grad, "dp", 1)

    up_grad = low(dot(mid_both, hidden_late, 0, 0))
    down_grad = low(dot(cot_late, activated_late, 0, 0))
    proj_grad = low(dot(attended, mid_low, 0, 0)).reshape(cols, cores, head_part, width_all)
    proj_sum = total([pick(proj_grad, core, 1), swap(pick(proj_grad, core ^ 1, 1), "dp", 1)])
    pack = hidden_part // features
    proj_sent = (
        low(proj_sum)
        .reshape(cols, pack, head_part // pack, rows, features)
        .transpose(3, 2, 0, 1, 4)
    )
    proj_sent = jnp.stack([pick(proj_sent, col ^ k, 2) for k in range(cols)], axis=2)
    proj_sent = proj_sent.reshape(rows, head_part // pack, cols * pack * features)
    bias_grad = low(jnp.sum(hidden_late, axis=0, dtype=jnp.float32))
    bias_sent = jnp.pad(bias_grad[None], ((0, 15), (0, 0)))
    up_grad = up_grad.reshape(rows, features, hidden_all)
    down_grad = down_grad.reshape(rows, features, hidden_all)
    grads_sent = [
        jnp.concatenate(
            [pick(part, row ^ k) for part in (up_grad, down_grad, proj_sent)] + [bias_sent], axis=0
        )
        for k in range(rows)
    ]
    grads_sent, rows_backward = lax.optimization_barrier((grads_sent, rows_backward))
    grads_got = exchange(grads_sent, "row")
    early = jnp.stack(
        [
            jnp.sum(mid_norm_grad * second_unit, axis=0),
            jnp.sum(mid_norm_grad, axis=0),
            jnp.sum(mid_low, axis=0, dtype=jnp.float32),
            jnp.sum(cot_low, axis=0, dtype=jnp.float32),
        ]
    )

    query_grad, query_grad_other, part_grads = attend_backward(
        *lists_backward,
        core_offsets,
        (q_own, q_other),
        (out_grad, grad_other),
        (head_out, out_other),
        core_codes,
        *rows_backward,
        core_parts,
        core_chunk,
        order,
        order_rows,
        grad_shape,
    )
    if not whole_chunks:
        part_grads = part_grads.reshape(heads, cores, cols, rows, piece, head_width)
        part_grads = part_grads.transpose(3, 0, 2, 1, 4, 5)

    part_grads, grads_got, activated_late = lax.optimization_barrier(
        (part_grads, grads_got, activated_late)
    )
    kv_got = trade(part_grads.reshape(rows, heads, queries, head_width), "row")
    kv_grad = low(jnp.sum(kv_got.astype(jnp.float32), axis=0))
    query_low = low((query_grad + swap(query_grad_other, "dp", 1))[:, :width])
    qkv_grad = jnp.concatenate([kv_grad[h] for h in range(heads)] + [query_low], axis=1)
    first_parts = low(dot(qkv_grad, qkv_full, 1, 1)).reshape(cols, own, width_all)
    row_sums = low(total(grads_got))
    col_sums = low(
        total(
            exchange(
                [
                    row_sums[:, k * hidden_part : (k + 1) * hidden_part]
                    for k in range(cols)
                ],
                "col",
            )
        )
    )
    mlp_both = dot(activated_late, down_full, 1, 1)
    mlp_out = own_sum(mlp_both) + vectors[5]
    output_rows = by_device(low(branch + mlp_out), cores, rows)
    first_parts, col_sums, output_rows, qkv_grad, early = lax.optimization_barrier(
        (first_parts, col_sums, output_rows, qkv_grad, early)
    )
    first_grad = jnp.sum(trade(first_parts, "col").astype(jnp.float32), axis=0)

    other_sums = swap(col_sums, "dp", 1)
    first_sums = jnp.where(core == 0, col_sums, other_sums).astype(jnp.float32)
    second_sums = jnp.where(core == 0, other_sums, col_sums).astype(jnp.float32)
    both_sums = jnp.concatenate([first_sums, second_sums], axis=1)
    up_weight_grad = both_sums[:features]
    down_weight_grad = both_sums[features : 2 * features]
    up_bias_grad = both_sums[2 * features + head_part // pack]

    def proj_rows(sums):
        values = sums[2 * features : 2 * features + head_part // pack]
        values = values[:, : pack * features].reshape(head_part // pack, pack, features)
        return values.transpose(1, 0, 2).reshape(head_part, features)

    proj_weight_grad = (
        jnp.concatenate([proj_rows(first_sums), proj_rows(second_sums)], axis=0)
        .reshape(heads, HEAD_DIM, features)
        .transpose(0, 2, 1)
        .reshape(heads, features * HEAD_DIM)
    )
    def vector_sums(values):
        pieces = values.reshape(-1, rows, features).transpose(1, 0, 2)
        summed = total(exchange([pick(pieces, row ^ k) for k in range(rows)], "row"))
        return everywhere(everywhere(summed, "col"), "dp")

    first_back = norm_backward(first_grad, first_unit, first_spread, vectors[0])
    late = jnp.stack([jnp.sum(first_grad * first_unit, axis=0), jnp.sum(first_grad, axis=0)])
    output_grown, input_grown, late_sums = collect(
        output_rows, low(second_back + first_back), three_low(late), cores, rows
    )
    block_output = block_input + output_grown
    input_grad = cotangent + input_grown
    late_sums = everywhere(jnp.sum(late_sums, axis=0).reshape(2, features), "col")
    sums = vector_sums(early)
    wide = low(dot(normed_all, qkv_grad, 0, 0)).reshape(rows, features, 3 * width)
    bias_part = low(jnp.sum(qkv_grad, axis=0, dtype=jnp.float32))
    bias_part = jnp.broadcast_to(
        jnp.pad(bias_part[None], ((0, 15), (0, 0)))[None], (rows, 16, 3 * width)
    )
    wide = jnp.concatenate([wide, bias_part], axis=1)
    wide_pieces = [pick(wide, row ^ k) for k in range(rows)]
    wide_sum = low(total(exchange(wide_pieces, "row")))
    wide_sum = everywhere(wide_sum, "dp")

    def unpacked(values):
        lead = values.shape[0]
        kv = values[:, : 2 * width].reshape(lead, heads, 2, HEAD_DIM).transpose(2, 1, 0, 3)
        q = values[:, 2 * width :].reshape(lead, heads, HEAD_DIM).transpose(1, 0, 2)
        return jnp.concatenate([q[None], kv], axis=0)

    qkv_weight_grad = unpacked(wide_sum[:features]).reshape(3, heads, features * HEAD_DIM)
    qkv_bias_grad = unpacked(wide_sum[features : features + 1]).reshape(3, width)
    return (
        block_output,
        input_grad,
        late_sums[0],
        late_sums[1],
        qkv_weight_grad,
        qkv_bias_grad,
        proj_weight_grad,
        sums[2],
        sums[0],
        sums[1],
        up_weight_grad,
        up_bias_grad,
        down_weight_grad,
        sums[3],
    )


def solution(mesh):
    return jax.shard_map(
        shards,
        mesh=mesh,
        in_specs=(
            P("row", ("dp", "col")),
            P(),
            P(),
            P("row"),
            P("row"),
            P(None, "col", "row"),
            P(None, "col"),
            P("col", "row"),
            P("row"),
            P("row"),
            P("row"),
            P("row", "col"),
            P("col"),
            P("row", "col"),
            P("row"),
            P("row", ("dp", "col")),
        ),
        out_specs=(
            P("row", ("dp", "col")),
            P("row", ("dp", "col")),
            P("row"),
            P("row"),
            P(None, "col", "row"),
            P(None, "col"),
            P("col", "row"),
            P("row"),
            P("row"),
            P("row"),
            P("row", "col"),
            P("col"),
            P("row", "col"),
            P("row"),
        ),
        check_vma=False,
    )
```
